32 devices in a mesh: dp: 16 (over z, y, x), seq: 2 (over core).
Axes of the slice: x: 2, y: 2, z: 4, core: 2. Of those that a mesh axis runs over, the one named last changes fastest.
Arguments:
- latents: bfloat16 [16, 1024, 1024], P('dp', 'seq'), may hold values from -6 to 6
- condition: bfloat16 [16, 1024], P('dp'), may hold values from -6 to 6
- adapter_choice: int32 [16, 5], P('dp'), may hold values from 0 to 7
- cotangent: bfloat16 [16, 1024, 1024], P('dp', 'seq'), may hold values from -6 to 6
- modulate_weight: bfloat16 [1024, 6144], P(('dp', 'seq')), may hold values from -0.1875 to 0.1875
- attend_weight: bfloat16 [1024, 3072], P(('dp', 'seq')), may hold values from -0.1875 to 0.1875
- project_weight: bfloat16 [1024, 1024], P(('dp', 'seq')), may hold values from -3 to 3
- expand_weight: bfloat16 [1024, 4096], P(('dp', 'seq')), may hold values from -0.1875 to 0.1875
- contract_weight: bfloat16 [4096, 1024], P(('dp', 'seq')), may hold values from -0.09375 to 0.09375
- modulate_down: bfloat16 [8, 1024, 16], P(None, ('dp', 'seq')), may hold values from -0.1875 to 0.1875
- modulate_up: bfloat16 [8, 16, 6144], P(None, None, ('dp', 'seq')), may hold values from -0.75 to 0.75
- attend_down: bfloat16 [8, 1024, 16], P(None, ('dp', 'seq')), may hold values from -0.1875 to 0.1875
- attend_up: bfloat16 [8, 16, 3072], P(None, None, ('dp', 'seq')), may hold values from -0.75 to 0.75
- project_down: bfloat16 [8, 1024, 16], P(None, ('dp', 'seq')), may hold values from -0.1875 to 0.1875
- project_up: bfloat16 [8, 16, 1024], P(None, None, ('dp', 'seq')), may hold values from -6 to 6
- expand_down: bfloat16 [8, 1024, 16], P(None, ('dp', 'seq')), may hold values from -0.1875 to 0.1875
- expand_up: bfloat16 [8, 16, 4096], P(None, None, ('dp', 'seq')), may hold values from -0.75 to 0.75
- contract_down: bfloat16 [8, 4096, 16], P(None, ('dp', 'seq')), may hold values from -0.09375 to 0.09375
- contract_up: bfloat16 [8, 16, 1024], P(None, None, ('dp', 'seq')), may hold values from -0.75 to 0.75
Outputs:
- block_output: bfloat16 [16, 1024, 1024], P('dp', 'seq')
- input_grad: float32 [16, 1024, 1024], P('dp', 'seq')
- condition_grad: float32 [16, 1024], P('dp')
- modulate_down_grad: float32 [8, 1024, 16], P(None, ('dp', 'seq'))
- modulate_up_grad: float32 [8, 16, 6144], P(None, None, ('dp', 'seq'))
- attend_down_grad: float32 [8, 1024, 16], P(None, ('dp', 'seq'))
- attend_up_grad: float32 [8, 16, 3072], P(None, None, ('dp', 'seq'))
- project_down_grad: float32 [8, 1024, 16], P(None, ('dp', 'seq'))
- project_up_grad: float32 [8, 16, 1024], P(None, None, ('dp', 'seq'))
- expand_down_grad: float32 [8, 1024, 16], P(None, ('dp', 'seq'))
- expand_up_grad: float32 [8, 16, 4096], P(None, None, ('dp', 'seq'))
- contract_down_grad: float32 [8, 4096, 16], P(None, ('dp', 'seq'))
- contract_up_grad: float32 [8, 16, 1024], P(None, None, ('dp', 'seq'))
The draws below stay inside these ranges and needn't reach their ends.
All inputs are finite; a program needn't handle non-finite values.
Results may differ from the reference program's by a relative error of at most 0.01195.
The reference program's roundings to bfloat16 on the way count: a program that leaves them out, or rounds other values in their place, can miss the bound.
Values may be sent and summed in bfloat16 or wider, within the bound.
No kernel may reach another device: no remote copies, remote signals or barrier semaphores. Data moves between devices by JAX's collectives and lax.ppermute only.
A program may use at most 256 MiB of HBM per device.

```python
import jax
import jax.numpy as jnp
from jax import lax

D = 1024
HEADS = 16
HEAD_DIM = 64
FF = 4096
RANK = 16
NADAPT = 8
TOKS = 1024
LATENTS = 16


def place_ends(drawn, rng, low, high):
    dims = drawn.shape
    place = [jax.random.randint(jax.random.fold_in(rng, axis), (), 0, dims[axis]) for axis in range(len(dims))]
    drawn = drawn.at[tuple(place)].set(low)
    longest = dims.index(max(dims))
    place[longest] = (place[longest] + 1) % dims[longest]
    return drawn.at[tuple(place)].set(high)


def block_levels(own_key, extent, pieces, low, top_value):
    def one(axis_at, blocks):
        steps = jax.random.uniform(jax.random.fold_in(jax.random.fold_in(own_key, 6), axis_at), (blocks,), jnp.float32, low / len(pieces), top_value / len(pieces))
        return jnp.repeat(jnp.exp(steps), extent[axis_at] // blocks).reshape((-1,) + (1,) * (len(extent) - axis_at - 1))

    gain = one(*pieces[0])
    for cut in pieces[1:]:
        gain = gain * one(*cut)
    return gain


def normal_values(stream_key, dims, deviation, most, pieces=(), dtype=jnp.bfloat16):
    loudness = block_levels(stream_key, dims, pieces, -0.22, 0.18) if pieces else 1.0
    result = jax.random.normal(stream_key, dims, jnp.float32) * deviation * loudness
    return jnp.minimum(jnp.maximum(result, -most), most).astype(dtype)


def setup_inputs(seed: int = 0) -> dict:
    streams_of = jax.random.split(jax.random.key(seed), 20)
    latents = normal_values(streams_of[0], (LATENTS, TOKS, D), 1.0, 6.0, ((0, 16), (1, 2)))
    condition = normal_values(streams_of[1], (LATENTS, D), 1.0, 6.0, ((0, 16),))
    adapter_choice = place_ends(jax.random.randint(streams_of[2], (LATENTS, 5), 0, NADAPT), jax.random.fold_in(streams_of[2], 1), 0, NADAPT - 1).astype(jnp.int32)
    cotangent = normal_values(streams_of[3], (LATENTS, TOKS, D), 1.0, 6.0, ((0, 16), (1, 2)))
    modulate_weight = normal_values(streams_of[4], (D, 6 * D), D ** -0.5, 0.1875, ((0, 32),))
    attend_weight = normal_values(streams_of[5], (D, 3 * D), D ** -0.5, 0.1875, ((0, 32),))
    project_weight = normal_values(streams_of[6], (D, D), (max(D // 256, 4)) ** -0.5, 3.0, ((0, 32),))
    expand_weight = normal_values(streams_of[7], (D, FF), D ** -0.5, 0.1875, ((0, 32),))
    contract_weight = normal_values(streams_of[8], (FF, D), FF ** -0.5, 0.09375, ((0, 32),))
    modulate_down = normal_values(streams_of[9], (NADAPT, D, RANK), D ** -0.5, 0.1875, ((1, 32),))
    modulate_up = normal_values(streams_of[10], (NADAPT, RANK, 6 * D), (4 * RANK) ** -0.5, 0.75, ((2, 32),))
    attend_down = normal_values(streams_of[11], (NADAPT, D, RANK), D ** -0.5, 0.1875, ((1, 32),))
    attend_up = normal_values(streams_of[12], (NADAPT, RANK, 3 * D), (4 * RANK) ** -0.5, 0.75, ((2, 32),))
    project_down = normal_values(streams_of[13], (NADAPT, D, RANK), D ** -0.5, 0.1875, ((1, 32),))
    project_up = normal_values(streams_of[14], (NADAPT, RANK, D), (max(RANK // 16, 1)) ** -0.5, 6.0, ((2, 32),))
    expand_down = normal_values(streams_of[15], (NADAPT, D, RANK), D ** -0.5, 0.1875, ((1, 32),))
    expand_up = normal_values(streams_of[16], (NADAPT, RANK, FF), (4 * RANK) ** -0.5, 0.75, ((2, 32),))
    contract_down = normal_values(streams_of[17], (NADAPT, FF, RANK), FF ** -0.5, 0.09375, ((1, 32),))
    contract_up = normal_values(streams_of[18], (NADAPT, RANK, D), (4 * RANK) ** -0.5, 0.75, ((2, 32),))
    return {"latents": latents, "condition": condition, "adapter_choice": adapter_choice, "cotangent": cotangent, "modulate_weight": modulate_weight, "attend_weight": attend_weight, "project_weight": project_weight, "expand_weight": expand_weight, "contract_weight": contract_weight, "modulate_down": modulate_down, "modulate_up": modulate_up, "attend_down": attend_down, "attend_up": attend_up, "project_down": project_down, "project_up": project_up, "expand_down": expand_down, "expand_up": expand_up, "contract_down": contract_down, "contract_up": contract_up}


@jax.custom_vjp
def low(v):
    return lax.optimization_barrier(v.astype(jnp.bfloat16)).astype(jnp.float32)

@jax.custom_vjp
def low_back(v):
    return v

def low_keep(v):
    return (low(v), None)

def low_pass(kept, grad):
    return (grad,)

def back_keep(v):
    return (v, None)

def back_low(kept, grad):
    return (low(grad),)
low.defvjp(low_keep, low_pass)
low_back.defvjp(back_keep, back_low)

def matmul_high(left, right):
    return jnp.dot(left, right, precision=lax.Precision.HIGHEST)

def adapted(inputs, down, upward):
    middle = low_back(low(matmul_high(inputs, down)))
    return matmul_high(middle, upward)

def normalize(values):
    centred = values - lax.optimization_barrier(jnp.mean(values, axis=-1, keepdims=True))
    variance = lax.optimization_barrier(jnp.mean(centred * centred, axis=-1, keepdims=True))
    return centred * lax.rsqrt(variance + 1e-06)

def forward_latent(tokens, condition, picked, weights, adapters):
    modulate_weight, attend_weight, project_weight, expand_weight, contract_weight = weights
    chosen = [adapters[member][picked[member // 2]] for member in range(10)]
    lifted = low(jax.nn.silu(condition))[None, :]
    modulation = low_back(matmul_high(lifted, modulate_weight) + adapted(lifted, chosen[0], chosen[1]))[0]
    shift_attend, scale_attend, gate_attend, shift_expand, scale_expand, gate_expand = jnp.split(modulation, 6)
    entering = low(normalize(tokens) * (1.0 + scale_attend) + shift_attend)
    projected = low(low_back(matmul_high(entering, attend_weight) + adapted(entering, chosen[2], chosen[3])))
    queries = projected[:, :D].reshape(TOKS, HEADS, HEAD_DIM)
    keys = projected[:, D:2 * D].reshape(TOKS, HEADS, HEAD_DIM)
    values = projected[:, 2 * D:].reshape(TOKS, HEADS, HEAD_DIM)
    scores = low_back(jnp.einsum('qhd,khd->hqk', queries, keys, precision=lax.Precision.HIGHEST) * HEAD_DIM ** (-0.5))
    probs = low(jax.nn.softmax(scores, axis=-1))
    attended = jnp.einsum('hqk,khd->qhd', probs, values, precision=lax.Precision.HIGHEST).reshape(TOKS, D)
    attended = low(low_back(attended))
    branch_attend = low_back(matmul_high(attended, project_weight) + adapted(attended, chosen[4], chosen[5]))
    middle_tokens = tokens + gate_attend * branch_attend
    entering_mlp = low(normalize(middle_tokens) * (1.0 + scale_expand) + shift_expand)
    hidden = low_back(matmul_high(entering_mlp, expand_weight) + adapted(entering_mlp, chosen[6], chosen[7]))
    activated = low(jax.nn.gelu(hidden, approximate=True))
    branch_mlp = low_back(matmul_high(activated, contract_weight) + adapted(activated, chosen[8], chosen[9]))
    return middle_tokens + gate_expand * branch_mlp

def reference(latents, condition, adapter_choice, cotangent, modulate_weight, attend_weight, project_weight, expand_weight, contract_weight, modulate_down, modulate_up, attend_down, attend_up, project_down, project_up, expand_down, expand_up, contract_down, contract_up):
    weights = tuple((matrix.astype(jnp.float32) for matrix in (modulate_weight, attend_weight, project_weight, expand_weight, contract_weight)))
    adapters = tuple((table.astype(jnp.float32) for table in (modulate_down, modulate_up, attend_down, attend_up, project_down, project_up, expand_down, expand_up, contract_down, contract_up)))

    def one_latent(totals, inputs):
        tokens, cond_row, picked, cotangent_row = inputs

        def forward(token_part, cond_part, tables):
            return forward_latent(token_part, cond_part, picked, weights, tables)
        output, pullback = jax.vjp(forward, tokens, cond_row, adapters)
        token_grad, cond_grad, table_grads = pullback(cotangent_row)
        totals = tuple((total + grad for total, grad in zip(totals, table_grads)))
        return (totals, (output.astype(jnp.bfloat16), token_grad, cond_grad))
    zeros = tuple((jnp.zeros_like(table) for table in adapters))
    totals, (outputs, token_grads, cond_grads) = lax.scan(one_latent, zeros, (latents.astype(jnp.float32), condition.astype(jnp.float32), adapter_choice.astype(jnp.int32), cotangent.astype(jnp.float32)))
    return (outputs, token_grads, cond_grads, totals[0], totals[1], totals[2], totals[3], totals[4], totals[5], totals[6], totals[7], totals[8], totals[9])
```

```python
import jax
import jax.numpy as jnp
from jax import lax
from jax.experimental import pallas as pl
from jax.experimental.pallas import tpu as pltpu
from jax.sharding import PartitionSpec as P

D = 1024
HEADS = 16
HEAD_DIM = 64
FF = 4096
RANK = 16
bf16 = jnp.bfloat16
f32 = jnp.float32
EPSILON = 1e-06
LOG2E = 1.4426950408889634
GROUP = 256
TILE = 512
GROUPS = 32
NADAPT = 8
CHUNK = 128
VMEM_LIMIT = 56 * 1024 * 1024
SHIFT_ATTEND, SCALE_ATTEND, GATE_ATTEND, SHIFT_EXPAND, SCALE_EXPAND, GATE_EXPAND = range(6)


def product(left, right):
    return lax.dot_general(left, right, (((1,), (0,)), ((), ())), preferred_element_type=f32)


def product_back(grads, right):
    return lax.dot_general(grads, right, (((1,), (1,)), ((), ())), preferred_element_type=f32)


def product_rows(left, right):
    return lax.dot_general(left, right, (((0,), (0,)), ((), ())), preferred_element_type=f32)


def normalize(values):
    centred = values - jnp.mean(values, axis=-1, keepdims=True)
    variance = jnp.mean(centred * centred, axis=-1, keepdims=True)
    inverse = lax.rsqrt(variance + EPSILON)
    return centred * inverse, inverse


def normalize_back(grads, normed, inverse):
    mean = jnp.mean(grads, axis=-1, keepdims=True)
    along = jnp.mean(grads * normed, axis=-1, keepdims=True)
    return (grads - mean - normed * along) * inverse


def each_chunk(rows, step):
    def body(position, carry):
        step(pl.ds(pl.multiple_of(position * CHUNK, CHUNK), CHUNK))
        return carry

    lax.fori_loop(0, rows // CHUNK, body, 0)


def whole(shape):
    return pl.BlockSpec(shape, lambda *_: (0,) * len(shape))


def params():
    return pltpu.CompilerParams(vmem_limit_bytes=VMEM_LIMIT)


def enter_kernel(latents, modulation, weight, down, up, projected, entering, middle):
    @pl.when(pl.program_id(0) == 0)
    def _():
        def step(rows):
            normed, _ = normalize(latents[rows].astype(f32))
            values = normed * (1.0 + modulation[SCALE_ATTEND : SCALE_ATTEND + 1]) + modulation[
                SHIFT_ATTEND : SHIFT_ATTEND + 1
            ]
            values = values.astype(bf16)
            entering[rows] = values
            middle[rows] = product_back(values, down[...]).astype(bf16)

        each_chunk(latents.shape[0], step)

    projected[...] = (
        product(entering[...], weight[...].reshape(D, TILE)) + product(middle[...], up[...])
    ).astype(bf16)


def enter(latents, modulation, weight, down, up):
    rows = latents.shape[0]
    groups, deep, columns = weight.shape
    return pl.pallas_call(
        enter_kernel,
        grid=(columns // TILE,),
        in_specs=[
            whole((rows, D)),
            whole(modulation.shape),
            pl.BlockSpec((groups, deep, TILE), lambda j: (0, 0, j)),
            whole(down.shape),
            pl.BlockSpec((RANK, TILE), lambda j: (0, j)),
        ],
        out_specs=[
            pl.BlockSpec((rows, TILE), lambda j: (0, j)),
            whole((rows, D)),
            whole((rows, RANK)),
        ],
        out_shape=[
            jax.ShapeDtypeStruct((rows, columns), bf16),
            jax.ShapeDtypeStruct((rows, D), bf16),
            jax.ShapeDtypeStruct((rows, RANK), bf16),
        ],
        compiler_params=params(),
        name="enter",
    )(latents, modulation, weight, down, up)


def head_mask(head, dtype=jnp.bool_):
    lane = lax.broadcasted_iota(jnp.int32, (1, GROUP), 1)
    return jnp.logical_and(lane >= head * HEAD_DIM, lane < (head + 1) * HEAD_DIM)


def attend_kernel(queries, keys_near, values_near, keys_far, values_far, attended, logsum):
    rows = queries.shape[0]
    block = 256
    scale = HEAD_DIM ** (-0.5)
    lane = lax.broadcasted_iota(jnp.int32, (1, 128), 1)

    for start in range(0, rows, block):
        here = pl.ds(start, block)
        q = queries[here] * jnp.asarray(scale, bf16)
        total = jnp.zeros((block, GROUP), f32)
        sums = jnp.zeros((block, 128), f32)
        for head in range(GROUP // HEAD_DIM):
            mask = head_mask(head)
            mine = jnp.where(mask, q, jnp.zeros_like(q))
            near = product_back(mine, keys_near[...])
            far = product_back(mine, keys_far[...])
            highest = jnp.maximum(
                jnp.max(near, axis=1, keepdims=True), jnp.max(far, axis=1, keepdims=True)
            )
            near = jnp.exp2((near - highest) * LOG2E)
            far = jnp.exp2((far - highest) * LOG2E)
            denominator = jnp.sum(near, axis=1, keepdims=True) + jnp.sum(
                far, axis=1, keepdims=True
            )
            share = 1.0 / denominator
            out = product((near * share).astype(bf16), values_near[...]) + product(
                (far * share).astype(bf16), values_far[...]
            )
            total = jnp.where(mask, out, total)
            sums = jnp.where(lane == head, highest + jnp.log(denominator), sums)
        attended[here] = total.astype(bf16)
        logsum[0, here] = sums


def attend(projected, other):
    rows = projected.shape[0]
    groups = D // GROUP

    def at(first):
        return pl.BlockSpec((rows, GROUP), lambda g: (0, first + g))

    return pl.pallas_call(
        attend_kernel,
        grid=(groups,),
        in_specs=[at(0), at(groups), at(2 * groups), at(0), at(groups)],
        out_specs=[at(0), pl.BlockSpec((1, rows, 128), lambda g: (g, 0, 0))],
        out_shape=[
            jax.ShapeDtypeStruct((rows, D), bf16),
            jax.ShapeDtypeStruct((groups, rows, 128), f32),
        ],
        compiler_params=params(),
        name="attend",
    )(projected, projected, projected, other, other)


def attend_back_kernel(
    queries, keys_near, values_near, keys_far, values_far, grads, logsum,
    grad_queries, grad_near, grad_far, keys_sum, values_sum
):
    rows = queries.shape[0]
    block = 256
    scale = HEAD_DIM ** (-0.5)
    scaled = queries[...] * jnp.asarray(scale, bf16)
    scaled_t = scaled.T
    grads_t = grads[...].T
    for start in range(0, rows, block):
        here = slice(start, start + block)
        q = scaled[here]
        g = grads[here]
        total = jnp.zeros((block, GROUP), f32)
        for head in range(GROUP // HEAD_DIM):
            mask = head_mask(head)
            part = slice(head * HEAD_DIM, (head + 1) * HEAD_DIM)
            mine = jnp.where(mask, q, jnp.zeros_like(q))
            mine_g = jnp.where(mask, g, jnp.zeros_like(g))
            shift = logsum[0, here, head : head + 1]
            pn = jnp.exp2((product_back(mine, keys_near[...]) - shift) * LOG2E)
            pf = jnp.exp2((product_back(mine, keys_far[...]) - shift) * LOG2E)
            gn = product_back(mine_g, values_near[...])
            gf = product_back(mine_g, values_far[...])
            inner = jnp.sum(pn * gn, axis=1, keepdims=True) + jnp.sum(
                pf * gf, axis=1, keepdims=True
            )
            sn = (pn * (gn - inner)).astype(bf16)
            sf = (pf * (gf - inner)).astype(bf16)
            out = product(sn, keys_near[...]) + product(sf, keys_far[...])
            total = jnp.where(mask, out * scale, total)
            vn = product(grads_t[part, here], pn.astype(bf16))
            vf = product(grads_t[part, here], pf.astype(bf16))
            kn = product(scaled_t[part, here], sn)
            kf = product(scaled_t[part, here], sf)
            if start == 0:
                values_sum[part, :rows] = vn
                values_sum[part, rows:] = vf
                keys_sum[part, :rows] = kn
                keys_sum[part, rows:] = kf
            else:
                values_sum[part, :rows] += vn
                values_sum[part, rows:] += vf
                keys_sum[part, :rows] += kn
                keys_sum[part, rows:] += kf
        grad_queries[here] = total.astype(bf16)
    grad_near[0] = keys_sum[:, :rows].T
    grad_near[1] = values_sum[:, :rows].T
    grad_far[0] = keys_sum[:, rows:].T
    grad_far[1] = values_sum[:, rows:].T


def attend_back(projected, other, grads, logsum):
    rows = projected.shape[0]
    groups = D // GROUP

    def at(first):
        return pl.BlockSpec((rows, GROUP), lambda g: (0, first + g))

    pair = pl.BlockSpec((2, rows, GROUP), lambda g: (0, 0, g))
    return pl.pallas_call(
        attend_back_kernel,
        grid=(groups,),
        in_specs=[at(0), at(groups), at(2 * groups), at(0), at(groups), at(0),
                  pl.BlockSpec((1, rows, 128), lambda g: (g, 0, 0))],
        out_specs=[at(0), pair, pair],
        out_shape=[
            jax.ShapeDtypeStruct((rows, D), bf16),
            jax.ShapeDtypeStruct((2, rows, D), f32),
            jax.ShapeDtypeStruct((2, rows, D), f32),
        ],
        scratch_shapes=[pltpu.VMEM((GROUP, 2 * rows), f32), pltpu.VMEM((GROUP, 2 * rows), f32)],
        compiler_params=params(),
        name="attend_back",
    )(projected, projected, projected, other, other, grads, logsum)


def gelu_both(values):
    root = 0.7978845608028654
    square = values * values
    inner = jnp.tanh(values * (root + (root * 0.044715) * square))
    half = 0.5 + 0.5 * inner
    slope = half + (0.5 * values) * (1.0 - inner * inner) * (root + (3.0 * root * 0.044715) * square)
    return values * half, slope


def feed_kernel(
    latents, attended, cotangent, modulation, project, expand, contract,
    project_down, project_up, expand_down, expand_up, contract_down, contract_up,
    block_output, grad_middle, grad_attended, sums,
    grad_project_down, grad_project_up, grad_expand_down, grad_expand_up,
    grad_contract_down, grad_contract_up,
    branch_attend, middle_tokens, entering, grad_branch, branch, grad_entering,
    middle_project, middle_expand, middle_contract, back_contract, back_expand, grad_branch_attend,
    back_project,
):
    step_at = pl.program_id(0)
    rows_all = latents.shape[0]

    def row(which):
        return modulation[which : which + 1]

    @pl.when(step_at == 0)
    def _():
        def step(rows):
            middle = product_back(attended[rows], project_down[...]).astype(bf16)
            middle_project[rows] = middle
            out = product(attended[rows], project[...].reshape(D, D)) + product(
                middle, project_up[...]
            )
            branch_attend[rows] = out
            tokens = latents[rows].astype(f32) + row(GATE_ATTEND) * out
            middle_tokens[rows] = tokens
            normed, _ = normalize(tokens)
            values = (normed * (1.0 + row(SCALE_EXPAND)) + row(SHIFT_EXPAND)).astype(bf16)
            entering[rows] = values
            middle_expand[rows] = product_back(values, expand_down[...]).astype(bf16)
            grads = (cotangent[rows].astype(f32) * row(GATE_EXPAND)).astype(bf16)
            grad_branch[rows] = grads
            back_contract[rows] = product_back(grads, contract_up[...]).astype(bf16)
            branch[rows] = jnp.zeros((CHUNK, D), f32)
            grad_entering[rows] = jnp.zeros((CHUNK, D), f32)
            middle_contract[rows] = jnp.zeros((CHUNK, RANK), f32)
            back_expand[rows] = jnp.zeros((CHUNK, RANK), f32)

        each_chunk(rows_all, step)

    wide = expand[...].reshape(D, TILE)
    deep = contract[...].reshape(TILE, D)
    hidden = product(entering[...], wide) + product(middle_expand[...], expand_up[...])
    activated, slope = gelu_both(hidden)
    activated = activated.astype(bf16)
    branch[...] += product(activated, deep)
    middle_contract[...] += product_back(activated, contract_down[...])
    grads = product_back(grad_branch[...], deep) + product(back_contract[...], contract_down[...])
    grads = (grads * slope).astype(bf16)
    grad_entering[...] += product_back(grads, wide)
    back_expand[...] += product_back(grads, expand_up[...])
    grad_contract_down[...] = product_rows(back_contract[...], activated)
    grad_expand_up[...] = product_rows(middle_expand[...], grads)

    @pl.when(step_at == pl.num_programs(0) - 1)
    def _():
        sums[...] = jnp.zeros_like(sums)
        last_middle = middle_contract[...].astype(bf16)
        last_back = back_expand[...].astype(bf16)
        grad_contract_up[...] = product_rows(last_middle, grad_branch[...])
        grad_expand_down[...] = product_rows(last_back, entering[...])

        def add(which, values):
            sums[which : which + 1] += jnp.sum(values, axis=0, keepdims=True)

        def step(rows):
            out = branch[rows] + product(middle_contract[rows].astype(bf16), contract_up[...])
            tokens = middle_tokens[rows]
            block_output[rows] = (tokens + row(GATE_EXPAND) * out).astype(bf16)
            cotangents = cotangent[rows].astype(f32)
            add(GATE_EXPAND, cotangents * out)
            grad = grad_entering[rows] + product(back_expand[rows].astype(bf16), expand_down[...])
            normed, inverse = normalize(tokens)
            add(SHIFT_EXPAND, grad)
            add(SCALE_EXPAND, grad * normed)
            grad = cotangents + normalize_back(grad * (1.0 + row(SCALE_EXPAND)), normed, inverse)
            grad_middle[rows] = grad
            add(GATE_ATTEND, grad * branch_attend[rows])
            grad = (grad * row(GATE_ATTEND)).astype(bf16)
            grad_branch_attend[rows] = grad
            back = product_back(grad, project_up[...]).astype(bf16)
            back_project[rows] = back
            grad_attended[rows] = (
                product_back(grad, project[...].reshape(D, D)) + product(back, project_down[...])
            ).astype(bf16)

        each_chunk(rows_all, step)
        grad_project_up[...] = product_rows(middle_project[...], grad_branch_attend[...])
        grad_project_down[...] = product_rows(back_project[...], attended[...])


def feed(latents, attended, cotangent, modulation, packed, chosen):
    rows = latents.shape[0]
    groups, nine, _ = packed.shape
    deep = nine // 9
    together = TILE // (4 * deep)
    project_down, project_up, expand_down, expand_up, contract_down, contract_up = chosen
    tile = pl.BlockSpec((RANK, TILE), lambda j: (0, j))
    narrow = whole((RANK, D))

    def buffer(columns, dtype):
        return pltpu.VMEM((rows, columns), dtype)

    return pl.pallas_call(
        feed_kernel,
        grid=(FF // TILE,),
        in_specs=[
            whole((rows, D)),
            whole((rows, D)),
            whole((rows, D)),
            whole(modulation.shape),
            pl.BlockSpec((groups, deep, D), lambda j: (0, 4, 0)),
            pl.BlockSpec((groups, deep, TILE), lambda j: (0, 5 + j // 2, j % 2)),
            pl.BlockSpec((together, 4 * deep, D), lambda j: (j, 0, 0)),
            narrow,
            narrow,
            narrow,
            tile,
            tile,
            narrow,
        ],
        out_specs=[
            whole((rows, D)),
            whole((rows, D)),
            whole((rows, D)),
            whole((8, D)),
            narrow,
            narrow,
            narrow,
            tile,
            tile,
            narrow,
        ],
        out_shape=[
            jax.ShapeDtypeStruct((rows, D), bf16),
            jax.ShapeDtypeStruct((rows, D), f32),
            jax.ShapeDtypeStruct((rows, D), bf16),
            jax.ShapeDtypeStruct((8, D), f32),
            jax.ShapeDtypeStruct((RANK, D), f32),
            jax.ShapeDtypeStruct((RANK, D), f32),
            jax.ShapeDtypeStruct((RANK, D), f32),
            jax.ShapeDtypeStruct((RANK, FF), f32),
            jax.ShapeDtypeStruct((RANK, FF), f32),
            jax.ShapeDtypeStruct((RANK, D), f32),
        ],
        scratch_shapes=[
            buffer(D, f32),
            buffer(D, f32),
            buffer(D, bf16),
            buffer(D, bf16),
            buffer(D, f32),
            buffer(D, f32),
            buffer(RANK, bf16),
            buffer(RANK, bf16),
            buffer(RANK, f32),
            buffer(RANK, bf16),
            buffer(RANK, f32),
            buffer(D, bf16),
            buffer(RANK, bf16),
        ],
        compiler_params=params(),
        name="feed",
    )(latents, attended, cotangent, modulation, packed, packed, packed,
      project_down, project_up, expand_down, expand_up, contract_down, contract_up)


def leave_kernel(
    grad_queries, grad_own, grad_other, weight, down, up, entering, middle, latents, modulation,
    grad_middle, input_grad, sums, grad_down, grad_up, back
):
    step_at = pl.program_id(0)
    rows_all = latents.shape[0]

    def accumulate(grads):
        grad_up[...] = product_rows(middle[...], grads)
        first = product_back(grads, weight[...].reshape(D, TILE))
        second = product_back(grads, up[...])

        @pl.when(step_at == 0)
        def _():
            input_grad[...] = first
            back[...] = second

        @pl.when(step_at > 0)
        def _():
            input_grad[...] += first
            back[...] += second

    @pl.when(step_at < D // TILE)
    def _():
        accumulate(grad_queries[...])

    @pl.when(step_at >= D // TILE)
    def _():
        accumulate((grad_own[0] + grad_other[0]).astype(bf16))

    @pl.when(step_at == pl.num_programs(0) - 1)
    def _():
        sums[...] = jnp.zeros_like(sums)
        grad_down[...] = product_rows(back[...].astype(bf16), entering[...])

        def step(rows):
            grad = input_grad[rows] + product(back[rows].astype(bf16), down[...])
            normed, inverse = normalize(latents[rows].astype(f32))
            sums[0:1] += jnp.sum(grad, axis=0, keepdims=True)
            sums[1:2] += jnp.sum(grad * normed, axis=0, keepdims=True)
            grad = grad * (1.0 + modulation[SCALE_ATTEND : SCALE_ATTEND + 1])
            input_grad[rows] = grad_middle[rows] + normalize_back(grad, normed, inverse)

        each_chunk(rows_all, step)


def leave(grad_queries, grad_own, grad_other, weight, down, up, entering, middle, latents,
          modulation, grad_middle):
    rows = latents.shape[0]
    groups, deep, columns = weight.shape
    each = D // TILE

    def pair(j):
        later = jnp.maximum(j - each, 0)
        return later // each, 0, later % each

    tile = pl.BlockSpec((RANK, TILE), lambda j: (0, j))
    return pl.pallas_call(
        leave_kernel,
        grid=(columns // TILE,),
        in_specs=[
            pl.BlockSpec((rows, TILE), lambda j: (0, jnp.minimum(j, each - 1))),
            pl.BlockSpec((1, rows, TILE), pair),
            pl.BlockSpec((1, rows, TILE), pair),
            pl.BlockSpec((groups, deep, TILE), lambda j: (0, 0, j)),
            whole(down.shape),
            tile,
            whole((rows, D)),
            whole((rows, RANK)),
            whole((rows, D)),
            whole(modulation.shape),
            whole((rows, D)),
        ],
        out_specs=[whole((rows, D)), whole((8, D)), whole((RANK, D)), tile],
        out_shape=[
            jax.ShapeDtypeStruct((rows, D), f32),
            jax.ShapeDtypeStruct((8, D), f32),
            jax.ShapeDtypeStruct((RANK, D), f32),
            jax.ShapeDtypeStruct((RANK, columns), f32),
        ],
        scratch_shapes=[pltpu.VMEM((rows, RANK), f32)],
        compiler_params=params(),
        name="leave",
    )(grad_queries, grad_own, grad_other, weight, down, up, entering, middle, latents, modulation,
      grad_middle)


WIDTHS = (D, 6 * D, D, 3 * D, D, D, D, FF, FF, D)


def swap_cores(values):
    return lax.ppermute(values, "seq", [(0, 1), (1, 0)])


def pick_kernel(starts, choice_ref, tables_ref, out_ref):
    lanes = lax.broadcasted_iota(jnp.int32, tables_ref.shape[1:], 1)
    for latent in range(out_ref.shape[0]):
        picked = tables_ref[choice_ref[latent, 0]]
        for member in range(1, 5):
            picked = jnp.where(lanes >= starts[member], tables_ref[choice_ref[latent, member]], picked)
        out_ref[latent] = picked


def pick_tables(starts, choice, tables):
    return pl.pallas_call(
        lambda *refs: pick_kernel(starts, *refs),
        out_shape=jax.ShapeDtypeStruct((choice.shape[0],) + tables.shape[1:], tables.dtype),
        in_specs=[pl.BlockSpec(memory_space=pltpu.SMEM), pl.BlockSpec(memory_space=pltpu.VMEM)],
        out_specs=pl.BlockSpec(memory_space=pltpu.VMEM),
        name="pick_tables",
    )(choice, tables)


def table_sum_kernel(starts, choice_ref, grads_ref, out_ref):
    lanes = lax.broadcasted_iota(jnp.int32, grads_ref.shape[1:], 1)
    out_ref[...] = jnp.zeros_like(out_ref)
    for latent in range(grads_ref.shape[0]):
        grads = grads_ref[latent]
        for member in range(5):
            inside = jnp.logical_and(lanes >= starts[member], lanes < starts[member + 1])
            out_ref[choice_ref[latent, member]] += jnp.where(inside, grads, 0.0)


def table_sums(starts, choice, grads):
    return pl.pallas_call(
        lambda *refs: table_sum_kernel(starts, *refs),
        out_shape=jax.ShapeDtypeStruct((NADAPT,) + grads.shape[1:], f32),
        in_specs=[pl.BlockSpec(memory_space=pltpu.SMEM), pl.BlockSpec(memory_space=pltpu.VMEM)],
        out_specs=pl.BlockSpec(memory_space=pltpu.VMEM),
        name="table_sums",
    )(choice, grads)


def regroup(gathered, devices):
    if devices <= GROUPS:
        return gathered
    deep = D // devices
    pieces = [gathered[:, : 4 * deep].reshape(GROUPS, -1, D)]
    for part in range(4, 9):
        pieces.append(gathered[:, part * deep : (part + 1) * deep].reshape(GROUPS, -1, D))
    return jnp.concatenate(pieces, axis=1)


def make_local(chips):
    devices = 2 * chips
    own = tuple(width // devices for width in WIDTHS)
    span = sum(own)
    padded = -(-span // 128) * 128
    offsets = [sum(own[:member]) for member in range(11)]
    starts = tuple(offsets[0:11:2])
    chip_rows = D // chips

    def local(
        latents,
        condition,
        adapter_choice,
        cotangent,
        modulate_weight,
        attend_weight,
        project_weight,
        expand_weight,
        contract_weight,
        *tables,
    ):
        chip = lax.axis_index("dp")
        core = lax.axis_index("seq")

        def half(array, which, axis):
            size = array.shape[axis] // 2
            return lax.dynamic_slice_in_dim(array, which * size, size, axis)

        def to_chips(values):
            return lax.all_to_all(values, "dp", split_axis=0, concat_axis=0, tiled=True)

        packed = jnp.concatenate(
            [contract_weight, project_weight]
            + [expand_weight[:, part * D : (part + 1) * D] for part in range(4)],
            axis=0,
        )
        attend_all = lax.all_gather(attend_weight, ("dp", "seq"), axis=0, tiled=True)
        attend_all = attend_all.reshape(GROUPS, D // GROUPS, 3 * D)
        gathered = regroup(
            lax.all_gather(packed, ("dp", "seq"), axis=0, tiled=False), devices
        )
        wide = D // devices
        modulate_mine = half(modulate_weight, core, 1)
        modulate_other = swap_cores(half(modulate_weight, 1 - core, 1))

        note = jnp.concatenate(
            [condition, jnp.pad(adapter_choice.astype(bf16), ((0, 0), (0, 123)))], axis=1
        )
        notes = to_chips(jnp.broadcast_to(note, (chips, note.shape[1])))
        choice = notes[:, D : D + 5].astype(jnp.int32)
        lifted_all = jax.nn.silu(notes[:, :D].astype(f32)).astype(bf16)

        lifted_mine = lax.dynamic_slice_in_dim(lifted_all, (2 * chip + core) * wide, wide, 1)
        lifted_other = lax.dynamic_slice_in_dim(lifted_all, (2 * chip + 1 - core) * wide, wide, 1)
        partial = product(lifted_mine, modulate_mine) + product(lifted_other, modulate_other)
        partial_high = lax.reduce_precision(partial, 8, 7)
        partial_low = (partial - partial_high).astype(bf16)
        partial_high = partial_high.astype(bf16)

        mine = [
            table.transpose(0, 2, 1) if member % 2 == 0 else table
            for member, table in enumerate(tables)
        ]
        mine = jnp.pad(jnp.concatenate(mine, axis=2), ((0, 0), (0, 0), (0, padded - span)))
        picked = pick_tables(starts, choice, mine)
        block = jnp.concatenate([picked.reshape(chips, RANK * padded), partial_high, partial_low], axis=1)
        block = to_chips(block)
        summed = jnp.sum(
            block[:, RANK * padded : RANK * padded + 3 * D].astype(f32)
            + block[:, RANK * padded + 3 * D :].astype(f32),
            axis=0,
        )
        both = jnp.concatenate([summed, swap_cores(summed)])
        modulation = jnp.where(core == 0, both, jnp.roll(both, 3 * D))[None]
        near = block[:, : RANK * padded].reshape(chips, 1, RANK, padded)
        far = swap_cores(near)
        pair = jnp.concatenate(
            [jnp.where(core == 0, near, far), jnp.where(core == 0, far, near)], axis=1
        )
        pair = pair.transpose(2, 0, 1, 3)
        chosen = [
            pair[..., offsets[member] : offsets[member + 1]].reshape(RANK, WIDTHS[member])
            for member in range(10)
        ]

        lifted_float, silu_pull = jax.vjp(jax.nn.silu, condition.astype(f32))
        lifted = lifted_float.astype(bf16)
        middle_modulate = product_back(lifted, chosen[0]).astype(bf16)
        modulation = modulation + product(middle_modulate, chosen[1])
        shift_attend, scale_attend, gate_attend, shift_expand, scale_expand, gate_expand = jnp.split(
            modulation, 6, axis=1
        )

        modulation = jnp.pad(modulation.reshape(6, D), ((0, 2), (0, 0)))

        tokens = latents[0]
        projected, entering, middle_attend = enter(
            tokens, modulation, attend_all, chosen[2], chosen[3]
        )
        other = swap_cores(projected[:, D:])
        attended, logsum = attend(projected, other)
        (
            block_output,
            grad_middle,
            grad_attended,
            sums_feed,
            grad_project_down,
            grad_project_up,
            grad_expand_down,
            grad_expand_up,
            grad_contract_down,
            grad_contract_up,
        ) = feed(tokens, attended, cotangent[0], modulation, gathered, chosen[4:])
        grad_queries, grad_near, grad_far = attend_back(projected, other, grad_attended, logsum)
        input_grad, sums_attend, grad_attend_down, grad_attend_up = leave(
            grad_queries,
            grad_near,
            swap_cores(grad_far),
            attend_all,
            chosen[2],
            chosen[3],
            entering,
            middle_attend,
            tokens,
            modulation,
            grad_middle,
        )

        partial_modulation = (sums_attend + sums_feed)[:6].reshape(1, 6 * D)
        grad_modulation = (partial_modulation + swap_cores(partial_modulation)).astype(bf16)
        grad_middle_modulate = product_back(grad_modulation, chosen[1]).astype(bf16)
        keep = (core == 0).astype(f32)
        grad_modulate_down = product_rows(grad_middle_modulate, lifted) * keep
        grad_modulate_up = product_rows(middle_modulate, grad_modulation) * keep

        table_grads = [
            grad_modulate_down,
            grad_modulate_up,
            grad_attend_down,
            grad_attend_up,
            grad_project_down,
            grad_project_up,
            grad_expand_down,
            grad_expand_up,
            grad_contract_down,
            grad_contract_up,
        ]
        sent = jnp.concatenate(
            [grad.reshape(RANK, chips, 2, width) for grad, width in zip(table_grads, own)], axis=3
        )
        sent = jnp.pad(sent, ((0, 0), (0, 0), (0, 0), (0, padded - span))).transpose(2, 1, 0, 3)
        near = lax.dynamic_index_in_dim(sent, core, 0, keepdims=False)
        far = lax.dynamic_index_in_dim(sent, 1 - core, 0, keepdims=False)
        arrived = to_chips(near + swap_cores(far))
        owned = table_sums(starts, choice, arrived)
        owned = [owned[:, :, offsets[member] : offsets[member + 1]] for member in range(10)]
        owned = [
            grad.transpose(0, 2, 1) if member % 2 == 0 else grad for member, grad in enumerate(owned)
        ]

        modulations = to_chips(jnp.broadcast_to(grad_modulation, (chips, 6 * D)))
        grad_lifted = product_back(modulations, modulate_weight)
        grad_lifted = to_chips(grad_lifted)
        near, far = grad_lifted[:, None], swap_cores(grad_lifted)[:, None]
        grad_lifted = jnp.concatenate(
            [jnp.where(core == 0, near, far), jnp.where(core == 0, far, near)], axis=1
        ).reshape(1, D)
        grad_lifted = grad_lifted + product(grad_middle_modulate, chosen[0])
        condition_grad = silu_pull(grad_lifted)[0]
        return (block_output[None], input_grad[None], condition_grad, *owned)

    return local


def solution(mesh):
    rows = P(("dp", "seq"), None)
    down = P(None, ("dp", "seq"), None)
    up = P(None, None, ("dp", "seq"))
    tokens = P("dp", "seq", None)
    return jax.shard_map(
        make_local(mesh.shape["dp"]),
        mesh=mesh,
        in_specs=(tokens, P("dp", None), P("dp", None), tokens) + (rows,) * 5 + (down, up) * 5,
        out_specs=(tokens, tokens, P("dp", None)) + (down, up) * 5,
        check_vma=False,
    )
```

```python
import jax
import jax.numpy as jnp
from jax import lax
from jax.experimental import pallas as pl
from jax.experimental.pallas import tpu as pltpu
from jax.sharding import PartitionSpec as P

D = 1024
HEADS = 16
HEAD_DIM = 64
FF = 4096
RANK = 16
bf16 = jnp.bfloat16
f32 = jnp.float32
EPSILON = 1e-06
TINY = pl.CostEstimate(flops=1, bytes_accessed=1, transcendentals=0)
LOG2E = 1.4426950408889634
GROUP = 256
TILE = 512
NADAPT = 8
CHUNK = 128
VMEM_LIMIT = 56 * 1024 * 1024
FIRST_ROWS = 48
SHIFT_ATTEND, SCALE_ATTEND, GATE_ATTEND, SHIFT_EXPAND, SCALE_EXPAND, GATE_EXPAND = range(6)


def product(left, right):
    return lax.dot_general(left, right, (((1,), (0,)), ((), ())), preferred_element_type=f32)


def product_back(grads, right):
    return lax.dot_general(grads, right, (((1,), (1,)), ((), ())), preferred_element_type=f32)


def product_rows(left, right):
    return lax.dot_general(left, right, (((0,), (0,)), ((), ())), preferred_element_type=f32)


def normalize(values):
    centred = values - jnp.mean(values, axis=-1, keepdims=True)
    variance = jnp.mean(centred * centred, axis=-1, keepdims=True)
    inverse = lax.rsqrt(variance + EPSILON)
    return centred * inverse, inverse


def normalize_back(grads, normed, inverse):
    mean = jnp.mean(grads, axis=-1, keepdims=True)
    along = jnp.mean(grads * normed, axis=-1, keepdims=True)
    return (grads - mean - normed * along) * inverse


def each_chunk(rows, step):
    def body(position, carry):
        step(pl.ds(pl.multiple_of(position * CHUNK, CHUNK), CHUNK))
        return carry

    lax.fori_loop(0, rows // CHUNK, body, 0)


def whole(shape):
    return pl.BlockSpec(shape, lambda *_: (0,) * len(shape))


def params():
    return pltpu.CompilerParams(vmem_limit_bytes=VMEM_LIMIT)


def piece_places(place, far, relative):
    chip_z, chip_y, chip_x, core = (place[axis] for axis in range(4))
    for dz in range(4):
        z = lax.rem(chip_z + 4 - dz, 4) if relative else dz
        for dy in range(2):
            for dx in range(2):
                chip = z * 4 + (chip_y ^ dy) * 2 + (chip_x ^ dx)
                yield dz, dy, dx, chip * 2 + (core ^ far)


def crossed(refs, half, dz, dy, dx):
    if half == 0:
        return refs[2 * dy].at[dx, dz % 2]
    return refs[1 + 2 * dx].at[dy, dz % 2]


def wait_for(target, semaphore):
    pltpu.make_async_copy(target, target, semaphore).wait()


def fetch_attend(place, refs, weight, semaphores):
    if len(refs) == 1:
        for half in range(2):
            columns = pl.ds(half * (3 * D // 2), 3 * D // 2)
            pltpu.make_async_copy(
                refs[0].at[:, columns], weight.at[:, columns], semaphores.at[half]
            ).start()
        return
    for half in range(2):
        columns = pl.ds(half * (3 * D // 2), 3 * D // 2)
        for far in range(2):
            for dz, dy, dx, device in piece_places(place, far, True):
                rows = pl.ds(pl.multiple_of(device * 32, 32), 32)
                pltpu.make_async_copy(
                    crossed(refs[4 * far : 4 * far + 4], dz // 2, dz, dy, dx).at[:, columns],
                    weight.at[rows, columns],
                    semaphores.at[half],
                ).start()


def wait_attend(weight, semaphores, half):
    columns = pl.ds(half * (3 * D // 2), 3 * D // 2)
    wait_for(weight.at[:, columns], semaphores.at[half])


def fetch_feed(place, refs, project, expand, contract, semaphores):
    if len(refs) == 3:
        pltpu.make_async_copy(refs[0], project, semaphores.at[0]).start()
        for tile in range(FF // TILE):
            pltpu.make_async_copy(
                refs[1].at[:, pl.ds(tile * TILE, TILE)],
                expand.at[tile // 2, tile % 2],
                semaphores.at[1],
            ).start()
        pltpu.make_async_copy(refs[2], contract, semaphores.at[2]).start()
        return

    def each(step):
        for far in range(2):
            for dz, dy, dx, device in piece_places(place, far, False):
                step(far, dz, dy, dx, device)

    def rows_of(device, deep, first, count):
        return pl.ds(pl.multiple_of(device * deep + first, 16), count)

    def main_rows(first, count, far, dz, dy, dx):
        held = refs[7 * far : 7 * far + 7]
        block = (
            held[0].at[dz] if dy + dx == 0 else held[2 * (dx + 2 * dy) - 1 + dz // 2].at[dz % 2]
        )
        return block.at[pl.ds(first, count)]

    def from_project(far, dz, dy, dx, device):
        pltpu.make_async_copy(
            main_rows(0, 32, far, dz, dy, dx),
            project.at[rows_of(device, 32, 0, 32)],
            semaphores.at[0],
        ).start()

    def from_expand(far, dz, dy, dx, device):
        for part in range(4):
            for half in range(2):
                pltpu.make_async_copy(
                    main_rows(32 * (1 + part), 32, far, dz, dy, dx).at[:, pl.ds(half * TILE, TILE)],
                    expand.at[part, half, rows_of(device, 32, 0, 32)],
                    semaphores.at[1],
                ).start()

    def from_contract(far, dz, dy, dx, device):
        pltpu.make_async_copy(
            main_rows(160, FIRST_ROWS, far, dz, dy, dx),
            contract.at[rows_of(device, 128, 0, FIRST_ROWS)],
            semaphores.at[2],
        ).start()
        pltpu.make_async_copy(
            refs[14 + far].at[dz, 2 * dy + dx],
            contract.at[rows_of(device, 128, FIRST_ROWS, 128 - FIRST_ROWS)],
            semaphores.at[2],
        ).start()

    each(from_project)
    each(from_expand)
    each(from_contract)


def smem():
    return pl.BlockSpec(memory_space=pltpu.SMEM)


def anywhere(arrays):
    return [pl.BlockSpec(memory_space=pltpu.HBM)] * len(arrays)


def enter_kernel(count, place, latents, modulation, down, up, *refs):
    weights = refs[:count]
    queries, keys_values, entering, middle, weight, semaphores = refs[count:]
    step_at = pl.program_id(0)

    @pl.when(step_at == 0)
    def _():
        fetch_attend(place, weights, weight, semaphores)

        def step(rows):
            normed, _ = normalize(latents[rows].astype(f32))
            values = normed * (1.0 + modulation[SCALE_ATTEND : SCALE_ATTEND + 1]) + modulation[
                SHIFT_ATTEND : SHIFT_ATTEND + 1
            ]
            values = values.astype(bf16)
            entering[rows] = values
            middle[rows] = product_back(values, down[...]).astype(bf16)

        each_chunk(latents.shape[0], step)
        wait_attend(weight, semaphores, 0)
        wait_attend(weight, semaphores, 1)

    here = pl.ds(pl.multiple_of(step_at * TILE, TILE), TILE)
    projected = (
        product(entering[...], weight[:, here]) + product(middle[...], up[...])
    ).astype(bf16)

    @pl.when(step_at < D // TILE)
    def _():
        queries[...] = projected

    @pl.when(step_at >= D // TILE)
    def _():
        keys_values[...] = projected


def enter(place, latents, modulation, weights, down, up):
    rows = latents.shape[0]
    columns = up.shape[1]
    return pl.pallas_call(
        lambda *refs: enter_kernel(len(weights), *refs),
        grid=(columns // TILE,),
        in_specs=[
            smem(),
            whole((rows, D)),
            whole(modulation.shape),
            whole(down.shape),
            pl.BlockSpec((RANK, TILE), lambda j: (0, j)),
        ]
        + anywhere(weights),
        out_specs=[
            pl.BlockSpec((rows, TILE), lambda j: (0, jnp.minimum(j, D // TILE - 1))),
            pl.BlockSpec((rows, TILE), lambda j: (0, jnp.maximum(j - D // TILE, 0))),
            whole((rows, D)),
            whole((rows, RANK)),
        ],
        out_shape=[
            jax.ShapeDtypeStruct((rows, D), bf16),
            jax.ShapeDtypeStruct((rows, columns - D), bf16),
            jax.ShapeDtypeStruct((rows, D), bf16),
            jax.ShapeDtypeStruct((rows, RANK), bf16),
        ],
        scratch_shapes=[pltpu.VMEM((D, columns), bf16), pltpu.SemaphoreType.DMA((2,))],
        compiler_params=params(),
        cost_estimate=TINY,
        name="enter",
    )(place, latents, modulation, down, up, *weights)


def head_mask(head, dtype=jnp.bool_):
    lane = lax.broadcasted_iota(jnp.int32, (1, GROUP), 1)
    return jnp.logical_and(lane >= head * HEAD_DIM, lane < (head + 1) * HEAD_DIM)


def attend_kernel(queries, keys_near, values_near, keys_far, values_far, attended, logsum):
    rows = queries.shape[0]
    block = 256
    scale = HEAD_DIM ** (-0.5)
    lane = lax.broadcasted_iota(jnp.int32, (1, 128), 1)

    for start in range(0, rows, block):
        here = pl.ds(start, block)
        q = queries[here] * jnp.asarray(scale, bf16)
        total = jnp.zeros((block, GROUP), f32)
        sums = jnp.zeros((block, 128), f32)
        for head in range(GROUP // HEAD_DIM):
            mask = head_mask(head)
            mine = jnp.where(mask, q, jnp.zeros_like(q))
            near = product_back(mine, keys_near[...])
            far = product_back(mine, keys_far[...])
            highest = jnp.maximum(
                jnp.max(near, axis=1, keepdims=True), jnp.max(far, axis=1, keepdims=True)
            )
            near = jnp.exp2((near - highest) * LOG2E)
            far = jnp.exp2((far - highest) * LOG2E)
            denominator = jnp.sum(near, axis=1, keepdims=True) + jnp.sum(
                far, axis=1, keepdims=True
            )
            share = 1.0 / denominator
            out = product((near * share).astype(bf16), values_near[...]) + product(
                (far * share).astype(bf16), values_far[...]
            )
            total = jnp.where(mask, out, total)
            sums = jnp.where(lane == head, highest + jnp.log(denominator), sums)
        attended[here] = total.astype(bf16)
        logsum[0, here] = sums


def attend(queries, near, far, first, groups, earlier=None):
    rows = queries.shape[0]
    every = D // GROUP

    def at(start):
        return pl.BlockSpec((rows, GROUP), lambda g: (0, start + first + g))

    given = [] if earlier is None else [earlier]
    return pl.pallas_call(
        lambda *refs: attend_kernel(*refs[:5], *refs[5 + len(given) :]),
        grid=(groups,),
        in_specs=[at(0), at(0), at(every), at(0), at(every)] + anywhere(given),
        out_specs=[at(0), pl.BlockSpec((1, rows, 128), lambda g: (g, 0, 0))],
        out_shape=[
            jax.ShapeDtypeStruct((rows, D), bf16),
            jax.ShapeDtypeStruct((groups, rows, 128), f32),
        ],
        input_output_aliases={5: 0} if given else {},
        compiler_params=params(),
        cost_estimate=TINY,
        name="attend",
    )(queries, near, near, far, far, *given)


def attend_back_kernel(
    queries, keys_near, values_near, keys_far, values_far, grads, logsum,
    grad_queries, grad_near, grad_far, keys_sum, values_sum
):
    rows = queries.shape[0]
    block = 256
    scale = HEAD_DIM ** (-0.5)
    scaled = queries[...] * jnp.asarray(scale, bf16)
    scaled_t = scaled.T
    grads_t = grads[...].T
    for start in range(0, rows, block):
        here = slice(start, start + block)
        q = scaled[here]
        g = grads[here]
        total = jnp.zeros((block, GROUP), f32)
        for head in range(GROUP // HEAD_DIM):
            mask = head_mask(head)
            part = slice(head * HEAD_DIM, (head + 1) * HEAD_DIM)
            mine = jnp.where(mask, q, jnp.zeros_like(q))
            mine_g = jnp.where(mask, g, jnp.zeros_like(g))
            shift = logsum[0, here, head : head + 1]
            pn = jnp.exp2((product_back(mine, keys_near[...]) - shift) * LOG2E)
            pf = jnp.exp2((product_back(mine, keys_far[...]) - shift) * LOG2E)
            gn = product_back(mine_g, values_near[...])
            gf = product_back(mine_g, values_far[...])
            inner = jnp.sum(pn * gn, axis=1, keepdims=True) + jnp.sum(
                pf * gf, axis=1, keepdims=True
            )
            sn = (pn * (gn - inner)).astype(bf16)
            sf = (pf * (gf - inner)).astype(bf16)
            out = product(sn, keys_near[...]) + product(sf, keys_far[...])
            total = jnp.where(mask, out * scale, total)
            vn = product(grads_t[part, here], pn.astype(bf16))
            vf = product(grads_t[part, here], pf.astype(bf16))
            kn = product(scaled_t[part, here], sn)
            kf = product(scaled_t[part, here], sf)
            if start == 0:
                values_sum[part, :rows] = vn
                values_sum[part, rows:] = vf
                keys_sum[part, :rows] = kn
                keys_sum[part, rows:] = kf
            else:
                values_sum[part, :rows] += vn
                values_sum[part, rows:] += vf
                keys_sum[part, :rows] += kn
                keys_sum[part, rows:] += kf
        grad_queries[here] = total.astype(bf16)
    grad_near[0] = keys_sum[:, :rows].T
    grad_near[1] = values_sum[:, :rows].T
    grad_far[0] = keys_sum[:, rows:].T
    grad_far[1] = values_sum[:, rows:].T


def attend_back(queries, near, far, grads, logsum, first):
    rows = queries.shape[0]
    every = D // GROUP
    groups = logsum.shape[0]

    def at(start):
        return pl.BlockSpec((rows, GROUP), lambda g: (0, start + first + g))

    pair = pl.BlockSpec((2, rows, GROUP), lambda g: (0, 0, g))
    return pl.pallas_call(
        attend_back_kernel,
        grid=(groups,),
        in_specs=[at(0), at(0), at(every), at(0), at(every), at(0),
                  pl.BlockSpec((1, rows, 128), lambda g: (g, 0, 0))],
        out_specs=[pl.BlockSpec((rows, GROUP), lambda g: (0, g)), pair, pair],
        out_shape=[
            jax.ShapeDtypeStruct((rows, groups * GROUP), bf16),
            jax.ShapeDtypeStruct((2, rows, groups * GROUP), f32),
            jax.ShapeDtypeStruct((2, rows, groups * GROUP), f32),
        ],
        scratch_shapes=[pltpu.VMEM((GROUP, 2 * rows), f32), pltpu.VMEM((GROUP, 2 * rows), f32)],
        compiler_params=params(),
        cost_estimate=TINY,
        name="attend_back",
    )(queries, near, near, far, far, grads, logsum)


def gelu_both(values):
    root = 0.7978845608028654
    square = values * values
    inner = jnp.tanh(values * (root + (root * 0.044715) * square))
    half = 0.5 + 0.5 * inner
    slope = half + (0.5 * values) * (1.0 - inner * inner) * (root + (3.0 * root * 0.044715) * square)
    return values * half, slope


def feed_kernel(
    count, place, latents, attended, cotangent, modulation,
    project_down, project_up, expand_down, expand_up, contract_down, contract_up,
    *refs,
):
    weights = refs[:count]
    (
        block_output, grad_middle, grad_attended, sums,
        grad_project_down, grad_project_up, grad_expand_down, grad_expand_up,
        grad_contract_down, grad_contract_up,
        branch_attend, middle_tokens, entering, grad_branch, branch, grad_entering,
        middle_project, middle_expand, middle_contract, back_contract, back_expand,
        grad_branch_attend, back_project, project, expand, contract, semaphores,
    ) = refs[count:]
    step_at = pl.program_id(0)
    rows_all = latents.shape[0]

    def row(which):
        return modulation[which : which + 1]

    @pl.when(step_at == 0)
    def _():
        fetch_feed(place, weights, project, expand, contract, semaphores)
        wait_for(project, semaphores.at[0])

        def step(rows):
            middle = product_back(attended[rows], project_down[...]).astype(bf16)
            middle_project[rows] = middle
            out = product(attended[rows], project[...]) + product(
                middle, project_up[...]
            )
            branch_attend[rows] = out
            tokens = latents[rows].astype(f32) + row(GATE_ATTEND) * out
            middle_tokens[rows] = tokens
            normed, _ = normalize(tokens)
            values = (normed * (1.0 + row(SCALE_EXPAND)) + row(SHIFT_EXPAND)).astype(bf16)
            entering[rows] = values
            middle_expand[rows] = product_back(values, expand_down[...]).astype(bf16)
            grads = (cotangent[rows].astype(f32) * row(GATE_EXPAND)).astype(bf16)
            grad_branch[rows] = grads
            back_contract[rows] = product_back(grads, contract_up[...]).astype(bf16)
            branch[rows] = jnp.zeros((CHUNK, D), f32)
            grad_entering[rows] = jnp.zeros((CHUNK, D), f32)
            middle_contract[rows] = jnp.zeros((CHUNK, RANK), f32)
            back_expand[rows] = jnp.zeros((CHUNK, RANK), f32)

        each_chunk(rows_all, step)
        wait_for(expand, semaphores.at[1])
        wait_for(contract, semaphores.at[2])

    wide = expand[step_at // 2, step_at % 2]
    deep = contract[pl.ds(pl.multiple_of(step_at * TILE, TILE), TILE)]
    hidden = product(entering[...], wide) + product(middle_expand[...], expand_up[...])
    activated, slope = gelu_both(hidden)
    activated = activated.astype(bf16)
    branch[...] += product(activated, deep)
    middle_contract[...] += product_back(activated, contract_down[...])
    grads = product_back(grad_branch[...], deep) + product(back_contract[...], contract_down[...])
    grads = (grads * slope).astype(bf16)
    grad_entering[...] += product_back(grads, wide)
    back_expand[...] += product_back(grads, expand_up[...])
    grad_contract_down[...] = product_rows(back_contract[...], activated)
    grad_expand_up[...] = product_rows(middle_expand[...], grads)

    @pl.when(step_at == pl.num_programs(0) - 1)
    def _():
        sums[...] = jnp.zeros_like(sums)
        last_middle = middle_contract[...].astype(bf16)
        last_back = back_expand[...].astype(bf16)
        grad_contract_up[...] = product_rows(last_middle, grad_branch[...])
        grad_expand_down[...] = product_rows(last_back, entering[...])

        def add(which, values):
            sums[which : which + 1] += jnp.sum(values, axis=0, keepdims=True)

        def step(rows):
            out = branch[rows] + product(middle_contract[rows].astype(bf16), contract_up[...])
            tokens = middle_tokens[rows]
            block_output[rows] = (tokens + row(GATE_EXPAND) * out).astype(bf16)
            cotangents = cotangent[rows].astype(f32)
            add(GATE_EXPAND, cotangents * out)
            grad = grad_entering[rows] + product(back_expand[rows].astype(bf16), expand_down[...])
            normed, inverse = normalize(tokens)
            add(SHIFT_EXPAND, grad)
            add(SCALE_EXPAND, grad * normed)
            grad = cotangents + normalize_back(grad * (1.0 + row(SCALE_EXPAND)), normed, inverse)
            grad_middle[rows] = grad
            add(GATE_ATTEND, grad * branch_attend[rows])
            grad = (grad * row(GATE_ATTEND)).astype(bf16)
            grad_branch_attend[rows] = grad
            back = product_back(grad, project_up[...]).astype(bf16)
            back_project[rows] = back
            grad_attended[rows] = (
                product_back(grad, project[...]) + product(back, project_down[...])
            ).astype(bf16)

        each_chunk(rows_all, step)
        grad_project_up[...] = product_rows(middle_project[...], grad_branch_attend[...])
        grad_project_down[...] = product_rows(back_project[...], attended[...])


def feed(place, latents, attended, cotangent, modulation, weights, chosen):
    rows = latents.shape[0]
    project_down, project_up, expand_down, expand_up, contract_down, contract_up = chosen
    tile = pl.BlockSpec((RANK, TILE), lambda j: (0, j))
    narrow = whole((RANK, D))

    def buffer(columns, dtype):
        return pltpu.VMEM((rows, columns), dtype)

    return pl.pallas_call(
        lambda *refs: feed_kernel(len(weights), *refs),
        grid=(FF // TILE,),
        in_specs=[
            smem(),
            whole((rows, D)),
            whole((rows, D)),
            whole((rows, D)),
            whole(modulation.shape),
            narrow,
            narrow,
            narrow,
            tile,
            tile,
            narrow,
        ]
        + anywhere(weights),
        out_specs=[
            whole((rows, D)),
            whole((rows, D)),
            whole((rows, D)),
            whole((8, D)),
            narrow,
            narrow,
            narrow,
            tile,
            tile,
            narrow,
        ],
        out_shape=[
            jax.ShapeDtypeStruct((rows, D), bf16),
            jax.ShapeDtypeStruct((rows, D), f32),
            jax.ShapeDtypeStruct((rows, D), bf16),
            jax.ShapeDtypeStruct((8, D), f32),
            jax.ShapeDtypeStruct((RANK, D), f32),
            jax.ShapeDtypeStruct((RANK, D), f32),
            jax.ShapeDtypeStruct((RANK, D), f32),
            jax.ShapeDtypeStruct((RANK, FF), f32),
            jax.ShapeDtypeStruct((RANK, FF), f32),
            jax.ShapeDtypeStruct((RANK, D), f32),
        ],
        scratch_shapes=[
            buffer(D, f32),
            buffer(D, f32),
            buffer(D, bf16),
            buffer(D, bf16),
            buffer(D, f32),
            buffer(D, f32),
            buffer(RANK, bf16),
            buffer(RANK, bf16),
            buffer(RANK, f32),
            buffer(RANK, bf16),
            buffer(RANK, f32),
            buffer(D, bf16),
            buffer(RANK, bf16),
            pltpu.VMEM((D, D), bf16),
            pltpu.VMEM((4, 2, D, TILE), bf16),
            pltpu.VMEM((FF, D), bf16),
            pltpu.SemaphoreType.DMA((3,)),
        ],
        compiler_params=params(),
        cost_estimate=TINY,
        name="feed",
    )(place, latents, attended, cotangent, modulation,
      project_down, project_up, expand_down, expand_up, contract_down, contract_up, *weights)


def leave_kernel(
    count, place, queries_0, queries_1, own_0, own_1, other_0, other_1, down, up, entering, middle,
    latents, modulation, grad_middle, *refs,
):
    weights = refs[:count]
    input_grad, sums, grad_down, grad_up, back, weight, semaphores = refs[count:]
    step_at = pl.program_id(0)
    rows_all = latents.shape[0]

    @pl.when(step_at == 0)
    def _():
        fetch_attend(place, weights, weight, semaphores)
        wait_attend(weight, semaphores, 0)

    @pl.when(step_at == 3)
    def _():
        wait_attend(weight, semaphores, 1)

    here = pl.ds(pl.multiple_of(leave_tile(step_at) * TILE, TILE), TILE)

    def accumulate(grads):
        grad_up[...] = product_rows(middle[...], grads)
        first = product_back(grads, weight[:, here])
        second = product_back(grads, up[...])

        @pl.when(step_at == 0)
        def _():
            input_grad[...] = first
            back[...] = second

        @pl.when(step_at > 0)
        def _():
            input_grad[...] += first
            back[...] += second

    @pl.when(step_at == 0)
    def _():
        accumulate(queries_0[...])

    @pl.when(step_at == 1)
    def _():
        accumulate(queries_1[...])

    @pl.when(jnp.logical_or(step_at == 2, step_at == 4))
    def _():
        accumulate((own_0[0] + other_0[0]).astype(bf16))

    @pl.when(jnp.logical_or(step_at == 3, step_at == 5))
    def _():
        accumulate((own_1[0] + other_1[0]).astype(bf16))

    @pl.when(step_at == pl.num_programs(0) - 1)
    def _():
        sums[...] = jnp.zeros_like(sums)
        grad_down[...] = product_rows(back[...].astype(bf16), entering[...])

        def step(rows):
            grad = input_grad[rows] + product(back[rows].astype(bf16), down[...])
            normed, inverse = normalize(latents[rows].astype(f32))
            sums[0:1] += jnp.sum(grad, axis=0, keepdims=True)
            sums[1:2] += jnp.sum(grad * normed, axis=0, keepdims=True)
            grad = grad * (1.0 + modulation[SCALE_ATTEND : SCALE_ATTEND + 1])
            input_grad[rows] = grad_middle[rows] + normalize_back(grad, normed, inverse)

        each_chunk(rows_all, step)


def leave_tile(step_at):
    return step_at


def leave(place, queries, own, other, weights, down, up, entering, middle, latents, modulation,
          grad_middle):
    rows = latents.shape[0]
    columns = up.shape[1]
    tile = pl.BlockSpec((RANK, TILE), lambda j: (0, leave_tile(j)))
    pair = pl.BlockSpec((1, rows, TILE), lambda j: (j // 4, 0, 0))
    return pl.pallas_call(
        lambda *refs: leave_kernel(len(weights), *refs),
        grid=(columns // TILE,),
        in_specs=[smem()]
        + [whole((rows, TILE))] * 2
        + [pair] * 4
        + [
            whole(down.shape),
            tile,
            whole((rows, D)),
            whole((rows, RANK)),
            whole((rows, D)),
            whole(modulation.shape),
            whole((rows, D)),
        ]
        + anywhere(weights),
        out_specs=[whole((rows, D)), whole((8, D)), whole((RANK, D)), tile],
        out_shape=[
            jax.ShapeDtypeStruct((rows, D), f32),
            jax.ShapeDtypeStruct((8, D), f32),
            jax.ShapeDtypeStruct((RANK, D), f32),
            jax.ShapeDtypeStruct((RANK, columns), f32),
        ],
        scratch_shapes=[
            pltpu.VMEM((rows, RANK), f32),
            pltpu.VMEM((D, columns), bf16),
            pltpu.SemaphoreType.DMA((2,)),
        ],
        compiler_params=params(),
        cost_estimate=TINY,
        name="leave",
    )(place, *queries, *own, *other, down, up, entering, middle, latents, modulation, grad_middle,
      *weights)


PARTS_OF_HALVES = (
    (SHIFT_ATTEND, GATE_ATTEND, SHIFT_EXPAND),
    (SCALE_ATTEND, SCALE_EXPAND, GATE_EXPAND),
)
WIDTHS = (D, 6 * D, D, 3 * D, D, D, D, FF, FF, D)


def swap_cores(values):
    return lax.ppermute(values, "seq", [(0, 1), (1, 0)])


def vmem(count):
    return [pl.BlockSpec(memory_space=pltpu.VMEM)] * count


def rounded_up(span):
    return -(-span // 128) * 128


def note_kernel(condition, choice, out):
    values = condition[...].astype(f32)
    lanes = lax.broadcasted_iota(jnp.int32, (1, 128), 1)
    last = jnp.zeros((1, 128), f32)
    for member in range(5):
        last = jnp.where(lanes == member, choice[0, member].astype(f32), last)
    rows = [values[:, 128 * at : 128 * (at + 1)] for at in range(D // 128)]
    note = jnp.concatenate(rows + [last] + [jnp.zeros((7, 128), f32)], axis=0).astype(bf16)
    for chip in range(out.shape[0]):
        out[chip] = note


def write_notes(chips, condition, choice):
    return pl.pallas_call(
        note_kernel,
        in_specs=vmem(1) + [smem()],
        out_specs=vmem(1)[0],
        out_shape=jax.ShapeDtypeStruct((chips, 16, 128), bf16),
        cost_estimate=TINY,
        name="write_notes",
    )(condition, choice)


def prepare_kernel(early, late, choice, at, lifted, mine, other, tables, out, weight, parts):
    weight[...] = jnp.zeros_like(weight)
    rows = 2 * mine.shape[0]
    m = mine[...].astype(f32)
    o = other[...].astype(f32)
    both = jnp.where(at[1] == 0, jnp.concatenate([m, o]), jnp.concatenate([o, m]))
    weight[pl.ds(pl.multiple_of(at[0], rows), rows)] = both.astype(bf16)
    partial = product(lifted[...], weight[...])
    high = partial.astype(bf16).astype(f32)
    span = parts.shape[2]
    for row in range(8):
        part = slice(row * span, (row + 1) * span)
        parts[:, row] = high[:, part]
        parts[:, 8 + row] = partial[:, part] - high[:, part]
    size = tables.shape[2]
    lanes = lax.broadcasted_iota(jnp.int32, (RANK, size), 1)
    starts = [0, early[0] + early[1], rounded_up(sum(early))]
    starts += [starts[2] + late[0] + late[1], starts[2] + sum(late[:4])]
    for latent in range(out.shape[0]):
        picked = tables[choice[latent, 0]]
        for member in range(1, 5):
            picked = jnp.where(lanes >= starts[member], tables[choice[latent, member]], picked)
        out[latent, :, :size] = picked
        out[latent, :, size:] = parts[latent].astype(bf16)


def prepare(early, late, choice, at, lifted, mine, other, tables):
    chips = choice.shape[0]
    size = tables.shape[2]
    span = mine.shape[1] // 8
    return pl.pallas_call(
        lambda *refs: prepare_kernel(early, late, *refs),
        in_specs=[smem()] * 2 + vmem(4),
        out_specs=vmem(1)[0],
        out_shape=jax.ShapeDtypeStruct((chips, RANK, size + span), bf16),
        scratch_shapes=[
            pltpu.VMEM((128, mine.shape[1]), bf16),
            pltpu.VMEM((chips, 16, span), f32),
        ],
        cost_estimate=TINY,
        name="prepare",
    )(choice, at, lifted, mine, other, tables)


def put_together(own, blocks, first, outs):
    for width, out in zip(own, outs):
        for start in range(0, out.shape[1], 128):
            pieces = []
            for device in range(start // width, (start + 127) // width + 1):
                low = max(start - device * width, 0)
                high = min(start + 128 - device * width, width)
                pieces.append(blocks[device][:, first + low : first + high])
            out[:, start : start + 128] = joined(pieces).astype(bf16)
        first += width


def open_kernel(early, late, core, condition, near, far, *outs):
    tables, (modulation, middle, lifted) = outs[:10], outs[10:]
    size = rounded_up(sum(early)) + rounded_up(sum(late))
    on_first = core[0] == 0
    blocks = []
    near_sum = jnp.zeros((16, near.shape[2] - size), f32)
    far_sum = near_sum
    for chip in range(near.shape[0]):
        n = near[chip].astype(f32)
        f = far[chip].astype(f32)
        near_sum += n[:, size:]
        far_sum += f[:, size:]
        n, f = n[:, :size], f[:, :size]
        blocks += [jnp.where(on_first, n, f), jnp.where(on_first, f, n)]
    put_together(early, blocks, 0, tables[:4])
    put_together(late, blocks, rounded_up(sum(early)), tables[4:])
    near_sum = near_sum[:8] + near_sum[8:]
    far_sum = far_sum[:8] + far_sum[8:]
    values = condition[...].astype(f32)
    lifted[...] = (values * (1.0 / (1.0 + jnp.exp(-values)))).astype(bf16)
    middle[...] = product_back(lifted[...], tables[0][...]).astype(bf16)
    adapted = product(middle[...], tables[1][...])
    halves = (jnp.where(on_first, near_sum, far_sum), jnp.where(on_first, far_sum, near_sum))
    modulation[...] = jnp.zeros_like(modulation)
    for half, targets in zip(halves, PARTS_OF_HALVES):
        for place in range(3 * D // 128):
            row, lane = targets[place // 8], place % 8 * 128
            modulation[row : row + 1, lane : lane + 128] = (
                half[place // 3 : place // 3 + 1, place % 3 * 128 : (place % 3 + 1) * 128]
                + adapted[:, row * D + lane : row * D + lane + 128]
            )


def open_block(early, late, core, condition, near, far):
    chips = near.shape[0]
    shapes = [((RANK, 2 * chips * width), bf16) for width in early + late]
    shapes += [((8, D), f32), ((1, RANK), bf16), ((1, D), bf16)]
    return pl.pallas_call(
        lambda *refs: open_kernel(early, late, *refs),
        in_specs=[smem()] + vmem(3),
        out_specs=vmem(len(shapes)),
        out_shape=[jax.ShapeDtypeStruct(*shape) for shape in shapes],
        compiler_params=params(),
        cost_estimate=TINY,
        name="open_block",
    )(core, condition, near, far)


def joined(pieces):
    return pieces[0] if len(pieces) == 1 else jnp.concatenate(pieces, axis=1)

def pack_into(own, core, grads, out):
    chips, span = out.shape[1], out.shape[3]
    for chip in range(chips):
        for k in range(2):
            device = 2 * chip + k
            pieces = [grad[:, device * width : (device + 1) * width] for width, grad in zip(own, grads)]
            if span > sum(own):
                pieces.append(jnp.zeros((RANK, span - sum(own)), f32))
            out[core[0] ^ k, chip] = joined(pieces)


def pack_late(own, core, grads):
    chips = grads[0].shape[1] // own[0] // 2
    return pl.pallas_call(
        lambda core, *refs: pack_into(own, core, refs[:-1], refs[-1]),
        out_shape=jax.ShapeDtypeStruct((2, chips, RANK, rounded_up(sum(own))), f32),
        in_specs=[smem()] + vmem(len(grads)),
        out_specs=vmem(1)[0],
        cost_estimate=TINY,
        name="pack_late",
    )(core, *grads)


def pack_early_kernel(
    own, core, attend, attend_there, feed, feed_there, middle, lifted, up, down_grad, up_grad,
    out, grad_modulation, grad_middle, modulate_down, modulate_up
):
    early = attend[...] + attend_there[...]
    late = feed[...] + feed_there[...]
    rows = [early[row : row + 1] if row < 2 else late[row : row + 1] for row in range(6)]
    grads = jnp.concatenate(rows, axis=1).astype(bf16)
    grad_modulation[...] = grads
    back = product_back(grads, up[...]).astype(bf16)
    grad_middle[...] = back
    keep = jnp.where(core[0] == 0, 1.0, 0.0)
    modulate_down[...] = product_rows(back, lifted[...]) * keep
    modulate_up[...] = product_rows(middle[...], grads) * keep
    pack_into(own, core, (modulate_down, modulate_up, down_grad, up_grad), out)


def pack_early(own, core, sums, middle, lifted, up, grads):
    chips = grads[0].shape[1] // own[2] // 2
    return pl.pallas_call(
        lambda *refs: pack_early_kernel(own, *refs),
        out_shape=[
            jax.ShapeDtypeStruct((2, chips, RANK, rounded_up(sum(own))), f32),
            jax.ShapeDtypeStruct((1, 6 * D), bf16),
            jax.ShapeDtypeStruct((1, RANK), bf16),
        ],
        in_specs=[smem()] + vmem(9),
        out_specs=vmem(3),
        scratch_shapes=[pltpu.VMEM((RANK, D), f32), pltpu.VMEM((RANK, 6 * D), f32)],
        cost_estimate=TINY,
        name="pack_early",
    )(core, *sums, middle, lifted, up, *grads)


def sums_kernel(own, members, choice, grads, *refs):
    outs, total = refs[:-1], refs[-1]
    lanes = lax.broadcasted_iota(jnp.int32, grads.shape[1:], 1)
    total[...] = jnp.zeros_like(total)
    for latent in range(grads.shape[0]):
        offset = 0
        for pair, member in enumerate(members):
            width = own[2 * pair] + own[2 * pair + 1]
            inside = jnp.logical_and(lanes >= offset, lanes < offset + width)
            total[choice[latent, member]] += jnp.where(inside, grads[latent], 0.0)
            offset += width
    for entry in range(NADAPT):
        values = total[entry]
        offset = 0
        for width, out in zip(own, outs):
            out[entry] = values[:, offset : offset + width]
            offset += width

def table_sums(own, members, choice, grads):
    sums = pl.pallas_call(
        lambda *refs: sums_kernel(own, members, *refs),
        out_shape=[jax.ShapeDtypeStruct((NADAPT, RANK, width), f32) for width in own],
        in_specs=[smem()] + vmem(1),
        out_specs=vmem(len(own)),
        scratch_shapes=[pltpu.VMEM((NADAPT,) + grads.shape[1:], f32)],
        cost_estimate=TINY,
        name="table_sums")(choice, grads)
    return [array.transpose(0, 2, 1) if which % 2 == 0 else array for which, array in enumerate(sums)]


def swap_all(arrays):
    return list(arrays) + [swap_cores(array) for array in arrays]


def after(values, *others):
    return lax.optimization_barrier((values, *others))[0]


def cut_kernel(project, expand, contract, main, last):
    deep = project.shape[0]
    main[:deep] = project[...]
    for part in range(4):
        main[(1 + part) * deep : (2 + part) * deep] = expand[:, part * D : (part + 1) * D]
    main[5 * deep :] = contract[: FIRST_ROWS]
    last[...] = contract[FIRST_ROWS:]


def cut_weights(project_weight, expand_weight, contract_weight):
    rows = contract_weight.shape[0] - FIRST_ROWS
    return pl.pallas_call(
        cut_kernel,
        in_specs=vmem(3),
        out_specs=vmem(2),
        out_shape=[
            jax.ShapeDtypeStruct((5 * project_weight.shape[0] + FIRST_ROWS, D), bf16),
            jax.ShapeDtypeStruct((rows, D), bf16),
        ],
        cost_estimate=TINY,
        name="cut_weights",
    )(project_weight, expand_weight, contract_weight)


class PermutedGather:
    chips = 16

    def exchange(self, values, over):
        return lax.ppermute(values, "dp", [(chip, chip ^ over) for chip in range(self.chips)])

    def along(self, values, step=1):
        return lax.ppermute(
            values, "dp", [(chip, (chip + 4 * step) % self.chips) for chip in range(self.chips)]
        )

    def begin(self, attend_weight, project_weight, expand_weight, contract_weight):
        main, last = cut_weights(project_weight, expand_weight, contract_weight)
        self.attend = [attend_weight] + [self.along(attend_weight, step) for step in (1, 2, 3)]
        self.main = self.lines(main)
        self.last = last
        self.attend_crossed = self.cross(jnp.stack(self.attend[:2]), jnp.stack(self.attend[2:]))
        return [self.attend_crossed[1], self.attend_crossed[3]]

    def cross_last(self):
        self.plane = [self.last] + [self.exchange(self.last, over) for over in (1, 2, 3)]
        return self.plane[1:]

    def lines(self, values):
        groups = [[z * 4 + line for z in range(self.chips // 4)] for line in range(4)]
        return lax.all_gather(values, "dp", axis=0, tiled=False, axis_index_groups=groups)

    def cross(self, first, second):
        return first, self.exchange(first, 1), second, self.exchange(second, 2)

    def cross_again(self, first, first_there, second, second_there):
        first = jnp.stack([first, first_there])
        second = jnp.stack([second, second_there])
        return [first, second, self.exchange(first, 2), self.exchange(second, 1)]

    def attend_all(self):
        return swap_all(self.cross_again(*self.attend_crossed))

    def cross_main(self):
        self.planes = self.lines(jnp.stack(self.plane))
        first, second = self.main[:2], self.main[2:]
        self.crossed = [
            self.exchange(first, 1), self.exchange(second, 1),
            self.exchange(first, 2), self.exchange(second, 2),
        ]

    def join(self, held, before):
        joined = lax.optimization_barrier((*before, *held))
        return joined[: len(before)], list(joined[len(before) :])

    def early_main(self, *before):
        before, joined = self.join([self.crossed[0], self.crossed[3]], before)
        self.crossed[0], self.crossed[3] = joined
        return before

    def more_main(self, *before):
        self.far_main = swap_cores(self.main)
        before, joined = self.join([self.crossed[1], self.crossed[2], self.far_main], before)
        self.crossed[1], self.crossed[2], self.far_main = joined
        first, second = after(self.crossed[0], before[0]), after(self.crossed[3], before[0])
        self.diagonal = [self.exchange(first, 2), self.exchange(second, 1)]
        return before

    def feed_all(self, *before):
        far = [swap_cores(self.crossed[0]), swap_cores(self.crossed[3])]
        before, joined = self.join([*far, *self.diagonal, self.planes], before)
        far, diagonal, planes = joined[:2], joined[2:4], joined[4:]
        main = [self.main, *self.crossed, *diagonal]
        other = [self.far_main, far[0], swap_cores(self.crossed[1]), swap_cores(self.crossed[2]), far[1]]
        return before, main + other + [swap_cores(array) for array in diagonal] + swap_all(planes)


class WholeGather:
    def begin(self, *matrices):
        self.all = [
            lax.all_gather(array, ("dp", "seq"), axis=0, tiled=True) for array in matrices
        ]
        return []

    def attend_all(self):
        return self.all[:1]

    def cross_last(self):
        return []

    def cross_main(self):
        pass

    def early_main(self, *before):
        return before

    def more_main(self, *before):
        return before

    def feed_all(self, *before):
        return before, self.all[1:]


def make_local(chips):
    devices = 2 * chips
    own = tuple(width // devices for width in WIDTHS)
    early, late = own[:4], own[4:]
    wide = D // devices

    def local(
        latents,
        condition,
        adapter_choice,
        cotangent,
        modulate_weight,
        attend_weight,
        project_weight,
        expand_weight,
        contract_weight,
        *tables,
    ):
        chip = lax.axis_index("dp")
        core = lax.axis_index("seq")
        place = jnp.stack([chip // 4, chip // 2 % 2, chip % 2, core]).astype(jnp.int32)
        core_at = place[3:]
        tokens = latents[0]

        def to_chips(values):
            return lax.all_to_all(values, "dp", split_axis=0, concat_axis=0, tiled=True)

        gather = PermutedGather() if chips == PermutedGather.chips else WholeGather()
        begun = gather.begin(attend_weight, project_weight, expand_weight, contract_weight)

        notes = to_chips(write_notes(chips, condition, adapter_choice))
        notes = after(notes, *gather.cross_last())
        choice = notes[:, 8, :5].astype(jnp.int32)
        row = 2 * wide * chip // 128
        lifted_all = lax.dynamic_index_in_dim(notes, row, 1, keepdims=False)
        lifted_all = jax.nn.silu(lifted_all.astype(f32)).astype(bf16)

        def columns_of(which):
            return jnp.concatenate(
                [
                    lax.dynamic_slice_in_dim(modulate_weight, which * D, D, 1),
                    lax.dynamic_slice_in_dim(modulate_weight, 2 * D + which * 2 * D, 2 * D, 1),
                ],
                axis=1,
            )

        def laid_out(own, tables):
            values = jnp.concatenate(
                [table.transpose(0, 2, 1) if which % 2 == 0 else table for which, table in enumerate(tables)],
                axis=2,
            )
            span = values.shape[2]
            return jnp.pad(values, ((0, 0), (0, 0), (0, rounded_up(span) - span)))

        at = jnp.stack([2 * wide * chip % 128, core])
        block = prepare(
            early,
            late,
            choice,
            at.astype(jnp.int32),
            lifted_all,
            columns_of(core),
            swap_cores(columns_of(1 - core)),
            jnp.concatenate([laid_out(early, tables[:4]), laid_out(late, tables[4:])], axis=2),
        )
        block = to_chips(after(block, *begun))
        *chosen, modulation, middle_modulate, lifted = open_block(
            early, late, core_at, condition, block, swap_cores(block)
        )
        modulate_down, modulate_up, attend_down, attend_up, *chosen_late = chosen

        attend_all = gather.attend_all()
        gather.cross_main()
        queries, near, entering, middle_attend = enter(
            place, tokens, modulation, attend_all, attend_down, attend_up
        )
        queries, near = gather.early_main(queries, near)
        far = swap_cores(near)
        attended, logsum_0 = attend(queries, near, far, 0, 2)
        logsum_0, far = gather.more_main(logsum_0, far)
        attended, logsum_1 = attend(queries, near, far, 2, 2, attended)
        (attended, logsum_1), feed_all = gather.feed_all(attended, logsum_1)
        modulate_all = lax.all_gather(
            after(modulate_weight, *feed_all), ("dp", "seq"), axis=0, tiled=True
        )
        block_output, grad_middle, grad_attended, sums_feed, *grads_late = feed(
            place, tokens, attended, cotangent[0], modulation, feed_all, chosen_late
        )
        grads_attended = [
            attend_back(queries, near, far, grad_attended, logsum, 2 * half)
            for half, logsum in enumerate((logsum_0, logsum_1))
        ]
        grad_queries, grad_near, grad_far = zip(*grads_attended)
        input_grad, sums_attend, *grads_attend = leave(
            place,
            grad_queries,
            grad_near,
            [swap_cores(grad) for grad in grad_far],
            attend_all,
            attend_down,
            attend_up,
            entering,
            middle_attend,
            tokens,
            modulation,
            grad_middle,
        )

        packed = pack_late(late, core_at, [after(grads_late[0], grad_far[1]), *grads_late[1:]])
        arrived_late = to_chips(packed[0] + swap_cores(packed[1]))
        packed, grad_modulation, grad_middle_modulate = pack_early(
            early,
            core_at,
            (sums_attend, swap_cores(sums_attend), sums_feed, swap_cores(sums_feed)),
            middle_modulate,
            lifted,
            modulate_up,
            grads_attend,
        )
        arrived_early = to_chips(packed[0] + swap_cores(packed[1]))
        grad_lifted = product_back(grad_modulation, modulate_all) + product(
            grad_middle_modulate, modulate_down
        )
        condition_grad = jax.vjp(jax.nn.silu, condition.astype(f32))[1](grad_lifted)[0]
        arrived_early, arrived_late, condition_grad = lax.optimization_barrier(
            (arrived_early, arrived_late, condition_grad)
        )
        owned_early = table_sums(early, (0, 1), choice, arrived_early)
        owned_late = table_sums(late, (2, 3, 4), choice, arrived_late)
        return (block_output[None], input_grad[None], condition_grad, *owned_early, *owned_late)

    return local


def solution(mesh):
    rows = P(("dp", "seq"), None)
    down = P(None, ("dp", "seq"), None)
    up = P(None, None, ("dp", "seq"))
    tokens = P("dp", "seq", None)
    return jax.shard_map(
        make_local(mesh.shape["dp"]),
        mesh=mesh,
        in_specs=(tokens, P("dp", None), P("dp", None), tokens) + (rows,) * 5 + (down, up) * 5,
        out_specs=(tokens, tokens, P("dp", None)) + (down, up) * 5,
        check_vma=False,
    )
```

```python
import jax
import jax.numpy as jnp
from jax import lax
from jax.experimental import pallas as pl
from jax.experimental.pallas import tpu as pltpu
from jax.sharding import PartitionSpec as P

D = 1024
HEADS = 16
HEAD_DIM = 64
FF = 4096
RANK = 16
bf16 = jnp.bfloat16
f32 = jnp.float32
EPSILON = 1e-06
TINY = pl.CostEstimate(flops=1, bytes_accessed=1, transcendentals=0)
LOG2E = 1.4426950408889634
GROUP = 256
TILE = 512
WIDE = D + 128
NADAPT = 8
CHUNK = 128
VMEM_LIMIT = 62 * 1024 * 1024
FIRST_ROWS = 32
SHIFT_ATTEND, SCALE_ATTEND, GATE_ATTEND, SHIFT_EXPAND, SCALE_EXPAND, GATE_EXPAND = range(6)


def product(left, right):
    return lax.dot_general(left, right, (((1,), (0,)), ((), ())), preferred_element_type=f32)


def product_back(grads, right):
    return lax.dot_general(grads, right, (((1,), (1,)), ((), ())), preferred_element_type=f32)


def product_rows(left, right):
    return lax.dot_general(left, right, (((0,), (0,)), ((), ())), preferred_element_type=f32)


def normalize(values):
    centred = values - jnp.mean(values, axis=-1, keepdims=True)
    variance = jnp.mean(centred * centred, axis=-1, keepdims=True)
    inverse = lax.rsqrt(variance + EPSILON)
    return centred * inverse, inverse


def normalize_back(grads, normed, inverse):
    mean = jnp.mean(grads, axis=-1, keepdims=True)
    along = jnp.mean(grads * normed, axis=-1, keepdims=True)
    return (grads - mean - normed * along) * inverse


def each_chunk(rows, step):
    def body(position, carry):
        step(pl.ds(pl.multiple_of(position * CHUNK, CHUNK), CHUNK))
        return carry

    lax.fori_loop(0, rows // CHUNK, body, 0)


def whole(shape):
    return pl.BlockSpec(shape, lambda *_: (0,) * len(shape))


def params():
    return pltpu.CompilerParams(vmem_limit_bytes=VMEM_LIMIT)


def piece_places(place, far, relative):
    chip_z, chip_y, chip_x, core = (place[axis] for axis in range(4))
    for dz in range(4):
        z = lax.rem(chip_z + 4 - dz, 4) if relative else dz
        for dy in range(2):
            for dx in range(2):
                chip = z * 4 + (chip_y ^ dy) * 2 + (chip_x ^ dx)
                yield dz, dy, dx, chip * 2 + (core ^ far)


def crossed(refs, half, dz, dy, dx):
    if half == 0:
        return refs[2 * dy].at[dx, dz % 2]
    return refs[1 + 2 * dx].at[dy, dz % 2]


def wait_for(target, semaphore):
    pltpu.make_async_copy(target, target, semaphore).wait()


def fetch_attend(place, refs, weight, semaphores):
    for part in range(3):
        columns = pl.ds(part * D, D)
        if len(refs) == 1:
            pltpu.make_async_copy(
                refs[0].at[:, columns], weight.at[pl.ds(0, D), columns], semaphores.at[part]
            ).start()
            continue
        for far in range(2):
            for dz, dy, dx, device in piece_places(place, far, True):
                rows = pl.ds(pl.multiple_of(device * 32, 32), 32)
                pltpu.make_async_copy(
                    crossed(refs[4 * far : 4 * far + 4], dz // 2, dz, dy, dx).at[:, columns],
                    weight.at[rows, columns],
                    semaphores.at[part],
                ).start()


def wait_attend(weight, semaphores, part):
    columns = pl.ds(pl.multiple_of(part * D, D), D)
    wait_for(weight.at[pl.ds(0, D), columns], semaphores.at[part])


def padded_rows(values):
    values = values.astype(f32)
    rest = jnp.zeros((WIDE - D - RANK, values.shape[1]), f32)
    return jnp.concatenate([values, rest])


def widen(target, middle):
    rest = jnp.zeros((middle.shape[0], WIDE - D - RANK), f32)
    target[:, D:] = jnp.concatenate([middle, rest], axis=1).astype(bf16)


def fetch_feed(place, refs, project, expand, contract, semaphores):
    if len(refs) == 3:
        pltpu.make_async_copy(refs[0], project, semaphores.at[0]).start()
        for part in range(4):
            pltpu.make_async_copy(
                refs[1].at[:, pl.ds(part * D, D)],
                expand.at[part, pl.ds(0, D)],
                semaphores.at[1 + part],
            ).start()
            pltpu.make_async_copy(
                refs[2].at[pl.ds(part * D, D)],
                contract.at[pl.ds(part * D, D), pl.ds(0, D)],
                semaphores.at[5 + part],
            ).start()
        return

    def rows_of(device, deep, first, count):
        return pl.ds(pl.multiple_of(device * deep + first, 16), count)

    def main_rows(first, count, far, dz, dy, dx):
        held = refs[7 * far : 7 * far + 7]
        block = (
            held[0].at[dz] if dy + dx == 0 else held[2 * (dx + 2 * dy) - 1 + dz // 2].at[dz % 2]
        )
        return block.at[pl.ds(first, count)]

    every = [
        (far, dz, dy, dx, device)
        for far in range(2)
        for dz, dy, dx, device in piece_places(place, far, False)
    ]
    for *at, device in every:
        pltpu.make_async_copy(
            main_rows(0, 32, *at), project.at[rows_of(device, 32, 0, 32)], semaphores.at[0]
        ).start()
    for part in range(4):
        for *at, device in every:
            pltpu.make_async_copy(
                main_rows(32 * (1 + part), 32, *at),
                expand.at[part, rows_of(device, 32, 0, 32)],
                semaphores.at[1 + part],
            ).start()
        for far, dz, dy, dx, device in every:
            if dz != part:
                continue
            columns = pl.ds(0, D)
            pltpu.make_async_copy(
                main_rows(160, FIRST_ROWS, far, dz, dy, dx),
                contract.at[rows_of(device, 128, 0, FIRST_ROWS), columns],
                semaphores.at[5 + part],
            ).start()
            pltpu.make_async_copy(
                refs[14].at[dz, place[3] ^ far, 2 * dy + dx],
                contract.at[rows_of(device, 128, FIRST_ROWS, 128 - FIRST_ROWS), columns],
                semaphores.at[5 + part],
            ).start()


def smem():
    return pl.BlockSpec(memory_space=pltpu.SMEM)


def anywhere(arrays):
    return [pl.BlockSpec(memory_space=pltpu.HBM)] * len(arrays)


def enter_kernel(count, place, latents, modulation, down, up, *refs):
    weights = refs[:count]
    queries, keys_values, entering, middle, wide, weight, semaphores = refs[count:]
    step_at = pl.program_id(0)

    @pl.when(step_at == 0)
    def _():
        fetch_attend(place, weights, weight, semaphores)

        def step(rows):
            normed, _ = normalize(latents[rows].astype(f32))
            values = normed * (1.0 + modulation[SCALE_ATTEND : SCALE_ATTEND + 1]) + modulation[
                SHIFT_ATTEND : SHIFT_ATTEND + 1
            ]
            values = values.astype(bf16)
            entering[rows] = values
            wide[rows, :D] = values

        each_chunk(latents.shape[0], step)
        weight[D:] = padded_rows(up[...]).astype(bf16)
        values = product_back(entering[...], down[...]).astype(bf16)
        middle[...] = values
        widen(wide, values.astype(f32))

    wait_attend(weight, semaphores, step_at)
    projected = product(wide[...], weight[:, pl.ds(pl.multiple_of(step_at * D, D), D)]).astype(bf16)

    @pl.when(step_at == 0)
    def _():
        queries[...] = projected

    @pl.when(step_at > 0)
    def _():
        keys_values[...] = projected


def enter(place, latents, modulation, weights, down, up):
    rows = latents.shape[0]
    columns = up.shape[1]
    return pl.pallas_call(
        lambda *refs: enter_kernel(len(weights), *refs),
        grid=(columns // D,),
        in_specs=[
            smem(),
            whole((rows, D)),
            whole(modulation.shape),
            whole(down.shape),
            whole(up.shape),
        ]
        + anywhere(weights),
        out_specs=[
            whole((rows, D)),
            pl.BlockSpec((rows, D), lambda j: (0, jnp.maximum(j - 1, 0))),
            whole((rows, D)),
            whole((rows, RANK)),
        ],
        out_shape=[
            jax.ShapeDtypeStruct((rows, D), bf16),
            jax.ShapeDtypeStruct((rows, columns - D), bf16),
            jax.ShapeDtypeStruct((rows, D), bf16),
            jax.ShapeDtypeStruct((rows, RANK), bf16),
        ],
        scratch_shapes=[
            pltpu.VMEM((rows, WIDE), bf16),
            pltpu.VMEM((WIDE, columns), bf16),
            pltpu.SemaphoreType.DMA((3,)),
        ],
        compiler_params=params(),
        cost_estimate=TINY,
        name="enter",
    )(place, latents, modulation, down, up, *weights)


def head_mask(head, dtype=jnp.bool_):
    lane = lax.broadcasted_iota(jnp.int32, (1, GROUP), 1)
    return jnp.logical_and(lane >= head * HEAD_DIM, lane < (head + 1) * HEAD_DIM)


def attend_kernel(queries, keys_near, values_near, keys_far, values_far, attended, logsum):
    rows = queries.shape[0]
    block = 256
    scale = HEAD_DIM ** (-0.5)
    lane = lax.broadcasted_iota(jnp.int32, (1, 128), 1)

    for start in range(0, rows, block):
        here = pl.ds(start, block)
        q = queries[here] * jnp.asarray(scale, bf16)
        total = jnp.zeros((block, GROUP), f32)
        sums = jnp.zeros((block, 128), f32)
        for head in range(GROUP // HEAD_DIM):
            mask = head_mask(head)
            mine = jnp.where(mask, q, jnp.zeros_like(q))
            near = product_back(mine, keys_near[...])
            far = product_back(mine, keys_far[...])
            highest = jnp.maximum(
                jnp.max(near, axis=1, keepdims=True), jnp.max(far, axis=1, keepdims=True)
            )
            near = jnp.exp2((near - highest) * LOG2E)
            far = jnp.exp2((far - highest) * LOG2E)
            denominator = jnp.sum(near, axis=1, keepdims=True) + jnp.sum(
                far, axis=1, keepdims=True
            )
            share = 1.0 / denominator
            out = product((near * share).astype(bf16), values_near[...]) + product(
                (far * share).astype(bf16), values_far[...]
            )
            total = jnp.where(mask, out, total)
            sums = jnp.where(lane == head, highest + jnp.log(denominator), sums)
        attended[here] = total.astype(bf16)
        logsum[0, here] = sums


def attend(queries, near, far, first, groups, earlier=None):
    rows = queries.shape[0]
    every = D // GROUP

    def at(start):
        return pl.BlockSpec((rows, GROUP), lambda g: (0, start + first + g))

    given = [] if earlier is None else [earlier]
    return pl.pallas_call(
        lambda *refs: attend_kernel(*refs[:5], *refs[5 + len(given) :]),
        grid=(groups,),
        in_specs=[at(0), at(0), at(every), at(0), at(every)] + anywhere(given),
        out_specs=[at(0), pl.BlockSpec((1, rows, 128), lambda g: (g, 0, 0))],
        out_shape=[
            jax.ShapeDtypeStruct((rows, D), bf16),
            jax.ShapeDtypeStruct((groups, rows, 128), f32),
        ],
        input_output_aliases={5: 0} if given else {},
        compiler_params=params(),
        cost_estimate=TINY,
        name="attend",
    )(queries, near, near, far, far, *given)


def attend_back_kernel(
    queries, keys_near, values_near, keys_far, values_far, grads, logsum,
    grad_queries, grad_near, grad_far, keys_sum, values_sum
):
    rows = queries.shape[0]
    block = 512
    scale = HEAD_DIM ** (-0.5)
    scaled = queries[...] * jnp.asarray(scale, bf16)
    scaled_t = scaled.T
    grads_t = grads[...].T
    for start in range(0, rows, block):
        here = slice(start, start + block)
        q = scaled[here]
        g = grads[here]
        total = jnp.zeros((block, GROUP), f32)
        for head in range(GROUP // HEAD_DIM):
            mask = head_mask(head)
            part = slice(head * HEAD_DIM, (head + 1) * HEAD_DIM)
            mine = jnp.where(mask, q, jnp.zeros_like(q))
            mine_g = jnp.where(mask, g, jnp.zeros_like(g))
            shift = logsum[0, here, head : head + 1]
            pn = jnp.exp2((product_back(mine, keys_near[...]) - shift) * LOG2E)
            pf = jnp.exp2((product_back(mine, keys_far[...]) - shift) * LOG2E)
            gn = product_back(mine_g, values_near[...])
            gf = product_back(mine_g, values_far[...])
            inner = jnp.sum(pn * gn, axis=1, keepdims=True) + jnp.sum(
                pf * gf, axis=1, keepdims=True
            )
            sn = (pn * (gn - inner)).astype(bf16)
            sf = (pf * (gf - inner)).astype(bf16)
            out = product(sn, keys_near[...]) + product(sf, keys_far[...])
            total = jnp.where(mask, out * scale, total)
            vn = product(grads_t[part, here], pn.astype(bf16))
            vf = product(grads_t[part, here], pf.astype(bf16))
            kn = product(scaled_t[part, here], sn)
            kf = product(scaled_t[part, here], sf)
            if start == 0:
                values_sum[part, :rows] = vn
                values_sum[part, rows:] = vf
                keys_sum[part, :rows] = kn
                keys_sum[part, rows:] = kf
            else:
                values_sum[part, :rows] += vn
                values_sum[part, rows:] += vf
                keys_sum[part, :rows] += kn
                keys_sum[part, rows:] += kf
        grad_queries[here] = total.astype(bf16)
    grad_near[0] = keys_sum[:, :rows].T
    grad_near[1] = values_sum[:, :rows].T
    grad_far[0] = keys_sum[:, rows:].T
    grad_far[1] = values_sum[:, rows:].T


def attend_back(queries, near, far, grads, logsum, first):
    rows = queries.shape[0]
    every = D // GROUP
    groups = logsum.shape[0]

    def at(start):
        return pl.BlockSpec((rows, GROUP), lambda g: (0, start + first + g))

    pair = pl.BlockSpec((2, rows, GROUP), lambda g: (0, 0, g))
    return pl.pallas_call(
        attend_back_kernel,
        grid=(groups,),
        in_specs=[at(0), at(0), at(every), at(0), at(every), at(0),
                  pl.BlockSpec((1, rows, 128), lambda g: (g, 0, 0))],
        out_specs=[pl.BlockSpec((rows, GROUP), lambda g: (0, g)), pair, pair],
        out_shape=[
            jax.ShapeDtypeStruct((rows, groups * GROUP), bf16),
            jax.ShapeDtypeStruct((2, rows, groups * GROUP), f32),
            jax.ShapeDtypeStruct((2, rows, groups * GROUP), f32),
        ],
        scratch_shapes=[pltpu.VMEM((GROUP, 2 * rows), f32), pltpu.VMEM((GROUP, 2 * rows), f32)],
        compiler_params=params(),
        cost_estimate=TINY,
        name="attend_back",
    )(queries, near, near, far, far, grads, logsum)


def gelu_both(values):
    root = 0.7978845608028654
    square = values * values
    inner = jnp.tanh(values * (root + (root * 0.044715) * square))
    half = 0.5 + 0.5 * inner
    slope = half + (0.5 * values) * (1.0 - inner * inner) * (root + (3.0 * root * 0.044715) * square)
    return values * half, slope


def feed_kernel(
    count, place, latents, attended, cotangent, modulation,
    project_down, project_up, expand_down, expand_up, contract_down, contract_up,
    *refs,
):
    weights = refs[:count]
    (
        block_output, grad_middle, grad_attended, sums,
        grad_project_down, grad_project_up, grad_expand_down, grad_expand_up,
        grad_contract_down, grad_contract_up,
        branch_attend, middle_tokens, entering, grad_branch, branch, grad_entering,
        middle_project, middle_expand, back_contract, grad_branch_attend, back_project,
        project, expand, contract, semaphores,
    ) = refs[count:]
    step_at = pl.program_id(0)
    rows_all = latents.shape[0]

    def row(which):
        return modulation[which : which + 1]

    @pl.when(step_at == 0)
    def _():
        fetch_feed(place, weights, project, expand, contract, semaphores)

        def first(rows):
            grad_branch[rows, :D] = (cotangent[rows].astype(f32) * row(GATE_EXPAND)).astype(bf16)
            branch[rows] = jnp.zeros((CHUNK, WIDE), f32)
            grad_entering[rows] = jnp.zeros((CHUNK, WIDE), f32)

        each_chunk(rows_all, first)
        middle = product_back(grad_branch[:, :D], contract_up[...]).astype(bf16)
        back_contract[...] = middle
        widen(grad_branch, middle.astype(f32))
        middle_project[...] = product_back(attended[...], project_down[...]).astype(bf16)
        wait_for(project, semaphores.at[0])
        branch_attend[...] = product(attended[...], project[...]) + product(
            middle_project[...], project_up[...]
        )

        def step(rows):
            tokens = latents[rows].astype(f32) + row(GATE_ATTEND) * branch_attend[rows]
            middle_tokens[rows] = tokens
            normed, _ = normalize(tokens)
            values = normed * (1.0 + row(SCALE_EXPAND)) + row(SHIFT_EXPAND)
            entering[rows, :D] = values.astype(bf16)

        each_chunk(rows_all, step)
        middle = product_back(entering[:, :D], expand_down[...]).astype(bf16)
        middle_expand[...] = middle
        widen(entering, middle.astype(f32))

    here = pl.ds(pl.multiple_of(step_at * D, D), D)
    expand[step_at, D:] = padded_rows(expand_up[...]).astype(bf16)
    contract[here, D:] = padded_rows(contract_down[...]).T.astype(bf16)
    wait_for(expand.at[step_at, pl.ds(0, D)], semaphores.at[1 + step_at])
    wait_for(contract.at[here, pl.ds(0, D)], semaphores.at[5 + step_at])
    wide = expand[step_at]
    deep = contract[here]
    grads = product_back(grad_branch[...], deep)
    hidden = product(entering[...], wide)
    activated, slope = gelu_both(hidden)
    activated = activated.astype(bf16)
    grads = (grads * slope).astype(bf16)
    branch[...] += product(activated, deep)
    grad_entering[...] += product_back(grads, wide)
    grad_contract_down[...] = product_rows(back_contract[...], activated)
    grad_expand_up[...] = product_rows(middle_expand[...], grads)

    @pl.when(step_at == pl.num_programs(0) - 1)
    def _():
        sums[...] = jnp.zeros_like(sums)
        last_middle = branch[:, D : D + RANK].astype(bf16)
        last_back = grad_entering[:, D : D + RANK].astype(bf16)
        grad_contract_up[...] = product_rows(last_middle, grad_branch[:, :D])
        grad_expand_down[...] = product_rows(last_back, entering[:, :D])
        branch[:, :D] += product(last_middle, contract_up[...])
        grad_entering[:, :D] += product(last_back, expand_down[...])

        def add(which, values):
            sums[which : which + 1] += jnp.sum(values, axis=0, keepdims=True)

        def step(rows):
            out = branch[rows, :D]
            tokens = middle_tokens[rows]
            block_output[rows] = (tokens + row(GATE_EXPAND) * out).astype(bf16)
            cotangents = cotangent[rows].astype(f32)
            add(GATE_EXPAND, cotangents * out)
            grad = grad_entering[rows, :D]
            normed, inverse = normalize(tokens)
            add(SHIFT_EXPAND, grad)
            add(SCALE_EXPAND, grad * normed)
            grad = cotangents + normalize_back(grad * (1.0 + row(SCALE_EXPAND)), normed, inverse)
            grad_middle[rows] = grad
            add(GATE_ATTEND, grad * branch_attend[rows])
            grad_branch_attend[rows] = (grad * row(GATE_ATTEND)).astype(bf16)

        each_chunk(rows_all, step)
        back_project[...] = product_back(grad_branch_attend[...], project_up[...]).astype(bf16)
        grad_attended[...] = (
            product_back(grad_branch_attend[...], project[...])
            + product(back_project[...], project_down[...])
        ).astype(bf16)
        grad_project_up[...] = product_rows(middle_project[...], grad_branch_attend[...])
        grad_project_down[...] = product_rows(back_project[...], attended[...])


def feed(place, latents, attended, cotangent, modulation, weights, chosen):
    rows = latents.shape[0]
    project_down, project_up, expand_down, expand_up, contract_down, contract_up = chosen
    tile = pl.BlockSpec((RANK, D), lambda j: (0, j))
    narrow = whole((RANK, D))

    def buffer(columns, dtype):
        return pltpu.VMEM((rows, columns), dtype)

    return pl.pallas_call(
        lambda *refs: feed_kernel(len(weights), *refs),
        grid=(FF // D,),
        in_specs=[
            smem(),
            whole((rows, D)),
            whole((rows, D)),
            whole((rows, D)),
            whole(modulation.shape),
            narrow,
            narrow,
            narrow,
            tile,
            tile,
            narrow,
        ]
        + anywhere(weights),
        out_specs=[
            whole((rows, D)),
            whole((rows, D)),
            whole((rows, D)),
            whole((8, D)),
            narrow,
            narrow,
            narrow,
            tile,
            tile,
            narrow,
        ],
        out_shape=[
            jax.ShapeDtypeStruct((rows, D), bf16),
            jax.ShapeDtypeStruct((rows, D), f32),
            jax.ShapeDtypeStruct((rows, D), bf16),
            jax.ShapeDtypeStruct((8, D), f32),
            jax.ShapeDtypeStruct((RANK, D), f32),
            jax.ShapeDtypeStruct((RANK, D), f32),
            jax.ShapeDtypeStruct((RANK, D), f32),
            jax.ShapeDtypeStruct((RANK, FF), f32),
            jax.ShapeDtypeStruct((RANK, FF), f32),
            jax.ShapeDtypeStruct((RANK, D), f32),
        ],
        scratch_shapes=[
            buffer(D, f32),
            buffer(D, f32),
            buffer(WIDE, bf16),
            buffer(WIDE, bf16),
            buffer(WIDE, f32),
            buffer(WIDE, f32),
            buffer(RANK, bf16),
            buffer(RANK, bf16),
            buffer(RANK, bf16),
            buffer(D, bf16),
            buffer(RANK, bf16),
            pltpu.VMEM((D, D), bf16),
            pltpu.VMEM((4, WIDE, D), bf16),
            pltpu.VMEM((FF, WIDE), bf16),
            pltpu.SemaphoreType.DMA((9,)),
        ],
        compiler_params=params(),
        cost_estimate=TINY,
        name="feed",
    )(place, latents, attended, cotangent, modulation,
      project_down, project_up, expand_down, expand_up, contract_down, contract_up, *weights)


def leave_kernel(
    count, place, queries_0, queries_1, own_0, own_1, other_0, other_1, down, up, middle,
    modulation, *refs,
):
    weights = refs[:count]
    (
        entering_there, latents_there, grad_middle_there, input_grad, sums, grad_down, grad_up,
        total, weight, entering, latents, grad_middle, semaphores, semaphore,
    ) = refs[count:]
    step_at = pl.program_id(0)
    rows_all = latents.shape[0]
    copies = [
        pltpu.make_async_copy(source, target, semaphore.at[which])
        for which, (source, target) in enumerate(
            ((entering_there, entering), (latents_there, latents), (grad_middle_there, grad_middle))
        )
    ]

    def through(first, second):
        grads = jnp.concatenate([first, second], axis=1)
        grad_up[...] = product_rows(middle[...], grads)
        return product_back(grads, weight[:, pl.ds(pl.multiple_of(step_at * D, D), D)])

    @pl.when(step_at == 0)
    def _():
        fetch_attend(place, weights, weight, semaphores)
        for copy in copies:
            copy.start()
        weight[D:] = padded_rows(up[...]).astype(bf16)
        wait_attend(weight, semaphores, 0)
        total[...] = through(queries_0[...], queries_1[...])

    @pl.when(step_at > 0)
    def _():
        wait_attend(weight, semaphores, step_at)
        total[...] += through(
            (own_0[0] + other_0[0]).astype(bf16), (own_1[0] + other_1[0]).astype(bf16)
        )

    @pl.when(step_at == pl.num_programs(0) - 1)
    def _():
        for copy in copies:
            copy.wait()
        sums[...] = jnp.zeros_like(sums)
        last = total[:, D : D + RANK].astype(bf16)
        grad_down[...] = product_rows(last, entering[...])
        total[:, :D] += product(last, down[...])

        def step(rows):
            grad = total[rows, :D]
            normed, inverse = normalize(latents[rows].astype(f32))
            sums[0:1] += jnp.sum(grad, axis=0, keepdims=True)
            sums[1:2] += jnp.sum(grad * normed, axis=0, keepdims=True)
            grad = grad * (1.0 + modulation[SCALE_ATTEND : SCALE_ATTEND + 1])
            input_grad[rows] = grad_middle[rows] + normalize_back(grad, normed, inverse)

        each_chunk(rows_all, step)


def leave(place, queries, own, other, weights, down, up, entering, middle, latents, modulation,
          grad_middle):
    rows = latents.shape[0]
    columns = up.shape[1]
    tile = pl.BlockSpec((RANK, D), lambda j: (0, j))
    pair = pl.BlockSpec((1, rows, TILE), lambda j: (j // 2, 0, 0))
    return pl.pallas_call(
        lambda *refs: leave_kernel(len(weights), *refs),
        grid=(columns // D,),
        in_specs=[smem()]
        + [whole((rows, TILE))] * 2
        + [pair] * 4
        + [whole(down.shape), whole(up.shape), whole((rows, RANK)), whole(modulation.shape)]
        + anywhere(weights)
        + anywhere(range(3)),
        out_specs=[whole((rows, D)), whole((8, D)), whole((RANK, D)), tile],
        out_shape=[
            jax.ShapeDtypeStruct((rows, D), f32),
            jax.ShapeDtypeStruct((8, D), f32),
            jax.ShapeDtypeStruct((RANK, D), f32),
            jax.ShapeDtypeStruct((RANK, columns), f32),
        ],
        scratch_shapes=[
            pltpu.VMEM((rows, WIDE), f32),
            pltpu.VMEM((WIDE, columns), bf16),
            pltpu.VMEM((rows, D), bf16),
            pltpu.VMEM((rows, D), bf16),
            pltpu.VMEM((rows, D), f32),
            pltpu.SemaphoreType.DMA((3,)),
            pltpu.SemaphoreType.DMA((3,)),
        ],
        compiler_params=params(),
        cost_estimate=TINY,
        name="leave",
    )(place, *queries, *own, *other, down, up, middle, modulation, *weights, entering, latents,
      grad_middle)


PARTS_OF_HALVES = (
    (SHIFT_ATTEND, GATE_ATTEND, SHIFT_EXPAND),
    (SCALE_ATTEND, SCALE_EXPAND, GATE_EXPAND),
)
WIDTHS = (D, 6 * D, D, 3 * D, D, D, D, FF, FF, D)


def swap_cores(values):
    return lax.ppermute(values, "seq", [(0, 1), (1, 0)])


def vmem(count):
    return [pl.BlockSpec(memory_space=pltpu.VMEM)] * count


def rounded_up(span):
    return -(-span // 128) * 128


def note_kernel(condition, choice, out):
    values = condition[...].astype(f32)
    lanes = lax.broadcasted_iota(jnp.int32, (1, 128), 1)
    last = jnp.zeros((1, 128), f32)
    for member in range(5):
        last = jnp.where(lanes == member, choice[0, member].astype(f32), last)
    rows = [values[:, 128 * at : 128 * (at + 1)] for at in range(D // 128)]
    note = jnp.concatenate(rows + [last] + [jnp.zeros((7, 128), f32)], axis=0).astype(bf16)
    for chip in range(out.shape[0]):
        out[chip] = note


def write_notes(chips, condition, choice):
    return pl.pallas_call(
        note_kernel,
        in_specs=vmem(1) + [smem()],
        out_specs=vmem(1)[0],
        out_shape=jax.ShapeDtypeStruct((chips, 16, 128), bf16),
        cost_estimate=TINY,
        name="write_notes",
    )(condition, choice)


def prepare_kernel(early, late, choice, at, lifted, mine, other, tables, out, weight, parts):
    weight[...] = jnp.zeros_like(weight)
    rows = 2 * mine.shape[0]
    m = mine[...].astype(f32)
    o = other[...].astype(f32)
    both = jnp.where(at[1] == 0, jnp.concatenate([m, o]), jnp.concatenate([o, m]))
    weight[pl.ds(pl.multiple_of(at[0], rows), rows)] = both.astype(bf16)
    partial = product(lifted[...], weight[...])
    high = partial.astype(bf16).astype(f32)
    span = parts.shape[2]
    for row in range(8):
        part = slice(row * span, (row + 1) * span)
        parts[:, row] = high[:, part]
        parts[:, 8 + row] = partial[:, part] - high[:, part]
    size = tables.shape[2]
    lanes = lax.broadcasted_iota(jnp.int32, (RANK, size), 1)
    starts = [0, early[0] + early[1], rounded_up(sum(early))]
    starts += [starts[2] + late[0] + late[1], starts[2] + sum(late[:4])]
    for latent in range(out.shape[0]):
        picked = tables[choice[latent, 0]]
        for member in range(1, 5):
            picked = jnp.where(lanes >= starts[member], tables[choice[latent, member]], picked)
        out[latent, :, :size] = picked
        out[latent, :, size:] = parts[latent].astype(bf16)


def prepare(early, late, choice, at, lifted, mine, other, tables):
    chips = choice.shape[0]
    size = tables.shape[2]
    span = mine.shape[1] // 8
    return pl.pallas_call(
        lambda *refs: prepare_kernel(early, late, *refs),
        in_specs=[smem()] * 2 + vmem(4),
        out_specs=vmem(1)[0],
        out_shape=jax.ShapeDtypeStruct((chips, RANK, size + span), bf16),
        scratch_shapes=[
            pltpu.VMEM((128, mine.shape[1]), bf16),
            pltpu.VMEM((chips, 16, span), f32),
        ],
        cost_estimate=TINY,
        name="prepare",
    )(choice, at, lifted, mine, other, tables)


def put_together(own, blocks, first, outs):
    for width, out in zip(own, outs):
        for start in range(0, out.shape[1], 128):
            pieces = []
            for device in range(start // width, (start + 127) // width + 1):
                low = max(start - device * width, 0)
                high = min(start + 128 - device * width, width)
                pieces.append(blocks[device][:, first + low : first + high])
            out[:, start : start + 128] = joined(pieces).astype(bf16)
        first += width


def open_kernel(early, late, core, condition, near, far, *outs):
    tables, (modulation, middle, lifted) = outs[:10], outs[10:]
    size = rounded_up(sum(early)) + rounded_up(sum(late))
    on_first = core[0] == 0
    blocks = []
    near_sum = jnp.zeros((16, near.shape[2] - size), f32)
    far_sum = near_sum
    for chip in range(near.shape[0]):
        n = near[chip].astype(f32)
        f = far[chip].astype(f32)
        near_sum += n[:, size:]
        far_sum += f[:, size:]
        n, f = n[:, :size], f[:, :size]
        blocks += [jnp.where(on_first, n, f), jnp.where(on_first, f, n)]
    put_together(early, blocks, 0, tables[:4])
    put_together(late, blocks, rounded_up(sum(early)), tables[4:])
    near_sum = near_sum[:8] + near_sum[8:]
    far_sum = far_sum[:8] + far_sum[8:]
    values = condition[...].astype(f32)
    lifted[...] = (values * (1.0 / (1.0 + jnp.exp(-values)))).astype(bf16)
    middle[...] = product_back(lifted[...], tables[0][...]).astype(bf16)
    adapted = product(middle[...], tables[1][...])
    halves = (jnp.where(on_first, near_sum, far_sum), jnp.where(on_first, far_sum, near_sum))
    modulation[...] = jnp.zeros_like(modulation)
    for half, targets in zip(halves, PARTS_OF_HALVES):
        for place in range(3 * D // 128):
            row, lane = targets[place // 8], place % 8 * 128
            modulation[row : row + 1, lane : lane + 128] = (
                half[place // 3 : place // 3 + 1, place % 3 * 128 : (place % 3 + 1) * 128]
                + adapted[:, row * D + lane : row * D + lane + 128]
            )


def open_block(early, late, core, condition, near, far):
    chips = near.shape[0]
    shapes = [((RANK, 2 * chips * width), bf16) for width in early + late]
    shapes += [((8, D), f32), ((1, RANK), bf16), ((1, D), bf16)]
    return pl.pallas_call(
        lambda *refs: open_kernel(early, late, *refs),
        in_specs=[smem()] + vmem(3),
        out_specs=vmem(len(shapes)),
        out_shape=[jax.ShapeDtypeStruct(*shape) for shape in shapes],
        compiler_params=params(),
        cost_estimate=TINY,
        name="open_block",
    )(core, condition, near, far)


def joined(pieces):
    return pieces[0] if len(pieces) == 1 else jnp.concatenate(pieces, axis=1)

def pack_into(own, core, grads, near, far):
    chips, span = near.shape[0], near.shape[2]
    on_first = core[0] == 0
    for chip in range(chips):
        parts = []
        for device in (2 * chip, 2 * chip + 1):
            pieces = [grad[:, device * width : (device + 1) * width] for width, grad in zip(own, grads)]
            if span > sum(own):
                pieces.append(jnp.zeros((RANK, span - sum(own)), f32))
            parts.append(joined(pieces))
        near[chip] = jnp.where(on_first, parts[0], parts[1])
        far[chip] = jnp.where(on_first, parts[1], parts[0])


def packed_shapes(own, chips):
    return [jax.ShapeDtypeStruct((chips, RANK, rounded_up(sum(own))), f32)] * 2


def pack_late(own, core, grads):
    return pl.pallas_call(
        lambda core, *refs: pack_into(own, core, refs[:-2], *refs[-2:]),
        out_shape=packed_shapes(own, grads[0].shape[1] // own[0] // 2),
        in_specs=[smem()] + vmem(len(grads)),
        out_specs=vmem(2),
        cost_estimate=TINY,
        name="pack_late",
    )(core, *grads)


def pack_early_kernel(
    own, core, attend, attend_there, feed, feed_there, middle, lifted, up, down_grad, up_grad,
    near, far, grad_modulation, grad_middle, modulate_down, modulate_up
):
    early = attend[...] + attend_there[...]
    late = feed[...] + feed_there[...]
    rows = [early[row : row + 1] if row < 2 else late[row : row + 1] for row in range(6)]
    grads = jnp.concatenate(rows, axis=1).astype(bf16)
    grad_modulation[...] = grads
    back = product_back(grads, up[...]).astype(bf16)
    grad_middle[...] = back
    keep = jnp.where(core[0] == 0, 1.0, 0.0)
    modulate_down[...] = product_rows(back, lifted[...]) * keep
    modulate_up[...] = product_rows(middle[...], grads) * keep
    pack_into(own, core, (modulate_down, modulate_up, down_grad, up_grad), near, far)


def pack_early(own, core, sums, middle, lifted, up, grads):
    return pl.pallas_call(
        lambda *refs: pack_early_kernel(own, *refs),
        out_shape=packed_shapes(own, grads[0].shape[1] // own[2] // 2)
        + [jax.ShapeDtypeStruct((1, 6 * D), bf16), jax.ShapeDtypeStruct((1, RANK), bf16)],
        in_specs=[smem()] + vmem(9),
        out_specs=vmem(4),
        scratch_shapes=[pltpu.VMEM((RANK, D), f32), pltpu.VMEM((RANK, 6 * D), f32)],
        cost_estimate=TINY,
        name="pack_early",
    )(core, *sums, middle, lifted, up, *grads)


def sums_kernel(own, members, choice, grads, *refs):
    outs, total = refs[:-1], refs[-1]
    lanes = lax.broadcasted_iota(jnp.int32, grads.shape[1:], 1)
    total[...] = jnp.zeros_like(total)
    for latent in range(grads.shape[0]):
        offset = 0
        for pair, member in enumerate(members):
            width = own[2 * pair] + own[2 * pair + 1]
            inside = jnp.logical_and(lanes >= offset, lanes < offset + width)
            total[choice[latent, member]] += jnp.where(inside, grads[latent], 0.0)
            offset += width
    for entry in range(NADAPT):
        values = total[entry]
        offset = 0
        for width, out in zip(own, outs):
            out[entry] = values[:, offset : offset + width]
            offset += width

def table_sums(own, members, choice, grads):
    sums = pl.pallas_call(
        lambda *refs: sums_kernel(own, members, *refs),
        out_shape=[jax.ShapeDtypeStruct((NADAPT, RANK, width), f32) for width in own],
        in_specs=[smem()] + vmem(1),
        out_specs=vmem(len(own)),
        scratch_shapes=[pltpu.VMEM((NADAPT,) + grads.shape[1:], f32)],
        cost_estimate=TINY,
        name="table_sums")(choice, grads)
    return [array.transpose(0, 2, 1) if which % 2 == 0 else array for which, array in enumerate(sums)]


def swap_all(arrays):
    return list(arrays) + [swap_cores(array) for array in arrays]


def after(values, *others):
    return lax.optimization_barrier((values, *others))[0]


def cut_kernel(project, expand, contract, main, last):
    deep = project.shape[0]
    main[:deep] = project[...]
    for part in range(4):
        main[(1 + part) * deep : (2 + part) * deep] = expand[:, part * D : (part + 1) * D]
    main[5 * deep :] = contract[: FIRST_ROWS]
    last[...] = contract[FIRST_ROWS:]


def cut_weights(project_weight, expand_weight, contract_weight):
    rows = contract_weight.shape[0] - FIRST_ROWS
    return pl.pallas_call(
        cut_kernel,
        in_specs=vmem(3),
        out_specs=vmem(2),
        out_shape=[
            jax.ShapeDtypeStruct((5 * project_weight.shape[0] + FIRST_ROWS, D), bf16),
            jax.ShapeDtypeStruct((rows, D), bf16),
        ],
        cost_estimate=TINY,
        name="cut_weights",
    )(project_weight, expand_weight, contract_weight)


class PermutedGather:
    chips = 16

    def exchange(self, values, over):
        return lax.ppermute(values, "dp", [(chip, chip ^ over) for chip in range(self.chips)])

    def along(self, values, step=1):
        return lax.ppermute(
            values, "dp", [(chip, (chip + 4 * step) % self.chips) for chip in range(self.chips)]
        )

    def begin(self, attend_weight, project_weight, expand_weight, contract_weight):
        main, last = cut_weights(project_weight, expand_weight, contract_weight)
        self.attend = [attend_weight] + [self.along(attend_weight, step) for step in (1, 2, 3)]
        self.main = self.lines(main)
        self.last = last
        self.attend_crossed = self.cross(jnp.stack(self.attend[:2]), jnp.stack(self.attend[2:]))
        return [self.attend_crossed[1], self.attend_crossed[3]]

    def cross_last(self):
        self.plane = [self.last, self.exchange(self.last, 1)]
        return self.plane[1:]

    def cross_last_y(self):
        self.plane.append(self.exchange(self.last, 2))
        return self.plane[2:]

    def cross_last_again(self, *before):
        self.plane.append(self.exchange(after(self.plane[1], *before), 2))
        return self.plane[3:]

    def lines(self, values):
        groups = [[z * 4 + line for z in range(self.chips // 4)] for line in range(4)]
        return lax.all_gather(values, "dp", axis=0, tiled=False, axis_index_groups=groups)

    def cross(self, first, second):
        return first, self.exchange(first, 1), second, self.exchange(second, 2)

    def cross_again(self, first, first_there, second, second_there):
        first = jnp.stack([first, first_there])
        second = jnp.stack([second, second_there])
        return [first, second, self.exchange(first, 2), self.exchange(second, 1)]

    def attend_all(self):
        return swap_all(self.cross_again(*self.attend_crossed))

    def cross_main(self):
        planes = lax.all_gather(
            jnp.stack(self.plane),
            ("dp", "seq"),
            axis=0,
            tiled=False,
            axis_index_groups=[
                [2 * (z * 4 + line) + core for z in range(self.chips // 4) for core in range(2)]
                for line in range(4)
            ],
        )
        self.planes = planes.reshape(self.chips // 4, 2, *planes.shape[1:])
        first, second = self.main[:2], self.main[2:]
        self.crossed = [
            self.exchange(first, 1), self.exchange(second, 1),
            self.exchange(first, 2), self.exchange(second, 2),
        ]

    def join(self, held, before):
        joined = lax.optimization_barrier((*before, *held))
        return joined[: len(before)], list(joined[len(before) :])

    def early_main(self, *before):
        before, joined = self.join([self.crossed[0], self.crossed[3]], before)
        self.crossed[0], self.crossed[3] = joined
        return before

    def more_main(self, *before):
        far = [swap_cores(self.main), swap_cores(self.crossed[0])]
        before, joined = self.join([self.crossed[1], self.crossed[2], *far], before)
        self.crossed[1:3], self.far = joined[:2], joined[2:]
        first, second = after(self.crossed[0], before[0]), after(self.crossed[3], before[0])
        self.diagonal = [self.exchange(first, 2), self.exchange(second, 1)]
        return before

    def feed_all(self, *before):
        far = [swap_cores(array) for array in self.crossed[1:]]
        before, joined = self.join([*self.diagonal, *far, self.planes], before)
        diagonal, far, planes = joined[:2], joined[2:-1], joined[-1]
        main = [self.main, *self.crossed, *diagonal]
        other = [*self.far, *far, *(swap_cores(array) for array in diagonal)]
        return before, main + other + [planes]


class WholeGather:
    def begin(self, *matrices):
        self.all = [
            lax.all_gather(array, ("dp", "seq"), axis=0, tiled=True) for array in matrices
        ]
        return []

    def attend_all(self):
        return self.all[:1]

    def cross_last(self):
        return []

    def cross_last_y(self):
        return []

    def cross_last_again(self, *before):
        return []

    def cross_main(self):
        pass

    def early_main(self, *before):
        return before

    def more_main(self, *before):
        return before

    def feed_all(self, *before):
        return before, self.all[1:]


def make_local(chips):
    devices = 2 * chips
    own = tuple(width // devices for width in WIDTHS)
    early, late = own[:4], own[4:]
    wide = D // devices

    def local(
        latents,
        condition,
        adapter_choice,
        cotangent,
        modulate_weight,
        attend_weight,
        project_weight,
        expand_weight,
        contract_weight,
        *tables,
    ):
        chip = lax.axis_index("dp")
        core = lax.axis_index("seq")
        place = jnp.stack([chip // 4, chip // 2 % 2, chip % 2, core]).astype(jnp.int32)
        core_at = place[3:]
        tokens = latents[0]

        def to_chips(values):
            return lax.all_to_all(values, "dp", split_axis=0, concat_axis=0, tiled=True)

        gather = PermutedGather() if chips == PermutedGather.chips else WholeGather()
        begun = gather.begin(attend_weight, project_weight, expand_weight, contract_weight)

        notes = to_chips(write_notes(chips, condition, adapter_choice))
        notes = after(notes, *gather.cross_last())
        choice = notes[:, 8, :5].astype(jnp.int32)
        row = 2 * wide * chip // 128
        lifted_all = lax.dynamic_index_in_dim(notes, row, 1, keepdims=False)
        lifted_all = jax.nn.silu(lifted_all.astype(f32)).astype(bf16)

        def columns_of(which):
            return jnp.concatenate(
                [
                    lax.dynamic_slice_in_dim(modulate_weight, which * D, D, 1),
                    lax.dynamic_slice_in_dim(modulate_weight, 2 * D + which * 2 * D, 2 * D, 1),
                ],
                axis=1,
            )

        def laid_out(own, tables):
            values = jnp.concatenate(
                [table.transpose(0, 2, 1) if which % 2 == 0 else table for which, table in enumerate(tables)],
                axis=2,
            )
            span = values.shape[2]
            return jnp.pad(values, ((0, 0), (0, 0), (0, rounded_up(span) - span)))

        at = jnp.stack([2 * wide * chip % 128, core])
        block = prepare(
            early,
            late,
            choice,
            at.astype(jnp.int32),
            lifted_all,
            columns_of(core),
            swap_cores(columns_of(1 - core)),
            jnp.concatenate([laid_out(early, tables[:4]), laid_out(late, tables[4:])], axis=2),
        )
        block = after(block, *begun, *gather.cross_last_y())
        block = after(to_chips(block), *gather.cross_last_again(block))
        *chosen, modulation, middle_modulate, lifted = open_block(
            early, late, core_at, condition, block, swap_cores(block)
        )
        modulate_down, modulate_up, attend_down, attend_up, *chosen_late = chosen

        attend_all = gather.attend_all()
        gather.cross_main()
        queries, near, entering, middle_attend = enter(
            place, tokens, modulation, attend_all, attend_down, attend_up
        )
        queries, near = gather.early_main(queries, near)
        far = swap_cores(near)
        attended, logsum_0 = attend(queries, near, far, 0, 2)
        logsum_0, far = gather.more_main(logsum_0, far)
        attended, logsum_1 = attend(queries, near, far, 2, 2, attended)
        (attended, logsum_1), feed_all = gather.feed_all(attended, logsum_1)
        modulate_all = lax.all_gather(
            after(modulate_weight, *feed_all), ("dp", "seq"), axis=0, tiled=True
        )
        block_output, grad_middle, grad_attended, sums_feed, *grads_late = feed(
            place, tokens, attended, cotangent[0], modulation, feed_all, chosen_late
        )
        packed, packed_far = pack_late(late, core_at, grads_late)
        half_0 = attend_back(queries, near, far, grad_attended, logsum_0, 0)
        packed_far = swap_cores(packed_far)
        grad_attended, packed_far = lax.optimization_barrier((grad_attended, packed_far))
        arrived_late = to_chips(packed + packed_far)
        half_1 = attend_back(queries, near, far, grad_attended, logsum_1, 2)
        grads_attended = [half_0, half_1]
        grad_queries, grad_near, grad_far = zip(*grads_attended)
        input_grad, sums_attend, *grads_attend = leave(
            place,
            grad_queries,
            grad_near,
            [swap_cores(grad) for grad in grad_far],
            attend_all,
            attend_down,
            attend_up,
            entering,
            middle_attend,
            tokens,
            modulation,
            grad_middle,
        )

        sums_attend, arrived_late = lax.optimization_barrier((sums_attend, arrived_late))
        packed, packed_far, grad_modulation, grad_middle_modulate = pack_early(
            early,
            core_at,
            (sums_attend, swap_cores(sums_attend), sums_feed, swap_cores(sums_feed)),
            middle_modulate,
            lifted,
            modulate_up,
            grads_attend,
        )
        arrived_early = to_chips(packed + swap_cores(packed_far))
        grad_lifted = product_back(grad_modulation, modulate_all) + product(
            grad_middle_modulate, modulate_down
        )
        condition_grad = jax.vjp(jax.nn.silu, condition.astype(f32))[1](grad_lifted)[0]
        arrived_late = after(arrived_late, condition_grad)
        owned_late = table_sums(late, (2, 3, 4), choice, arrived_late)
        arrived_early, *owned_late = lax.optimization_barrier((arrived_early, *owned_late))
        owned_early = table_sums(early, (0, 1), choice, arrived_early)
        return (block_output[None], input_grad[None], condition_grad, *owned_early, *owned_late)

    return local


def solution(mesh):
    rows = P(("dp", "seq"), None)
    down = P(None, ("dp", "seq"), None)
    up = P(None, None, ("dp", "seq"))
    tokens = P("dp", "seq", None)
    return jax.shard_map(
        make_local(mesh.shape["dp"]),
        mesh=mesh,
        in_specs=(tokens, P("dp", None), P("dp", None), tokens) + (rows,) * 5 + (down, up) * 5,
        out_specs=(tokens, tokens, P("dp", None)) + (down, up) * 5,
        check_vma=False,
    )
```

```python
import jax
import jax.numpy as jnp
from jax import lax
from jax.experimental import pallas as pl
from jax.experimental.pallas import tpu as pltpu
from jax.sharding import PartitionSpec as P

D = 1024
HEADS = 16
HEAD_DIM = 64
FF = 4096
RANK = 16
bf16 = jnp.bfloat16
f32 = jnp.float32
EPSILON = 1e-06
TINY = pl.CostEstimate(flops=1, bytes_accessed=1, transcendentals=0)
LOG2E = 1.4426950408889634
GROUP = 256
TILE = 512
WIDE = D + 128
NADAPT = 8
CHUNK = 128
VMEM_LIMIT = 62 * 1024 * 1024
FIRST_ROWS = 32
SHIFT_ATTEND, SCALE_ATTEND, GATE_ATTEND, SHIFT_EXPAND, SCALE_EXPAND, GATE_EXPAND = range(6)


def product(left, right):
    return lax.dot_general(left, right, (((1,), (0,)), ((), ())), preferred_element_type=f32)


def product_back(grads, right):
    return lax.dot_general(grads, right, (((1,), (1,)), ((), ())), preferred_element_type=f32)


def product_rows(left, right):
    return lax.dot_general(left, right, (((0,), (0,)), ((), ())), preferred_element_type=f32)


def normalize(values):
    centred = values - jnp.mean(values, axis=-1, keepdims=True)
    variance = jnp.mean(centred * centred, axis=-1, keepdims=True)
    inverse = lax.rsqrt(variance + EPSILON)
    return centred * inverse, inverse


def normalize_back(grads, normed, inverse):
    mean = jnp.mean(grads, axis=-1, keepdims=True)
    along = jnp.mean(grads * normed, axis=-1, keepdims=True)
    return (grads - mean - normed * along) * inverse


def each_chunk(rows, step):
    def body(position, carry):
        step(pl.ds(pl.multiple_of(position * CHUNK, CHUNK), CHUNK))
        return carry

    lax.fori_loop(0, rows // CHUNK, body, 0)


def whole(shape):
    return pl.BlockSpec(shape, lambda *_: (0,) * len(shape))


def params():
    return pltpu.CompilerParams(vmem_limit_bytes=VMEM_LIMIT)


def piece_places(place, far, relative):
    chip_z, chip_y, chip_x, core = (place[axis] for axis in range(4))
    for dz in range(4):
        z = lax.rem(chip_z + 4 - dz, 4) if relative else dz
        for dy in range(2):
            for dx in range(2):
                chip = z * 4 + (chip_y ^ dy) * 2 + (chip_x ^ dx)
                yield dz, dy, dx, chip * 2 + (core ^ far)


def crossed(refs, half, dz, dy, dx):
    if half == 0:
        return refs[2 * dy].at[dx, dz % 2]
    return refs[1 + 2 * dx].at[dy, dz % 2]


def wait_for(target, semaphore):
    pltpu.make_async_copy(target, target, semaphore).wait()


def fetch_attend(place, refs, weight, semaphores):
    for part in range(3):
        columns = pl.ds(part * D, D)
        if len(refs) == 1:
            pltpu.make_async_copy(
                refs[0].at[:, columns], weight.at[pl.ds(0, D), columns], semaphores.at[part]
            ).start()
            continue
        for far in range(2):
            for dz, dy, dx, device in piece_places(place, far, True):
                rows = pl.ds(pl.multiple_of(device * 32, 32), 32)
                pltpu.make_async_copy(
                    crossed(refs[4 * far : 4 * far + 4], dz // 2, dz, dy, dx).at[:, columns],
                    weight.at[rows, columns],
                    semaphores.at[part],
                ).start()


def wait_attend(weight, semaphores, part):
    columns = pl.ds(pl.multiple_of(part * D, D), D)
    wait_for(weight.at[pl.ds(0, D), columns], semaphores.at[part])


def padded_rows(values):
    values = values.astype(f32)
    rest = jnp.zeros((WIDE - D - RANK, values.shape[1]), f32)
    return jnp.concatenate([values, rest])


def widen(target, middle):
    rest = jnp.zeros((middle.shape[0], WIDE - D - RANK), f32)
    target[:, D:] = jnp.concatenate([middle, rest], axis=1).astype(bf16)


def fetch_feed(place, refs, project, expand, contract, semaphores):
    if len(refs) == 3:
        pltpu.make_async_copy(refs[0], project, semaphores.at[0]).start()
        for part in range(4):
            pltpu.make_async_copy(
                refs[1].at[:, pl.ds(part * D, D)],
                expand.at[part, pl.ds(0, D)],
                semaphores.at[1 + part],
            ).start()
            pltpu.make_async_copy(
                refs[2].at[pl.ds(part * D, D)],
                contract.at[pl.ds(part * D, D), pl.ds(0, D)],
                semaphores.at[5 + part],
            ).start()
        return

    def rows_of(device, deep, first, count):
        return pl.ds(pl.multiple_of(device * deep + first, 16), count)

    def main_rows(first, count, far, dz, dy, dx):
        held = refs[7 * far : 7 * far + 7]
        block = (
            held[0].at[dz] if dy + dx == 0 else held[2 * (dx + 2 * dy) - 1 + dz // 2].at[dz % 2]
        )
        return block.at[pl.ds(first, count)]

    every = [
        (far, dz, dy, dx, device)
        for far in range(2)
        for dz, dy, dx, device in piece_places(place, far, False)
    ]
    for *at, device in every:
        pltpu.make_async_copy(
            main_rows(0, 32, *at), project.at[rows_of(device, 32, 0, 32)], semaphores.at[0]
        ).start()
    for part in range(4):
        for *at, device in every:
            pltpu.make_async_copy(
                main_rows(32 * (1 + part), 32, *at),
                expand.at[part, rows_of(device, 32, 0, 32)],
                semaphores.at[1 + part],
            ).start()
        for far, dz, dy, dx, device in every:
            if dz != part:
                continue
            columns = pl.ds(0, D)
            pltpu.make_async_copy(
                main_rows(160, FIRST_ROWS, far, dz, dy, dx),
                contract.at[rows_of(device, 128, 0, FIRST_ROWS), columns],
                semaphores.at[5 + part],
            ).start()
            pltpu.make_async_copy(
                refs[14].at[dz, place[3] ^ far, 2 * dy + dx],
                contract.at[rows_of(device, 128, FIRST_ROWS, 128 - FIRST_ROWS), columns],
                semaphores.at[5 + part],
            ).start()


def smem():
    return pl.BlockSpec(memory_space=pltpu.SMEM)


def anywhere(arrays):
    return [pl.BlockSpec(memory_space=pltpu.HBM)] * len(arrays)


def enter_kernel(count, place, latents, modulation, down, up, *refs):
    weights = refs[:count]
    queries, keys_values, middle, wide, weight, semaphores = refs[count:]
    step_at = pl.program_id(0)

    @pl.when(step_at == 0)
    def _():
        fetch_attend(place, weights, weight, semaphores)

        def step(rows):
            normed, _ = normalize(latents[rows].astype(f32))
            values = normed * (1.0 + modulation[SCALE_ATTEND : SCALE_ATTEND + 1]) + modulation[
                SHIFT_ATTEND : SHIFT_ATTEND + 1
            ]
            wide[rows, :D] = values.astype(bf16)

        each_chunk(latents.shape[0], step)
        weight[D:] = padded_rows(up[...]).astype(bf16)
        values = product_back(wide[:, :D], down[...]).astype(bf16)
        middle[...] = values
        widen(wide, values.astype(f32))

    wait_attend(weight, semaphores, step_at)
    projected = product(wide[...], weight[:, pl.ds(pl.multiple_of(step_at * D, D), D)]).astype(bf16)

    @pl.when(step_at == 0)
    def _():
        queries[...] = projected

    @pl.when(step_at > 0)
    def _():
        keys_values[...] = projected


def enter(place, latents, modulation, weights, down, up):
    rows = latents.shape[0]
    columns = up.shape[1]
    return pl.pallas_call(
        lambda *refs: enter_kernel(len(weights), *refs),
        grid=(columns // D,),
        in_specs=[
            smem(),
            whole((rows, D)),
            whole(modulation.shape),
            whole(down.shape),
            whole(up.shape),
        ]
        + anywhere(weights),
        out_specs=[
            whole((rows, D)),
            pl.BlockSpec((rows, D), lambda j: (0, jnp.maximum(j - 1, 0))),
            whole((rows, RANK)),
        ],
        out_shape=[
            jax.ShapeDtypeStruct((rows, D), bf16),
            jax.ShapeDtypeStruct((rows, columns - D), bf16),
            jax.ShapeDtypeStruct((rows, RANK), bf16),
        ],
        scratch_shapes=[
            pltpu.VMEM((rows, WIDE), bf16),
            pltpu.VMEM((WIDE, columns), bf16),
            pltpu.SemaphoreType.DMA((3,)),
        ],
        compiler_params=params(),
        cost_estimate=TINY,
        name="enter",
    )(place, latents, modulation, down, up, *weights)


def head_mask(head, dtype=jnp.bool_):
    lane = lax.broadcasted_iota(jnp.int32, (1, GROUP), 1)
    return jnp.logical_and(lane >= head * HEAD_DIM, lane < (head + 1) * HEAD_DIM)


def attend_kernel(queries, keys_near, values_near, keys_far, values_far, attended, logsum):
    rows = queries.shape[0]
    block = 256
    scale = HEAD_DIM ** (-0.5)
    lane = lax.broadcasted_iota(jnp.int32, (1, 128), 1)
    heads = GROUP // HEAD_DIM
    work = [(start, head) for start in range(0, rows, block) for head in range(heads)]

    def scores(start, head):
        q = queries[start : start + block] * jnp.asarray(scale, bf16)
        mine = jnp.where(head_mask(head), q, jnp.zeros_like(q))
        return product_back(mine, keys_near[...]), product_back(mine, keys_far[...])

    ready = scores(*work[0])
    for at, (start, head) in enumerate(work):
        near, far = ready
        if at + 1 < len(work):
            ready = scores(*work[at + 1])
        if head == 0:
            total = jnp.zeros((block, GROUP), f32)
            sums = jnp.zeros((block, 128), f32)
        highest = jnp.maximum(
            jnp.max(near, axis=1, keepdims=True), jnp.max(far, axis=1, keepdims=True)
        )
        near = jnp.exp2((near - highest) * LOG2E)
        far = jnp.exp2((far - highest) * LOG2E)
        denominator = jnp.sum(near, axis=1, keepdims=True) + jnp.sum(far, axis=1, keepdims=True)
        share = 1.0 / denominator
        out = product((near * share).astype(bf16), values_near[...]) + product(
            (far * share).astype(bf16), values_far[...]
        )
        total = jnp.where(head_mask(head), out, total)
        sums = jnp.where(lane == head, highest + jnp.log(denominator), sums)
        if head == heads - 1:
            attended[start : start + block] = total.astype(bf16)
            logsum[0, start : start + block] = sums


def attend(queries, near, far, first, groups, earlier=None):
    rows = queries.shape[0]
    every = D // GROUP

    def at(start):
        return pl.BlockSpec((rows, GROUP), lambda g: (0, start + first + g))

    given = [] if earlier is None else [earlier]
    return pl.pallas_call(
        lambda *refs: attend_kernel(*refs[:5], *refs[5 + len(given) :]),
        grid=(groups,),
        in_specs=[at(0), at(0), at(every), at(0), at(every)] + anywhere(given),
        out_specs=[at(0), pl.BlockSpec((1, rows, 128), lambda g: (g, 0, 0))],
        out_shape=[
            jax.ShapeDtypeStruct((rows, D), bf16),
            jax.ShapeDtypeStruct((groups, rows, 128), f32),
        ],
        input_output_aliases={5: 0} if given else {},
        compiler_params=params(),
        cost_estimate=TINY,
        name="attend",
    )(queries, near, near, far, far, *given)


def attend_back_kernel(
    queries, keys_near, values_near, keys_far, values_far, grads, logsum,
    grad_queries, grad_near, grad_far, keys_sum, values_sum
):
    rows = queries.shape[0]
    block = 512
    scale = HEAD_DIM ** (-0.5)
    scaled = queries[...] * jnp.asarray(scale, bf16)
    scaled_t = scaled.T
    grads_t = grads[...].T
    heads = GROUP // HEAD_DIM
    work = [(start, head) for start in range(0, rows, block) for head in range(heads)]

    def scores(start, head):
        here = slice(start, start + block)
        mask = head_mask(head)
        q = scaled[here]
        g = grads[here]
        mine = jnp.where(mask, q, jnp.zeros_like(q))
        mine_g = jnp.where(mask, g, jnp.zeros_like(g))
        return (
            product_back(mine, keys_near[...]),
            product_back(mine, keys_far[...]),
            product_back(mine_g, values_near[...]),
            product_back(mine_g, values_far[...]),
        )

    ready = scores(*work[0])
    for at, (start, head) in enumerate(work):
        sn, sf, gn, gf = ready
        if at + 1 < len(work):
            ready = scores(*work[at + 1])
        here = slice(start, start + block)
        part = slice(head * HEAD_DIM, (head + 1) * HEAD_DIM)
        if head == 0:
            total = jnp.zeros((block, GROUP), f32)
        shift = logsum[0, here, head : head + 1]
        pn = jnp.exp2((sn - shift) * LOG2E)
        pf = jnp.exp2((sf - shift) * LOG2E)
        inner = jnp.sum(pn * gn, axis=1, keepdims=True) + jnp.sum(pf * gf, axis=1, keepdims=True)
        dn = (pn * (gn - inner)).astype(bf16)
        df = (pf * (gf - inner)).astype(bf16)
        pn = pn.astype(bf16)
        pf = pf.astype(bf16)
        out = product(dn, keys_near[...]) + product(df, keys_far[...])
        total = jnp.where(head_mask(head), out * scale, total)
        vn = product(grads_t[part, here], pn)
        vf = product(grads_t[part, here], pf)
        kn = product(scaled_t[part, here], dn)
        kf = product(scaled_t[part, here], df)
        if start == 0:
            values_sum[part, :rows] = vn
            values_sum[part, rows:] = vf
            keys_sum[part, :rows] = kn
            keys_sum[part, rows:] = kf
        else:
            values_sum[part, :rows] += vn
            values_sum[part, rows:] += vf
            keys_sum[part, :rows] += kn
            keys_sum[part, rows:] += kf
        if head == heads - 1:
            grad_queries[here] = total.astype(bf16)
    grad_near[0] = keys_sum[:, :rows].T
    grad_near[1] = values_sum[:, :rows].T
    grad_far[0] = keys_sum[:, rows:].T.astype(bf16)
    grad_far[1] = values_sum[:, rows:].T.astype(bf16)


def attend_back(queries, near, far, grads, logsum, first):
    rows = queries.shape[0]
    every = D // GROUP
    groups = logsum.shape[0]

    def at(start):
        return pl.BlockSpec((rows, GROUP), lambda g: (0, start + first + g))

    pair = pl.BlockSpec((2, rows, GROUP), lambda g: (0, 0, g))
    return pl.pallas_call(
        attend_back_kernel,
        grid=(groups,),
        in_specs=[at(0), at(0), at(every), at(0), at(every), at(0),
                  pl.BlockSpec((1, rows, 128), lambda g: (g, 0, 0))],
        out_specs=[pl.BlockSpec((rows, GROUP), lambda g: (0, g)), pair, pair],
        out_shape=[
            jax.ShapeDtypeStruct((rows, groups * GROUP), bf16),
            jax.ShapeDtypeStruct((2, rows, groups * GROUP), f32),
            jax.ShapeDtypeStruct((2, rows, groups * GROUP), bf16),
        ],
        scratch_shapes=[pltpu.VMEM((GROUP, 2 * rows), f32), pltpu.VMEM((GROUP, 2 * rows), f32)],
        compiler_params=params(),
        cost_estimate=TINY,
        name="attend_back",
    )(queries, near, near, far, far, grads, logsum)


def gelu_both(values):
    root = 0.7978845608028654
    square = values * values
    inner = jnp.tanh(values * (root + (root * 0.044715) * square))
    half = 0.5 + 0.5 * inner
    slope = half + (0.5 * values) * (1.0 - inner * inner) * (root + (3.0 * root * 0.044715) * square)
    return values * half, slope


def feed_kernel(
    count, place, latents, attended, cotangent, modulation,
    project_down, project_up, expand_down, expand_up, contract_down, contract_up,
    *refs,
):
    weights = refs[:count]
    (
        block_output, grad_middle, grad_attended, sums,
        grad_project_down, grad_project_up, grad_expand_down, grad_expand_up,
        grad_contract_down, grad_contract_up,
        branch_attend, middle_tokens, entering, grad_branch, branch, grad_entering,
        middle_project, middle_expand, back_contract, grad_branch_attend, back_project,
        project, expand, contract, semaphores,
    ) = refs[count:]
    step_at = pl.program_id(0)
    rows_all = latents.shape[0]

    def row(which):
        return modulation[which : which + 1]

    @pl.when(step_at == 0)
    def _():
        fetch_feed(place, weights, project, expand, contract, semaphores)

        def first(rows):
            grad_branch[rows, :D] = (cotangent[rows].astype(f32) * row(GATE_EXPAND)).astype(bf16)
            branch[rows] = jnp.zeros((CHUNK, WIDE), f32)
            grad_entering[rows] = jnp.zeros((CHUNK, WIDE), f32)

        each_chunk(rows_all, first)
        middle = product_back(grad_branch[:, :D], contract_up[...]).astype(bf16)
        back_contract[...] = middle
        widen(grad_branch, middle.astype(f32))
        middle_project[...] = product_back(attended[...], project_down[...]).astype(bf16)
        wait_for(project, semaphores.at[0])
        branch_attend[...] = product(attended[...], project[...]) + product(
            middle_project[...], project_up[...]
        )

        def step(rows):
            tokens = latents[rows].astype(f32) + row(GATE_ATTEND) * branch_attend[rows]
            middle_tokens[rows] = tokens
            normed, _ = normalize(tokens)
            values = normed * (1.0 + row(SCALE_EXPAND)) + row(SHIFT_EXPAND)
            entering[rows, :D] = values.astype(bf16)

        each_chunk(rows_all, step)
        middle = product_back(entering[:, :D], expand_down[...]).astype(bf16)
        middle_expand[...] = middle
        widen(entering, middle.astype(f32))

    here = pl.ds(pl.multiple_of(step_at * D, D), D)
    expand[step_at, D:] = padded_rows(expand_up[...]).astype(bf16)
    contract[here, D:] = padded_rows(contract_down[...]).T.astype(bf16)
    wait_for(expand.at[step_at, pl.ds(0, D)], semaphores.at[1 + step_at])
    wait_for(contract.at[here, pl.ds(0, D)], semaphores.at[5 + step_at])
    wide = expand[step_at]
    deep = contract[here]
    grads = product_back(grad_branch[...], deep)
    hidden = product(entering[...], wide)
    activated, slope = gelu_both(hidden)
    activated = activated.astype(bf16)
    grads = (grads * slope).astype(bf16)
    branch[...] += product(activated, deep)
    grad_entering[...] += product_back(grads, wide)
    grad_contract_down[...] = product_rows(back_contract[...], activated)
    grad_expand_up[...] = product_rows(middle_expand[...], grads)

    @pl.when(step_at == pl.num_programs(0) - 1)
    def _():
        sums[...] = jnp.zeros_like(sums)
        last_middle = branch[:, D : D + RANK].astype(bf16)
        last_back = grad_entering[:, D : D + RANK].astype(bf16)
        grad_contract_up[...] = product_rows(last_middle, grad_branch[:, :D])
        grad_expand_down[...] = product_rows(last_back, entering[:, :D])
        branch[:, :D] += product(last_middle, contract_up[...])
        grad_entering[:, :D] += product(last_back, expand_down[...])

        def add(which, values):
            sums[which : which + 1] += jnp.sum(values, axis=0, keepdims=True)

        def step(rows):
            out = branch[rows, :D]
            tokens = middle_tokens[rows]
            block_output[rows] = (tokens + row(GATE_EXPAND) * out).astype(bf16)
            cotangents = cotangent[rows].astype(f32)
            add(GATE_EXPAND, cotangents * out)
            grad = grad_entering[rows, :D]
            normed, inverse = normalize(tokens)
            add(SHIFT_EXPAND, grad)
            add(SCALE_EXPAND, grad * normed)
            grad = cotangents + normalize_back(grad * (1.0 + row(SCALE_EXPAND)), normed, inverse)
            grad_middle[rows] = grad
            add(GATE_ATTEND, grad * branch_attend[rows])
            grad_branch_attend[rows] = (grad * row(GATE_ATTEND)).astype(bf16)

        each_chunk(rows_all, step)
        back_project[...] = product_back(grad_branch_attend[...], project_up[...]).astype(bf16)
        grad_attended[...] = (
            product_back(grad_branch_attend[...], project[...])
            + product(back_project[...], project_down[...])
        ).astype(bf16)
        grad_project_up[...] = product_rows(middle_project[...], grad_branch_attend[...])
        grad_project_down[...] = product_rows(back_project[...], attended[...])


def feed(place, latents, attended, cotangent, modulation, weights, chosen):
    rows = latents.shape[0]
    project_down, project_up, expand_down, expand_up, contract_down, contract_up = chosen
    tile = pl.BlockSpec((RANK, D), lambda j: (0, j))
    narrow = whole((RANK, D))

    def buffer(columns, dtype):
        return pltpu.VMEM((rows, columns), dtype)

    return pl.pallas_call(
        lambda *refs: feed_kernel(len(weights), *refs),
        grid=(FF // D,),
        in_specs=[
            smem(),
            whole((rows, D)),
            whole((rows, D)),
            whole((rows, D)),
            whole(modulation.shape),
            narrow,
            narrow,
            narrow,
            tile,
            tile,
            narrow,
        ]
        + anywhere(weights),
        out_specs=[
            whole((rows, D)),
            whole((rows, D)),
            whole((rows, D)),
            whole((8, D)),
            narrow,
            narrow,
            narrow,
            tile,
            tile,
            narrow,
        ],
        out_shape=[
            jax.ShapeDtypeStruct((rows, D), bf16),
            jax.ShapeDtypeStruct((rows, D), f32),
            jax.ShapeDtypeStruct((rows, D), bf16),
            jax.ShapeDtypeStruct((8, D), f32),
            jax.ShapeDtypeStruct((RANK, D), f32),
            jax.ShapeDtypeStruct((RANK, D), f32),
            jax.ShapeDtypeStruct((RANK, D), f32),
            jax.ShapeDtypeStruct((RANK, FF), f32),
            jax.ShapeDtypeStruct((RANK, FF), f32),
            jax.ShapeDtypeStruct((RANK, D), f32),
        ],
        scratch_shapes=[
            buffer(D, f32),
            buffer(D, f32),
            buffer(WIDE, bf16),
            buffer(WIDE, bf16),
            buffer(WIDE, f32),
            buffer(WIDE, f32),
            buffer(RANK, bf16),
            buffer(RANK, bf16),
            buffer(RANK, bf16),
            buffer(D, bf16),
            buffer(RANK, bf16),
            pltpu.VMEM((D, D), bf16),
            pltpu.VMEM((4, WIDE, D), bf16),
            pltpu.VMEM((FF, WIDE), bf16),
            pltpu.SemaphoreType.DMA((9,)),
        ],
        compiler_params=params(),
        cost_estimate=TINY,
        name="feed",
    )(place, latents, attended, cotangent, modulation,
      project_down, project_up, expand_down, expand_up, contract_down, contract_up, *weights)


def leave_kernel(
    count, place, queries_0, queries_1, own_0, own_1, other_0, other_1, down, up, middle,
    modulation, *refs,
):
    weights = refs[:count]
    (
        latents_there, grad_middle_there, input_grad, sums, grad_down, grad_up,
        total, weight, entering, latents, grad_middle, semaphores, semaphore,
    ) = refs[count:]
    step_at = pl.program_id(0)
    rows_all = latents.shape[0]
    copies = [
        pltpu.make_async_copy(source, target, semaphore.at[which])
        for which, (source, target) in enumerate(
            ((latents_there, latents), (grad_middle_there, grad_middle))
        )
    ]

    def through(first, second):
        grads = jnp.concatenate([first, second], axis=1)
        grad_up[...] = product_rows(middle[...], grads)
        return product_back(grads, weight[:, pl.ds(pl.multiple_of(step_at * D, D), D)])

    @pl.when(step_at == 0)
    def _():
        fetch_attend(place, weights, weight, semaphores)
        for copy in copies:
            copy.start()
        weight[D:] = padded_rows(up[...]).astype(bf16)
        wait_attend(weight, semaphores, 0)
        total[...] = through(queries_0[...], queries_1[...])

    @pl.when(step_at > 0)
    def _():
        wait_attend(weight, semaphores, step_at)
        total[...] += through(
            (own_0[0] + other_0[0].astype(f32)).astype(bf16),
            (own_1[0] + other_1[0].astype(f32)).astype(bf16),
        )

    @pl.when(step_at == pl.num_programs(0) - 1)
    def _():
        for copy in copies:
            copy.wait()
        sums[...] = jnp.zeros_like(sums)
        last = total[:, D : D + RANK].astype(bf16)
        total[:, :D] += product(last, down[...])

        def step(rows):
            grad = total[rows, :D]
            normed, inverse = normalize(latents[rows].astype(f32))
            sums[0:1] += jnp.sum(grad, axis=0, keepdims=True)
            sums[1:2] += jnp.sum(grad * normed, axis=0, keepdims=True)
            scale = 1.0 + modulation[SCALE_ATTEND : SCALE_ATTEND + 1]
            shift = modulation[SHIFT_ATTEND : SHIFT_ATTEND + 1]
            entering[rows] = (normed * scale + shift).astype(bf16)
            input_grad[rows] = grad_middle[rows] + normalize_back(grad * scale, normed, inverse)

        each_chunk(rows_all, step)
        grad_down[...] = product_rows(last, entering[...])


def leave(place, queries, own, other, weights, down, up, middle, latents, modulation, grad_middle):
    rows = latents.shape[0]
    columns = up.shape[1]
    tile = pl.BlockSpec((RANK, D), lambda j: (0, j))
    pair = pl.BlockSpec((1, rows, TILE), lambda j: (j // 2, 0, 0))
    return pl.pallas_call(
        lambda *refs: leave_kernel(len(weights), *refs),
        grid=(columns // D,),
        in_specs=[smem()]
        + [whole((rows, TILE))] * 2
        + [pair] * 4
        + [whole(down.shape), whole(up.shape), whole((rows, RANK)), whole(modulation.shape)]
        + anywhere(weights)
        + anywhere(range(2)),
        out_specs=[whole((rows, D)), whole((8, D)), whole((RANK, D)), tile],
        out_shape=[
            jax.ShapeDtypeStruct((rows, D), f32),
            jax.ShapeDtypeStruct((8, D), f32),
            jax.ShapeDtypeStruct((RANK, D), f32),
            jax.ShapeDtypeStruct((RANK, columns), f32),
        ],
        scratch_shapes=[
            pltpu.VMEM((rows, WIDE), f32),
            pltpu.VMEM((WIDE, columns), bf16),
            pltpu.VMEM((rows, D), bf16),
            pltpu.VMEM((rows, D), bf16),
            pltpu.VMEM((rows, D), f32),
            pltpu.SemaphoreType.DMA((3,)),
            pltpu.SemaphoreType.DMA((2,)),
        ],
        compiler_params=params(),
        cost_estimate=TINY,
        name="leave",
    )(place, *queries, *own, *other, down, up, middle, modulation, *weights, latents,
      grad_middle)


PARTS_OF_HALVES = (
    (SHIFT_ATTEND, GATE_ATTEND, SHIFT_EXPAND),
    (SCALE_ATTEND, SCALE_EXPAND, GATE_EXPAND),
)
WIDTHS = (D, 6 * D, D, 3 * D, D, D, D, FF, FF, D)


def swap_cores(values):
    return lax.ppermute(values, "seq", [(0, 1), (1, 0)])


def vmem(count):
    return [pl.BlockSpec(memory_space=pltpu.VMEM)] * count


def rounded_up(span):
    return -(-span // 128) * 128


def note_kernel(condition, choice, out):
    values = condition[...].astype(f32)
    lanes = lax.broadcasted_iota(jnp.int32, (1, 128), 1)
    last = jnp.zeros((1, 128), f32)
    for member in range(5):
        last = jnp.where(lanes == member, choice[0, member].astype(f32), last)
    rows = [values[:, 128 * at : 128 * (at + 1)] for at in range(D // 128)]
    note = jnp.concatenate(rows + [last] + [jnp.zeros((7, 128), f32)], axis=0).astype(bf16)
    for chip in range(out.shape[0]):
        out[chip] = note


def write_notes(chips, condition, choice):
    return pl.pallas_call(
        note_kernel,
        in_specs=vmem(1) + [smem()],
        out_specs=vmem(1)[0],
        out_shape=jax.ShapeDtypeStruct((chips, 16, 128), bf16),
        cost_estimate=TINY,
        name="write_notes",
    )(condition, choice)


def prepare_kernel(early, late, choice, at, lifted, mine, other, tables, out, weight, parts):
    weight[...] = jnp.zeros_like(weight)
    rows = 2 * mine.shape[0]
    m = mine[...].astype(f32)
    o = other[...].astype(f32)
    both = jnp.where(at[1] == 0, jnp.concatenate([m, o]), jnp.concatenate([o, m]))
    weight[pl.ds(pl.multiple_of(at[0], rows), rows)] = both.astype(bf16)
    partial = product(lifted[...], weight[...])
    high = partial.astype(bf16).astype(f32)
    span = parts.shape[2]
    for row in range(8):
        part = slice(row * span, (row + 1) * span)
        parts[:, row] = high[:, part]
        parts[:, 8 + row] = partial[:, part] - high[:, part]
    size = tables.shape[2]
    lanes = lax.broadcasted_iota(jnp.int32, (RANK, size), 1)
    starts = [0, early[0] + early[1], rounded_up(sum(early))]
    starts += [starts[2] + late[0] + late[1], starts[2] + sum(late[:4])]
    for latent in range(out.shape[0]):
        picked = tables[choice[latent, 0]]
        for member in range(1, 5):
            picked = jnp.where(lanes >= starts[member], tables[choice[latent, member]], picked)
        out[latent, :, :size] = picked
        out[latent, :, size:] = parts[latent].astype(bf16)


def prepare(early, late, choice, at, lifted, mine, other, tables):
    chips = choice.shape[0]
    size = tables.shape[2]
    span = mine.shape[1] // 8
    return pl.pallas_call(
        lambda *refs: prepare_kernel(early, late, *refs),
        in_specs=[smem()] * 2 + vmem(4),
        out_specs=vmem(1)[0],
        out_shape=jax.ShapeDtypeStruct((chips, RANK, size + span), bf16),
        scratch_shapes=[
            pltpu.VMEM((128, mine.shape[1]), bf16),
            pltpu.VMEM((chips, 16, span), f32),
        ],
        cost_estimate=TINY,
        name="prepare",
    )(choice, at, lifted, mine, other, tables)


def put_together(own, blocks, first, outs):
    for width, out in zip(own, outs):
        for start in range(0, out.shape[1], 128):
            pieces = []
            for device in range(start // width, (start + 127) // width + 1):
                low = max(start - device * width, 0)
                high = min(start + 128 - device * width, width)
                pieces.append(blocks[device][:, first + low : first + high])
            out[:, start : start + 128] = joined(pieces).astype(bf16)
        first += width


def open_kernel(early, late, core, condition, near, far, *outs):
    tables, (modulation, middle, lifted) = outs[:10], outs[10:]
    size = rounded_up(sum(early)) + rounded_up(sum(late))
    on_first = core[0] == 0
    blocks = []
    near_sum = jnp.zeros((16, near.shape[2] - size), f32)
    far_sum = near_sum
    for chip in range(near.shape[0]):
        n = near[chip].astype(f32)
        f = far[chip].astype(f32)
        near_sum += n[:, size:]
        far_sum += f[:, size:]
        n, f = n[:, :size], f[:, :size]
        blocks += [jnp.where(on_first, n, f), jnp.where(on_first, f, n)]
    put_together(early, blocks, 0, tables[:4])
    put_together(late, blocks, rounded_up(sum(early)), tables[4:])
    near_sum = near_sum[:8] + near_sum[8:]
    far_sum = far_sum[:8] + far_sum[8:]
    values = condition[...].astype(f32)
    lifted[...] = (values * (1.0 / (1.0 + jnp.exp(-values)))).astype(bf16)
    middle[...] = product_back(lifted[...], tables[0][...]).astype(bf16)
    adapted = product(middle[...], tables[1][...])
    halves = (jnp.where(on_first, near_sum, far_sum), jnp.where(on_first, far_sum, near_sum))
    modulation[...] = jnp.zeros_like(modulation)
    for half, targets in zip(halves, PARTS_OF_HALVES):
        for place in range(3 * D // 128):
            row, lane = targets[place // 8], place % 8 * 128
            modulation[row : row + 1, lane : lane + 128] = (
                half[place // 3 : place // 3 + 1, place % 3 * 128 : (place % 3 + 1) * 128]
                + adapted[:, row * D + lane : row * D + lane + 128]
            )


def open_block(early, late, core, condition, near, far):
    chips = near.shape[0]
    shapes = [((RANK, 2 * chips * width), bf16) for width in early + late]
    shapes += [((8, D), f32), ((1, RANK), bf16), ((1, D), bf16)]
    return pl.pallas_call(
        lambda *refs: open_kernel(early, late, *refs),
        in_specs=[smem()] + vmem(3),
        out_specs=vmem(len(shapes)),
        out_shape=[jax.ShapeDtypeStruct(*shape) for shape in shapes],
        compiler_params=params(),
        cost_estimate=TINY,
        name="open_block",
    )(core, condition, near, far)


def joined(pieces):
    return pieces[0] if len(pieces) == 1 else jnp.concatenate(pieces, axis=1)

def pack_into(own, core, grads, near, far):
    chips, span = near.shape[0], near.shape[2]
    on_first = core[0] == 0
    for chip in range(chips):
        parts = []
        for device in (2 * chip, 2 * chip + 1):
            pieces = [grad[:, device * width : (device + 1) * width] for width, grad in zip(own, grads)]
            if span > sum(own):
                pieces.append(jnp.zeros((RANK, span - sum(own)), f32))
            parts.append(joined(pieces))
        near[chip] = jnp.where(on_first, parts[0], parts[1])
        far[chip] = jnp.where(on_first, parts[1], parts[0])


def packed_shapes(own, chips):
    return [jax.ShapeDtypeStruct((chips, RANK, rounded_up(sum(own))), f32)] * 2


def pack_late(own, core, grads):
    return pl.pallas_call(
        lambda core, *refs: pack_into(own, core, refs[:-2], *refs[-2:]),
        out_shape=packed_shapes(own, grads[0].shape[1] // own[0] // 2),
        in_specs=[smem()] + vmem(len(grads)),
        out_specs=vmem(2),
        cost_estimate=TINY,
        name="pack_late",
    )(core, *grads)


def pack_early_kernel(
    own, core, attend, attend_there, feed, feed_there, middle, lifted, up, down_grad, up_grad,
    near, far, grad_modulation, grad_middle, modulate_down, modulate_up
):
    early = attend[...] + attend_there[...]
    late = feed[...] + feed_there[...]
    rows = [early[row : row + 1] if row < 2 else late[row : row + 1] for row in range(6)]
    grads = jnp.concatenate(rows, axis=1).astype(bf16)
    grad_modulation[...] = grads
    back = product_back(grads, up[...]).astype(bf16)
    grad_middle[...] = back
    keep = jnp.where(core[0] == 0, 1.0, 0.0)
    modulate_down[...] = product_rows(back, lifted[...]) * keep
    modulate_up[...] = product_rows(middle[...], grads) * keep
    pack_into(own, core, (modulate_down, modulate_up, down_grad, up_grad), near, far)


def pack_early(own, core, sums, middle, lifted, up, grads):
    return pl.pallas_call(
        lambda *refs: pack_early_kernel(own, *refs),
        out_shape=packed_shapes(own, grads[0].shape[1] // own[2] // 2)
        + [jax.ShapeDtypeStruct((1, 6 * D), bf16), jax.ShapeDtypeStruct((1, RANK), bf16)],
        in_specs=[smem()] + vmem(9),
        out_specs=vmem(4),
        scratch_shapes=[pltpu.VMEM((RANK, D), f32), pltpu.VMEM((RANK, 6 * D), f32)],
        cost_estimate=TINY,
        name="pack_early",
    )(core, *sums, middle, lifted, up, *grads)


def condition_kernel(grads, weight, back, down, condition, out):
    total = jnp.zeros((weight.shape[0], 128), f32)
    for start in range(0, weight.shape[1], 128):
        lanes = slice(start, start + 128)
        total += weight[:, lanes].astype(f32) * grads[:, lanes].astype(f32)
    lifted = jnp.sum(total.T, axis=0, keepdims=True) + product(back[...], down[...])
    values = condition[...].astype(f32)
    gate = 1.0 / (1.0 + jnp.exp(-values))
    out[...] = lifted * gate * (1.0 + values * (1.0 - gate))


def condition_back(grads, weight, back, down, condition):
    part = pl.BlockSpec((1, 128), lambda j: (0, j))
    return pl.pallas_call(
        condition_kernel,
        grid=(D // 128,),
        in_specs=[
            whole(grads.shape),
            pl.BlockSpec((128, weight.shape[1]), lambda j: (j, 0)),
            whole(back.shape),
            pl.BlockSpec((RANK, 128), lambda j: (0, j)),
            part,
        ],
        out_specs=part,
        out_shape=jax.ShapeDtypeStruct(condition.shape, f32),
        cost_estimate=TINY,
        compiler_params=params(),
        name="condition_back",
    )(grads, weight, back, down, condition)


def sums_kernel(own, starts, choice, grads, *refs):
    outs, total = refs[:-1], refs[-1]
    lanes = lax.broadcasted_iota(jnp.int32, grads.shape[1:], 1)
    total[...] = jnp.zeros_like(total)
    for latent in range(grads.shape[0]):
        for member in range(5):
            first = starts[2 * member]
            last = starts[2 * member + 1] + own[2 * member + 1]
            inside = jnp.logical_and(lanes >= first, lanes < last)
            total[choice[latent, member]] += jnp.where(inside, grads[latent].astype(f32), 0.0)
    for entry in range(NADAPT):
        values = total[entry]
        for start, width, out in zip(starts, own, outs):
            out[entry] = values[:, start : start + width]


def table_sums(own, starts, choice, grads):
    sums = pl.pallas_call(
        lambda *refs: sums_kernel(own, starts, *refs),
        out_shape=[jax.ShapeDtypeStruct((NADAPT, RANK, width), f32) for width in own],
        in_specs=[smem()] + vmem(1),
        out_specs=vmem(len(own)),
        scratch_shapes=[pltpu.VMEM((NADAPT,) + grads.shape[1:], f32)],
        cost_estimate=TINY,
        name="table_sums",
    )(choice, grads)
    return [array.transpose(0, 2, 1) if which % 2 == 0 else array for which, array in enumerate(sums)]


def swap_all(arrays):
    return list(arrays) + [swap_cores(array) for array in arrays]


def after(values, *others):
    return lax.optimization_barrier((values, *others))[0]


def cut_kernel(project, expand, contract, main, last):
    deep = project.shape[0]
    main[:deep] = project[...]
    for part in range(4):
        main[(1 + part) * deep : (2 + part) * deep] = expand[:, part * D : (part + 1) * D]
    main[5 * deep :] = contract[: FIRST_ROWS]
    last[...] = contract[FIRST_ROWS:]


def cut_weights(project_weight, expand_weight, contract_weight):
    rows = contract_weight.shape[0] - FIRST_ROWS
    return pl.pallas_call(
        cut_kernel,
        in_specs=vmem(3),
        out_specs=vmem(2),
        out_shape=[
            jax.ShapeDtypeStruct((5 * project_weight.shape[0] + FIRST_ROWS, D), bf16),
            jax.ShapeDtypeStruct((rows, D), bf16),
        ],
        cost_estimate=TINY,
        name="cut_weights",
    )(project_weight, expand_weight, contract_weight)


class PermutedGather:
    chips = 16

    def exchange(self, values, over):
        return lax.ppermute(values, "dp", [(chip, chip ^ over) for chip in range(self.chips)])

    def along(self, values, step=1):
        return lax.ppermute(
            values, "dp", [(chip, (chip + 4 * step) % self.chips) for chip in range(self.chips)]
        )

    def begin(self, attend_weight, project_weight, expand_weight, contract_weight):
        main, last = cut_weights(project_weight, expand_weight, contract_weight)
        self.attend = [attend_weight] + [self.along(attend_weight, step) for step in (1, 2, 3)]
        self.main = self.lines(main)
        self.last = last
        self.attend_crossed = self.cross(jnp.stack(self.attend[:2]), jnp.stack(self.attend[2:]))
        return [self.attend_crossed[1], self.attend_crossed[3]]

    def cross_last(self):
        self.plane = [self.last, self.exchange(self.last, 1), self.exchange(self.last, 2)]
        return self.plane[1:]

    def cross_last_again(self, *before):
        self.attend = self.cross_again(*self.attend_crossed)
        more = [*self.attend[2:], self.exchange(self.plane[1], 2)]
        before, more = self.join(more, before)
        self.attend[2:] = more[:2]
        self.plane += more[2:]
        return before

    def lines(self, values):
        groups = [[z * 4 + line for z in range(self.chips // 4)] for line in range(4)]
        return lax.all_gather(values, "dp", axis=0, tiled=False, axis_index_groups=groups)

    def cross(self, first, second):
        return first, self.exchange(first, 1), second, self.exchange(second, 2)

    def cross_again(self, first, first_there, second, second_there):
        first = jnp.stack([first, first_there])
        second = jnp.stack([second, second_there])
        return [first, second, self.exchange(first, 2), self.exchange(second, 1)]

    def attend_all(self):
        return swap_all(self.attend)

    def cross_main(self):
        planes = lax.all_gather(
            jnp.stack(self.plane),
            ("dp", "seq"),
            axis=0,
            tiled=False,
            axis_index_groups=[
                [2 * (z * 4 + line) + core for z in range(self.chips // 4) for core in range(2)]
                for line in range(4)
            ],
        )
        self.planes = planes.reshape(self.chips // 4, 2, *planes.shape[1:])
        first, second = self.main[:2], self.main[2:]
        self.crossed = [
            self.exchange(first, 1), self.exchange(second, 1),
            self.exchange(first, 2), self.exchange(second, 2),
        ]

    def join(self, held, before):
        joined = lax.optimization_barrier((*before, *held))
        return joined[: len(before)], list(joined[len(before) :])

    def early_main(self, *before):
        before, joined = self.join([self.crossed[0], self.crossed[3]], before)
        self.crossed[0], self.crossed[3] = joined
        return before

    def more_main(self, *before):
        far = [swap_cores(self.main), swap_cores(self.crossed[0])]
        before, joined = self.join([self.crossed[1], self.crossed[2], *far], before)
        self.crossed[1:3], self.far = joined[:2], joined[2:]
        first, second = after(self.crossed[0], before[0]), after(self.crossed[3], before[0])
        self.diagonal = [self.exchange(first, 2), self.exchange(second, 1)]
        return before

    def feed_all(self, *before):
        far = [swap_cores(array) for array in self.crossed[1:]]
        before, joined = self.join([*self.diagonal, *far, self.planes], before)
        diagonal, far, planes = joined[:2], joined[2:-1], joined[-1]
        main = [self.main, *self.crossed, *diagonal]
        other = [*self.far, *far, *(swap_cores(array) for array in diagonal)]
        return before, main + other + [planes]


class WholeGather:
    def begin(self, *matrices):
        self.all = [
            lax.all_gather(array, ("dp", "seq"), axis=0, tiled=True) for array in matrices
        ]
        return []

    def attend_all(self):
        return self.all[:1]

    def cross_last(self):
        return []

    def cross_last_again(self, *before):
        return before

    def cross_main(self):
        pass

    def early_main(self, *before):
        return before

    def more_main(self, *before):
        return before

    def feed_all(self, *before):
        return before, self.all[1:]


def make_local(chips):
    devices = 2 * chips
    own = tuple(width // devices for width in WIDTHS)
    early, late = own[:4], own[4:]
    wide = D // devices

    def local(
        latents,
        condition,
        adapter_choice,
        cotangent,
        modulate_weight,
        attend_weight,
        project_weight,
        expand_weight,
        contract_weight,
        *tables,
    ):
        chip = lax.axis_index("dp")
        core = lax.axis_index("seq")
        place = jnp.stack([chip // 4, chip // 2 % 2, chip % 2, core]).astype(jnp.int32)
        core_at = place[3:]
        tokens = latents[0]

        def to_chips(values):
            return lax.all_to_all(values, "dp", split_axis=0, concat_axis=0, tiled=True)

        gather = PermutedGather() if chips == PermutedGather.chips else WholeGather()
        begun = gather.begin(attend_weight, project_weight, expand_weight, contract_weight)

        notes = to_chips(write_notes(chips, condition, adapter_choice))
        notes = after(notes, *gather.cross_last())
        choice = notes[:, 8, :5].astype(jnp.int32)
        row = 2 * wide * chip // 128
        lifted_all = lax.dynamic_index_in_dim(notes, row, 1, keepdims=False)
        lifted_all = jax.nn.silu(lifted_all.astype(f32)).astype(bf16)

        def columns_of(which):
            return jnp.concatenate(
                [
                    lax.dynamic_slice_in_dim(modulate_weight, which * D, D, 1),
                    lax.dynamic_slice_in_dim(modulate_weight, 2 * D + which * 2 * D, 2 * D, 1),
                ],
                axis=1,
            )

        def laid_out(own, tables):
            values = jnp.concatenate(
                [table.transpose(0, 2, 1) if which % 2 == 0 else table for which, table in enumerate(tables)],
                axis=2,
            )
            span = values.shape[2]
            return jnp.pad(values, ((0, 0), (0, 0), (0, rounded_up(span) - span)))

        at = jnp.stack([2 * wide * chip % 128, core])
        block = prepare(
            early,
            late,
            choice,
            at.astype(jnp.int32),
            lifted_all,
            columns_of(core),
            swap_cores(after(columns_of(1 - core), notes)),
            jnp.concatenate([laid_out(early, tables[:4]), laid_out(late, tables[4:])], axis=2),
        )
        block = after(block, *begun)
        (block,) = gather.cross_last_again(to_chips(block))
        *chosen, modulation, middle_modulate, lifted = open_block(
            early, late, core_at, condition, block, swap_cores(block)
        )
        modulate_down, modulate_up, attend_down, attend_up, *chosen_late = chosen

        attend_all = gather.attend_all()
        gather.cross_main()
        queries, near, middle_attend = enter(
            place, tokens, modulation, attend_all, attend_down, attend_up
        )
        queries, near = gather.early_main(queries, near)
        far = swap_cores(near)
        attended, logsum_0 = attend(queries, near, far, 0, 2)
        logsum_0, far = gather.more_main(logsum_0, far)
        attended, logsum_1 = attend(queries, near, far, 2, 2, attended)
        (attended, logsum_1), feed_all = gather.feed_all(attended, logsum_1)
        modulate_all = lax.all_gather(
            after(modulate_weight, *feed_all), ("dp", "seq"), axis=0, tiled=True
        )
        block_output, grad_middle, grad_attended, sums_feed, *grads_late = feed(
            place, tokens, attended, cotangent[0], modulation, feed_all, chosen_late
        )
        packed, packed_far = pack_late(late, core_at, grads_late)
        half_0 = attend_back(queries, near, far, grad_attended, logsum_0, 0)
        packed_far = swap_cores(packed_far)
        grad_attended, packed_far = lax.optimization_barrier((grad_attended, packed_far))
        grads_late = (packed + packed_far).astype(bf16)
        half_1 = attend_back(queries, near, far, grad_attended, logsum_1, 2)
        grads_attended = [half_0, half_1]
        grad_queries, grad_near, grad_far = zip(*grads_attended)
        input_grad, sums_attend, *grads_attend = leave(
            place,
            grad_queries,
            grad_near,
            [swap_cores(grad) for grad in grad_far],
            attend_all,
            attend_down,
            attend_up,
            middle_attend,
            tokens,
            modulation,
            grad_middle,
        )

        sums_attend, grads_late = lax.optimization_barrier((sums_attend, grads_late))
        packed, packed_far, grad_modulation, grad_middle_modulate = pack_early(
            early,
            core_at,
            (sums_attend, swap_cores(sums_attend), sums_feed, swap_cores(sums_feed)),
            middle_modulate,
            lifted,
            modulate_up,
            grads_attend,
        )
        grads_early = (packed + swap_cores(packed_far)).astype(bf16)
        arrived = to_chips(jnp.concatenate([grads_early, grads_late], axis=2))
        condition_grad = condition_back(
            grad_modulation, modulate_all, grad_middle_modulate, modulate_down, condition
        )
        arrived = after(arrived, condition_grad)
        starts = [sum(early[:member]) for member in range(4)]
        starts += [rounded_up(sum(early)) + sum(late[:member]) for member in range(6)]
        owned = table_sums(own, starts, choice, arrived)
        return (block_output[None], input_grad[None], condition_grad, *owned)

    return local


def solution(mesh):
    rows = P(("dp", "seq"), None)
    down = P(None, ("dp", "seq"), None)
    up = P(None, None, ("dp", "seq"))
    tokens = P("dp", "seq", None)
    return jax.shard_map(
        make_local(mesh.shape["dp"]),
        mesh=mesh,
        in_specs=(tokens, P("dp", None), P("dp", None), tokens) + (rows,) * 5 + (down, up) * 5,
        out_specs=(tokens, tokens, P("dp", None)) + (down, up) * 5,
        check_vma=False,
    )
```

```python
import jax
import jax.numpy as jnp
from jax import lax
from jax.experimental import pallas as pl
from jax.experimental.pallas import tpu as pltpu
from jax.sharding import PartitionSpec as P

D = 1024
HEADS = 16
HEAD_DIM = 64
FF = 4096
RANK = 16
bf16 = jnp.bfloat16
f32 = jnp.float32
EPSILON = 1e-06
TINY = pl.CostEstimate(flops=1, bytes_accessed=1, transcendentals=0)
LOG2E = 1.4426950408889634
GROUP = 256
TILE = 512
WIDE = D + 128
NADAPT = 8
CHUNK = 256
VMEM_LIMIT = 62 * 1024 * 1024
FIRST_ROWS = 32
SHIFT_ATTEND, SCALE_ATTEND, GATE_ATTEND, SHIFT_EXPAND, SCALE_EXPAND, GATE_EXPAND = range(6)


def product(left, right):
    return lax.dot_general(left, right, (((1,), (0,)), ((), ())), preferred_element_type=f32)


def product_back(grads, right):
    return lax.dot_general(grads, right, (((1,), (1,)), ((), ())), preferred_element_type=f32)


def product_rows(left, right):
    return lax.dot_general(left, right, (((0,), (0,)), ((), ())), preferred_element_type=f32)


def normalize(values):
    centred = values - jnp.mean(values, axis=-1, keepdims=True)
    variance = jnp.mean(centred * centred, axis=-1, keepdims=True)
    inverse = lax.rsqrt(variance + EPSILON)
    return centred * inverse, inverse


def normalize_back(grads, normed, inverse):
    mean = jnp.mean(grads, axis=-1, keepdims=True)
    along = jnp.mean(grads * normed, axis=-1, keepdims=True)
    return (grads - mean - normed * along) * inverse


def each_chunk(rows, step):
    def body(position, carry):
        step(pl.ds(pl.multiple_of(position * CHUNK, CHUNK), CHUNK))
        return carry

    lax.fori_loop(0, rows // CHUNK, body, 0)


def whole(shape):
    return pl.BlockSpec(shape, lambda *_: (0,) * len(shape))


def params():
    return pltpu.CompilerParams(vmem_limit_bytes=VMEM_LIMIT)


def piece_places(place, far, relative):
    chip_z, chip_y, chip_x, core = (place[axis] for axis in range(4))
    for dz in range(4):
        z = lax.rem(chip_z + 4 - dz, 4) if relative else dz
        for dy in range(2):
            for dx in range(2):
                chip = z * 4 + (chip_y ^ dy) * 2 + (chip_x ^ dx)
                yield dz, dy, dx, chip * 2 + (core ^ far)


def crossed(refs, half, dz, dy, dx):
    if half == 0:
        return refs[2 * dy].at[dx, dz % 2]
    return refs[1 + 2 * dx].at[dy, dz % 2]


def wait_for(target, semaphore):
    pltpu.make_async_copy(target, target, semaphore).wait()


def fetch_attend(place, refs, weight, semaphores):
    for part in range(3):
        columns = pl.ds(part * D, D)
        if len(refs) == 1:
            pltpu.make_async_copy(
                refs[0].at[:, columns], weight.at[pl.ds(0, D), columns], semaphores.at[part]
            ).start()
            continue
        for far in range(2):
            for dz, dy, dx, device in piece_places(place, far, True):
                rows = pl.ds(pl.multiple_of(device * 32, 32), 32)
                pltpu.make_async_copy(
                    crossed(refs[4 * far : 4 * far + 4], dz // 2, dz, dy, dx).at[:, columns],
                    weight.at[rows, columns],
                    semaphores.at[part],
                ).start()


def wait_attend(weight, semaphores, part):
    columns = pl.ds(pl.multiple_of(part * D, D), D)
    wait_for(weight.at[pl.ds(0, D), columns], semaphores.at[part])


def padded_rows(values):
    values = values.astype(f32)
    rest = jnp.zeros((WIDE - D - RANK, values.shape[1]), f32)
    return jnp.concatenate([values, rest])


def widen(target, middle):
    rest = jnp.zeros((middle.shape[0], WIDE - D - RANK), f32)
    target[:, D:] = jnp.concatenate([middle, rest], axis=1).astype(bf16)


def fetch_feed(place, refs, project, expand, contract, semaphores):
    if len(refs) == 3:
        pltpu.make_async_copy(refs[0], project, semaphores.at[0]).start()
        for part in range(4):
            pltpu.make_async_copy(
                refs[1].at[:, pl.ds(part * D, D)],
                expand.at[part, pl.ds(0, D)],
                semaphores.at[1 + part],
            ).start()
            pltpu.make_async_copy(
                refs[2].at[pl.ds(part * D, D)],
                contract.at[pl.ds(part * D, D), pl.ds(0, D)],
                semaphores.at[5 + part],
            ).start()
        return

    def rows_of(device, deep, first, count):
        return pl.ds(pl.multiple_of(device * deep + first, 16), count)

    def main_rows(first, count, far, dz, dy, dx):
        held = refs[7 * far : 7 * far + 7]
        block = (
            held[0].at[dz] if dy + dx == 0 else held[2 * (dx + 2 * dy) - 1 + dz // 2].at[dz % 2]
        )
        return block.at[pl.ds(first, count)]

    every = [
        (far, dz, dy, dx, device)
        for far in range(2)
        for dz, dy, dx, device in piece_places(place, far, False)
    ]
    for *at, device in every:
        pltpu.make_async_copy(
            main_rows(0, 32, *at), project.at[rows_of(device, 32, 0, 32)], semaphores.at[0]
        ).start()
    for part in range(4):
        for *at, device in every:
            pltpu.make_async_copy(
                main_rows(32 * (1 + part), 32, *at),
                expand.at[part, rows_of(device, 32, 0, 32)],
                semaphores.at[1 + part],
            ).start()
        for far, dz, dy, dx, device in every:
            if dz != part:
                continue
            columns = pl.ds(0, D)
            pltpu.make_async_copy(
                main_rows(160, FIRST_ROWS, far, dz, dy, dx),
                contract.at[rows_of(device, 128, 0, FIRST_ROWS), columns],
                semaphores.at[5 + part],
            ).start()
            pltpu.make_async_copy(
                refs[14].at[dz, place[3] ^ far, 2 * dy + dx],
                contract.at[rows_of(device, 128, FIRST_ROWS, 128 - FIRST_ROWS), columns],
                semaphores.at[5 + part],
            ).start()


def smem():
    return pl.BlockSpec(memory_space=pltpu.SMEM)


def anywhere(arrays):
    return [pl.BlockSpec(memory_space=pltpu.HBM)] * len(arrays)


def enter_kernel(count, place, latents, modulation, down, up, *refs):
    weights = refs[:count]
    queries, keys_values, middle, wide, weight, semaphores = refs[count:]
    step_at = pl.program_id(0)

    @pl.when(step_at == 0)
    def _():
        fetch_attend(place, weights, weight, semaphores)

        def step(rows):
            normed, _ = normalize(latents[rows].astype(f32))
            values = normed * (1.0 + modulation[SCALE_ATTEND : SCALE_ATTEND + 1]) + modulation[
                SHIFT_ATTEND : SHIFT_ATTEND + 1
            ]
            wide[rows, :D] = values.astype(bf16)

        each_chunk(latents.shape[0], step)
        weight[D:] = padded_rows(up[...]).astype(bf16)
        values = product_back(wide[:, :D], down[...]).astype(bf16)
        middle[...] = values
        widen(wide, values.astype(f32))

    wait_attend(weight, semaphores, step_at)
    projected = product(wide[...], weight[:, pl.ds(pl.multiple_of(step_at * D, D), D)]).astype(bf16)

    @pl.when(step_at == 0)
    def _():
        queries[...] = projected

    @pl.when(step_at > 0)
    def _():
        keys_values[...] = projected


def enter(place, latents, modulation, weights, down, up):
    rows = latents.shape[0]
    columns = up.shape[1]
    return pl.pallas_call(
        lambda *refs: enter_kernel(len(weights), *refs),
        grid=(columns // D,),
        in_specs=[
            smem(),
            whole((rows, D)),
            whole(modulation.shape),
            whole(down.shape),
            whole(up.shape),
        ]
        + anywhere(weights),
        out_specs=[
            whole((rows, D)),
            pl.BlockSpec((rows, D), lambda j: (0, jnp.maximum(j - 1, 0))),
            whole((rows, RANK)),
        ],
        out_shape=[
            jax.ShapeDtypeStruct((rows, D), bf16),
            jax.ShapeDtypeStruct((rows, columns - D), bf16),
            jax.ShapeDtypeStruct((rows, RANK), bf16),
        ],
        scratch_shapes=[
            pltpu.VMEM((rows, WIDE), bf16),
            pltpu.VMEM((WIDE, columns), bf16),
            pltpu.SemaphoreType.DMA((3,)),
        ],
        compiler_params=params(),
        cost_estimate=TINY,
        name="enter",
    )(place, latents, modulation, down, up, *weights)


def head_mask(head, dtype=jnp.bool_):
    lane = lax.broadcasted_iota(jnp.int32, (1, GROUP), 1)
    return jnp.logical_and(lane >= head * HEAD_DIM, lane < (head + 1) * HEAD_DIM)


def attend_kernel(queries, keys_near, values_near, keys_far, values_far, attended, logsum):
    rows = queries.shape[0]
    block = 256
    scale = HEAD_DIM ** (-0.5)
    lane = lax.broadcasted_iota(jnp.int32, (1, 128), 1)
    heads = GROUP // HEAD_DIM
    work = [(start, head) for start in range(0, rows, block) for head in range(heads)]

    def scores(start, head):
        q = queries[start : start + block] * jnp.asarray(scale, bf16)
        mine = jnp.where(head_mask(head), q, jnp.zeros_like(q))
        return product_back(mine, keys_near[...]), product_back(mine, keys_far[...])

    ready = scores(*work[0])
    for at, (start, head) in enumerate(work):
        near, far = ready
        if at + 1 < len(work):
            ready = scores(*work[at + 1])
        if head == 0:
            total = jnp.zeros((block, GROUP), f32)
            sums = jnp.zeros((block, 128), f32)
        highest = jnp.maximum(
            jnp.max(near, axis=1, keepdims=True), jnp.max(far, axis=1, keepdims=True)
        )
        near = jnp.exp2((near - highest) * LOG2E)
        far = jnp.exp2((far - highest) * LOG2E)
        denominator = jnp.sum(near, axis=1, keepdims=True) + jnp.sum(far, axis=1, keepdims=True)
        share = 1.0 / denominator
        out = product((near * share).astype(bf16), values_near[...]) + product(
            (far * share).astype(bf16), values_far[...]
        )
        total = jnp.where(head_mask(head), out, total)
        sums = jnp.where(lane == head, highest + jnp.log(denominator), sums)
        if head == heads - 1:
            attended[start : start + block] = total.astype(bf16)
            logsum[0, start : start + block] = sums


def attend(queries, near, far, first, groups, earlier=None):
    rows = queries.shape[0]
    every = D // GROUP

    def at(start):
        return pl.BlockSpec((rows, GROUP), lambda g: (0, start + first + g))

    given = [] if earlier is None else [earlier]
    return pl.pallas_call(
        lambda *refs: attend_kernel(*refs[:5], *refs[5 + len(given) :]),
        grid=(groups,),
        in_specs=[at(0), at(0), at(every), at(0), at(every)] + anywhere(given),
        out_specs=[at(0), pl.BlockSpec((1, rows, 128), lambda g: (g, 0, 0))],
        out_shape=[
            jax.ShapeDtypeStruct((rows, D), bf16),
            jax.ShapeDtypeStruct((groups, rows, 128), f32),
        ],
        input_output_aliases={5: 0} if given else {},
        compiler_params=params(),
        cost_estimate=TINY,
        name="attend",
    )(queries, near, near, far, far, *given)


def attend_back_kernel(
    queries, keys_near, values_near, keys_far, values_far, grads, logsum,
    grad_queries, grad_near, grad_far, keys_sum, values_sum
):
    rows = queries.shape[0]
    block = 512
    scale = HEAD_DIM ** (-0.5)
    scaled = queries[...] * jnp.asarray(scale, bf16)
    scaled_t = scaled.T
    grads_t = grads[...].T
    heads = GROUP // HEAD_DIM
    work = [(start, head) for start in range(0, rows, block) for head in range(heads)]

    def scores(start, head):
        here = slice(start, start + block)
        mask = head_mask(head)
        q = scaled[here]
        g = grads[here]
        mine = jnp.where(mask, q, jnp.zeros_like(q))
        mine_g = jnp.where(mask, g, jnp.zeros_like(g))
        return (
            product_back(mine, keys_near[...]),
            product_back(mine, keys_far[...]),
            product_back(mine_g, values_near[...]),
            product_back(mine_g, values_far[...]),
        )

    ready = scores(*work[0])
    for at, (start, head) in enumerate(work):
        sn, sf, gn, gf = ready
        if at + 1 < len(work):
            ready = scores(*work[at + 1])
        here = slice(start, start + block)
        part = slice(head * HEAD_DIM, (head + 1) * HEAD_DIM)
        if head == 0:
            total = jnp.zeros((block, GROUP), f32)
        shift = logsum[0, here, head : head + 1]
        pn = jnp.exp2((sn - shift) * LOG2E)
        pf = jnp.exp2((sf - shift) * LOG2E)
        inner = jnp.sum(pn * gn, axis=1, keepdims=True) + jnp.sum(pf * gf, axis=1, keepdims=True)
        dn = (pn * (gn - inner)).astype(bf16)
        df = (pf * (gf - inner)).astype(bf16)
        pn = pn.astype(bf16)
        pf = pf.astype(bf16)
        out = product(dn, keys_near[...]) + product(df, keys_far[...])
        total = jnp.where(head_mask(head), out * scale, total)
        vn = product(grads_t[part, here], pn)
        vf = product(grads_t[part, here], pf)
        kn = product(scaled_t[part, here], dn)
        kf = product(scaled_t[part, here], df)
        if start == 0:
            values_sum[part, :rows] = vn
            values_sum[part, rows:] = vf
            keys_sum[part, :rows] = kn
            keys_sum[part, rows:] = kf
        else:
            values_sum[part, :rows] += vn
            values_sum[part, rows:] += vf
            keys_sum[part, :rows] += kn
            keys_sum[part, rows:] += kf
        if head == heads - 1:
            grad_queries[here] = total.astype(bf16)
    grad_near[0] = keys_sum[:, :rows].T
    grad_near[1] = values_sum[:, :rows].T
    grad_far[0] = keys_sum[:, rows:].T.astype(bf16)
    grad_far[1] = values_sum[:, rows:].T.astype(bf16)


def attend_back(queries, near, far, grads, logsum, first):
    rows = queries.shape[0]
    every = D // GROUP
    groups = logsum.shape[0]

    def at(start):
        return pl.BlockSpec((rows, GROUP), lambda g: (0, start + first + g))

    pair = pl.BlockSpec((2, rows, GROUP), lambda g: (0, 0, g))
    return pl.pallas_call(
        attend_back_kernel,
        grid=(groups,),
        in_specs=[at(0), at(0), at(every), at(0), at(every), at(0),
                  pl.BlockSpec((1, rows, 128), lambda g: (g, 0, 0))],
        out_specs=[pl.BlockSpec((rows, GROUP), lambda g: (0, g)), pair, pair],
        out_shape=[
            jax.ShapeDtypeStruct((rows, groups * GROUP), bf16),
            jax.ShapeDtypeStruct((2, rows, groups * GROUP), f32),
            jax.ShapeDtypeStruct((2, rows, groups * GROUP), bf16),
        ],
        scratch_shapes=[pltpu.VMEM((GROUP, 2 * rows), f32), pltpu.VMEM((GROUP, 2 * rows), f32)],
        compiler_params=params(),
        cost_estimate=TINY,
        name="attend_back",
    )(queries, near, near, far, far, grads, logsum)


def gelu_both(values):
    root = 0.7978845608028654
    square = values * values
    inner = jnp.tanh(values * (root + (root * 0.044715) * square))
    half = 0.5 + 0.5 * inner
    slope = half + (0.5 * values) * (1.0 - inner * inner) * (root + (3.0 * root * 0.044715) * square)
    return values * half, slope


def feed_kernel(
    count, place, latents, attended, cotangent, modulation,
    project_down, project_up, expand_down, expand_up, contract_down, contract_up,
    *refs,
):
    weights = refs[:count]
    (
        block_output, grad_middle, grad_attended, sums,
        grad_project_down, grad_project_up, grad_expand_down, grad_expand_up,
        grad_contract_down, grad_contract_up,
        branch_attend, middle_tokens, entering, grad_branch, branch, grad_entering,
        middle_project, middle_expand, back_contract, grad_branch_attend, back_project,
        project, expand, contract, semaphores,
    ) = refs[count:]
    step_at = pl.program_id(0)
    rows_all = latents.shape[0]

    def row(which):
        return modulation[which : which + 1]

    @pl.when(step_at == 0)
    def _():
        fetch_feed(place, weights, project, expand, contract, semaphores)

        def first(rows):
            grad_branch[rows, :D] = (cotangent[rows].astype(f32) * row(GATE_EXPAND)).astype(bf16)
            branch[rows] = jnp.zeros((CHUNK, WIDE), f32)
            grad_entering[rows] = jnp.zeros((CHUNK, WIDE), f32)

        each_chunk(rows_all, first)
        middle = product_back(grad_branch[:, :D], contract_up[...]).astype(bf16)
        back_contract[...] = middle
        widen(grad_branch, middle.astype(f32))
        middle_project[...] = product_back(attended[...], project_down[...]).astype(bf16)
        wait_for(project, semaphores.at[0])
        branch_attend[...] = product(attended[...], project[...]) + product(
            middle_project[...], project_up[...]
        )

        def step(rows):
            tokens = latents[rows].astype(f32) + row(GATE_ATTEND) * branch_attend[rows]
            middle_tokens[rows] = tokens
            normed, _ = normalize(tokens)
            values = normed * (1.0 + row(SCALE_EXPAND)) + row(SHIFT_EXPAND)
            entering[rows, :D] = values.astype(bf16)

        each_chunk(rows_all, step)
        middle = product_back(entering[:, :D], expand_down[...]).astype(bf16)
        middle_expand[...] = middle
        widen(entering, middle.astype(f32))

    here = pl.ds(pl.multiple_of(step_at * D, D), D)
    expand[step_at, D:] = padded_rows(expand_up[...]).astype(bf16)
    contract[here, D:] = padded_rows(contract_down[...]).T.astype(bf16)
    wait_for(expand.at[step_at, pl.ds(0, D)], semaphores.at[1 + step_at])
    wait_for(contract.at[here, pl.ds(0, D)], semaphores.at[5 + step_at])
    wide = expand[step_at]
    deep = contract[here]
    grads = product_back(grad_branch[...], deep)
    hidden = product(entering[...], wide)
    activated, slope = gelu_both(hidden)
    activated = activated.astype(bf16)
    grads = (grads * slope).astype(bf16)
    branch[...] += product(activated, deep)
    grad_entering[...] += product_back(grads, wide)
    grad_contract_down[...] = product_rows(back_contract[...], activated)
    grad_expand_up[...] = product_rows(middle_expand[...], grads)

    @pl.when(step_at == pl.num_programs(0) - 1)
    def _():
        sums[...] = jnp.zeros_like(sums)
        last_middle = branch[:, D : D + RANK].astype(bf16)
        last_back = grad_entering[:, D : D + RANK].astype(bf16)
        grad_contract_up[...] = product_rows(last_middle, grad_branch[:, :D])
        grad_expand_down[...] = product_rows(last_back, entering[:, :D])
        branch[:, :D] += product(last_middle, contract_up[...])
        grad_entering[:, :D] += product(last_back, expand_down[...])

        def add(which, values):
            sums[which : which + 1] += jnp.sum(values, axis=0, keepdims=True)

        def step(rows):
            out = branch[rows, :D]
            tokens = middle_tokens[rows]
            block_output[rows] = (tokens + row(GATE_EXPAND) * out).astype(bf16)
            cotangents = cotangent[rows].astype(f32)
            add(GATE_EXPAND, cotangents * out)
            grad = grad_entering[rows, :D]
            normed, inverse = normalize(tokens)
            add(SHIFT_EXPAND, grad)
            add(SCALE_EXPAND, grad * normed)
            grad = cotangents + normalize_back(grad * (1.0 + row(SCALE_EXPAND)), normed, inverse)
            grad_middle[rows] = grad
            add(GATE_ATTEND, grad * branch_attend[rows])
            grad_branch_attend[rows] = (grad * row(GATE_ATTEND)).astype(bf16)

        each_chunk(rows_all, step)
        back_project[...] = product_back(grad_branch_attend[...], project_up[...]).astype(bf16)
        grad_attended[...] = (
            product_back(grad_branch_attend[...], project[...])
            + product(back_project[...], project_down[...])
        ).astype(bf16)
        grad_project_up[...] = product_rows(middle_project[...], grad_branch_attend[...])
        grad_project_down[...] = product_rows(back_project[...], attended[...])


def feed(place, latents, attended, cotangent, modulation, weights, chosen):
    rows = latents.shape[0]
    project_down, project_up, expand_down, expand_up, contract_down, contract_up = chosen
    tile = pl.BlockSpec((RANK, D), lambda j: (0, j))
    narrow = whole((RANK, D))

    def buffer(columns, dtype):
        return pltpu.VMEM((rows, columns), dtype)

    return pl.pallas_call(
        lambda *refs: feed_kernel(len(weights), *refs),
        grid=(FF // D,),
        in_specs=[
            smem(),
            whole((rows, D)),
            whole((rows, D)),
            whole((rows, D)),
            whole(modulation.shape),
            narrow,
            narrow,
            narrow,
            tile,
            tile,
            narrow,
        ]
        + anywhere(weights),
        out_specs=[
            whole((rows, D)),
            whole((rows, D)),
            whole((rows, D)),
            whole((8, D)),
            narrow,
            narrow,
            narrow,
            tile,
            tile,
            narrow,
        ],
        out_shape=[
            jax.ShapeDtypeStruct((rows, D), bf16),
            jax.ShapeDtypeStruct((rows, D), f32),
            jax.ShapeDtypeStruct((rows, D), bf16),
            jax.ShapeDtypeStruct((8, D), f32),
            jax.ShapeDtypeStruct((RANK, D), f32),
            jax.ShapeDtypeStruct((RANK, D), f32),
            jax.ShapeDtypeStruct((RANK, D), f32),
            jax.ShapeDtypeStruct((RANK, FF), f32),
            jax.ShapeDtypeStruct((RANK, FF), f32),
            jax.ShapeDtypeStruct((RANK, D), f32),
        ],
        scratch_shapes=[
            buffer(D, f32),
            buffer(D, f32),
            buffer(WIDE, bf16),
            buffer(WIDE, bf16),
            buffer(WIDE, f32),
            buffer(WIDE, f32),
            buffer(RANK, bf16),
            buffer(RANK, bf16),
            buffer(RANK, bf16),
            buffer(D, bf16),
            buffer(RANK, bf16),
            pltpu.VMEM((D, D), bf16),
            pltpu.VMEM((4, WIDE, D), bf16),
            pltpu.VMEM((FF, WIDE), bf16),
            pltpu.SemaphoreType.DMA((9,)),
        ],
        compiler_params=params(),
        cost_estimate=TINY,
        name="feed",
    )(place, latents, attended, cotangent, modulation,
      project_down, project_up, expand_down, expand_up, contract_down, contract_up, *weights)


def leave_kernel(
    count, place, queries_0, queries_1, own_0, own_1, other_0, other_1, down, up, middle,
    modulation, *refs,
):
    weights = refs[:count]
    (
        latents_there, grad_middle_there, input_grad, sums, grad_down, grad_up,
        total, weight, entering, latents, grad_middle, semaphores, semaphore,
    ) = refs[count:]
    step_at = pl.program_id(0)
    rows_all = latents.shape[0]
    copies = [
        pltpu.make_async_copy(source, target, semaphore.at[which])
        for which, (source, target) in enumerate(
            ((latents_there, latents), (grad_middle_there, grad_middle))
        )
    ]

    def through(first, second):
        grads = jnp.concatenate([first, second], axis=1)
        grad_up[...] = product_rows(middle[...], grads)
        return product_back(grads, weight[:, pl.ds(pl.multiple_of(step_at * D, D), D)])

    @pl.when(step_at == 0)
    def _():
        fetch_attend(place, weights, weight, semaphores)
        for copy in copies:
            copy.start()
        weight[D:] = padded_rows(up[...]).astype(bf16)
        wait_attend(weight, semaphores, 0)
        total[...] = through(queries_0[...], queries_1[...])

    @pl.when(step_at > 0)
    def _():
        wait_attend(weight, semaphores, step_at)
        total[...] += through(
            (own_0[0] + other_0[0].astype(f32)).astype(bf16),
            (own_1[0] + other_1[0].astype(f32)).astype(bf16),
        )

    @pl.when(step_at == pl.num_programs(0) - 1)
    def _():
        for copy in copies:
            copy.wait()
        sums[...] = jnp.zeros_like(sums)
        last = total[:, D : D + RANK].astype(bf16)
        total[:, :D] += product(last, down[...])

        def step(rows):
            grad = total[rows, :D]
            normed, inverse = normalize(latents[rows].astype(f32))
            sums[0:1] += jnp.sum(grad, axis=0, keepdims=True)
            sums[1:2] += jnp.sum(grad * normed, axis=0, keepdims=True)
            scale = 1.0 + modulation[SCALE_ATTEND : SCALE_ATTEND + 1]
            shift = modulation[SHIFT_ATTEND : SHIFT_ATTEND + 1]
            entering[rows] = (normed * scale + shift).astype(bf16)
            input_grad[rows] = grad_middle[rows] + normalize_back(grad * scale, normed, inverse)

        each_chunk(rows_all, step)
        grad_down[...] = product_rows(last, entering[...])


def leave(place, queries, own, other, weights, down, up, middle, latents, modulation, grad_middle):
    rows = latents.shape[0]
    columns = up.shape[1]
    tile = pl.BlockSpec((RANK, D), lambda j: (0, j))
    pair = pl.BlockSpec((1, rows, TILE), lambda j: (j // 2, 0, 0))
    return pl.pallas_call(
        lambda *refs: leave_kernel(len(weights), *refs),
        grid=(columns // D,),
        in_specs=[smem()]
        + [whole((rows, TILE))] * 2
        + [pair] * 4
        + [whole(down.shape), whole(up.shape), whole((rows, RANK)), whole(modulation.shape)]
        + anywhere(weights)
        + anywhere(range(2)),
        out_specs=[whole((rows, D)), whole((8, D)), whole((RANK, D)), tile],
        out_shape=[
            jax.ShapeDtypeStruct((rows, D), f32),
            jax.ShapeDtypeStruct((8, D), f32),
            jax.ShapeDtypeStruct((RANK, D), f32),
            jax.ShapeDtypeStruct((RANK, columns), f32),
        ],
        scratch_shapes=[
            pltpu.VMEM((rows, WIDE), f32),
            pltpu.VMEM((WIDE, columns), bf16),
            pltpu.VMEM((rows, D), bf16),
            pltpu.VMEM((rows, D), bf16),
            pltpu.VMEM((rows, D), f32),
            pltpu.SemaphoreType.DMA((3,)),
            pltpu.SemaphoreType.DMA((2,)),
        ],
        compiler_params=params(),
        cost_estimate=TINY,
        name="leave",
    )(place, *queries, *own, *other, down, up, middle, modulation, *weights, latents,
      grad_middle)


PARTS_OF_HALVES = (
    (SHIFT_ATTEND, GATE_ATTEND, SHIFT_EXPAND),
    (SCALE_ATTEND, SCALE_EXPAND, GATE_EXPAND),
)
WIDTHS = (D, 6 * D, D, 3 * D, D, D, D, FF, FF, D)


def swap_cores(values):
    return lax.ppermute(values, "seq", [(0, 1), (1, 0)])


def vmem(count):
    return [pl.BlockSpec(memory_space=pltpu.VMEM)] * count


def rounded_up(span):
    return -(-span // 128) * 128


def note_kernel(condition, choice, out):
    values = condition[...].astype(f32)
    lanes = lax.broadcasted_iota(jnp.int32, (1, 128), 1)
    last = jnp.zeros((1, 128), f32)
    for member in range(5):
        last = jnp.where(lanes == member, choice[0, member].astype(f32), last)
    rows = [values[:, 128 * at : 128 * (at + 1)] for at in range(D // 128)]
    note = jnp.concatenate(rows + [last] + [jnp.zeros((7, 128), f32)], axis=0).astype(bf16)
    for chip in range(out.shape[0]):
        out[chip] = note


def write_notes(chips, condition, choice):
    return pl.pallas_call(
        note_kernel,
        in_specs=vmem(1) + [smem()],
        out_specs=vmem(1)[0],
        out_shape=jax.ShapeDtypeStruct((chips, 16, 128), bf16),
        cost_estimate=TINY,
        name="write_notes",
    )(condition, choice)


def prepare_kernel(early, late, choice, at, lifted, mine, other, tables, out, weight, parts):
    weight[...] = jnp.zeros_like(weight)
    rows = 2 * mine.shape[0]
    m = mine[...].astype(f32)
    o = other[...].astype(f32)
    both = jnp.where(at[1] == 0, jnp.concatenate([m, o]), jnp.concatenate([o, m]))
    weight[pl.ds(pl.multiple_of(at[0], rows), rows)] = both.astype(bf16)
    partial = product(lifted[...], weight[...])
    high = partial.astype(bf16).astype(f32)
    span = parts.shape[2]
    for row in range(8):
        part = slice(row * span, (row + 1) * span)
        parts[:, row] = high[:, part]
        parts[:, 8 + row] = partial[:, part] - high[:, part]
    size = tables.shape[2]
    lanes = lax.broadcasted_iota(jnp.int32, (RANK, size), 1)
    starts = [0, early[0] + early[1], rounded_up(sum(early))]
    starts += [starts[2] + late[0] + late[1], starts[2] + sum(late[:4])]
    for latent in range(out.shape[0]):
        picked = tables[choice[latent, 0]]
        for member in range(1, 5):
            picked = jnp.where(lanes >= starts[member], tables[choice[latent, member]], picked)
        out[latent, :, :size] = picked
        out[latent, :, size:] = parts[latent].astype(bf16)


def prepare(early, late, choice, at, lifted, mine, other, tables):
    chips = choice.shape[0]
    size = tables.shape[2]
    span = mine.shape[1] // 8
    return pl.pallas_call(
        lambda *refs: prepare_kernel(early, late, *refs),
        in_specs=[smem()] * 2 + vmem(4),
        out_specs=vmem(1)[0],
        out_shape=jax.ShapeDtypeStruct((chips, RANK, size + span), bf16),
        scratch_shapes=[
            pltpu.VMEM((128, mine.shape[1]), bf16),
            pltpu.VMEM((chips, 16, span), f32),
        ],
        cost_estimate=TINY,
        name="prepare",
    )(choice, at, lifted, mine, other, tables)


def put_together(own, blocks, first, outs):
    for width, out in zip(own, outs):
        for start in range(0, out.shape[1], 128):
            pieces = []
            for device in range(start // width, (start + 127) // width + 1):
                low = max(start - device * width, 0)
                high = min(start + 128 - device * width, width)
                pieces.append(blocks[device][:, first + low : first + high])
            out[:, start : start + 128] = joined(pieces).astype(bf16)
        first += width


def open_kernel(early, late, core, condition, near, far, *outs):
    tables, (modulation, middle, lifted) = outs[:10], outs[10:]
    size = rounded_up(sum(early)) + rounded_up(sum(late))
    on_first = core[0] == 0
    blocks = []
    near_sum = jnp.zeros((16, near.shape[2] - size), f32)
    far_sum = near_sum
    for chip in range(near.shape[0]):
        n = near[chip].astype(f32)
        f = far[chip].astype(f32)
        near_sum += n[:, size:]
        far_sum += f[:, size:]
        n, f = n[:, :size], f[:, :size]
        blocks += [jnp.where(on_first, n, f), jnp.where(on_first, f, n)]
    put_together(early, blocks, 0, tables[:4])
    put_together(late, blocks, rounded_up(sum(early)), tables[4:])
    near_sum = near_sum[:8] + near_sum[8:]
    far_sum = far_sum[:8] + far_sum[8:]
    values = condition[...].astype(f32)
    lifted[...] = (values * (1.0 / (1.0 + jnp.exp(-values)))).astype(bf16)
    middle[...] = product_back(lifted[...], tables[0][...]).astype(bf16)
    adapted = product(middle[...], tables[1][...])
    halves = (jnp.where(on_first, near_sum, far_sum), jnp.where(on_first, far_sum, near_sum))
    modulation[...] = jnp.zeros_like(modulation)
    for half, targets in zip(halves, PARTS_OF_HALVES):
        for place in range(3 * D // 128):
            row, lane = targets[place // 8], place % 8 * 128
            modulation[row : row + 1, lane : lane + 128] = (
                half[place // 3 : place // 3 + 1, place % 3 * 128 : (place % 3 + 1) * 128]
                + adapted[:, row * D + lane : row * D + lane + 128]
            )


def open_block(early, late, core, condition, near, far):
    chips = near.shape[0]
    shapes = [((RANK, 2 * chips * width), bf16) for width in early + late]
    shapes += [((8, D), f32), ((1, RANK), bf16), ((1, D), bf16)]
    return pl.pallas_call(
        lambda *refs: open_kernel(early, late, *refs),
        in_specs=[smem()] + vmem(3),
        out_specs=vmem(len(shapes)),
        out_shape=[jax.ShapeDtypeStruct(*shape) for shape in shapes],
        compiler_params=params(),
        cost_estimate=TINY,
        name="open_block",
    )(core, condition, near, far)


def joined(pieces):
    return pieces[0] if len(pieces) == 1 else jnp.concatenate(pieces, axis=1)

def pack_into(own, core, grads, near, far):
    chips, span = near.shape[0], near.shape[2]
    on_first = core[0] == 0
    for chip in range(chips):
        parts = []
        for device in (2 * chip, 2 * chip + 1):
            pieces = [grad[:, device * width : (device + 1) * width] for width, grad in zip(own, grads)]
            if span > sum(own):
                pieces.append(jnp.zeros((RANK, span - sum(own)), f32))
            parts.append(joined(pieces))
        near[chip] = jnp.where(on_first, parts[0], parts[1])
        far[chip] = jnp.where(on_first, parts[1], parts[0])


def packed_shapes(own, chips):
    return [jax.ShapeDtypeStruct((chips, RANK, rounded_up(sum(own))), f32)] * 2


def pack_late(own, core, grads):
    return pl.pallas_call(
        lambda core, *refs: pack_into(own, core, refs[:-2], *refs[-2:]),
        out_shape=packed_shapes(own, grads[0].shape[1] // own[0] // 2),
        in_specs=[smem()] + vmem(len(grads)),
        out_specs=vmem(2),
        cost_estimate=TINY,
        name="pack_late",
    )(core, *grads)


def pack_early_kernel(
    own, core, attend, attend_there, feed, feed_there, middle, lifted, up, down_grad, up_grad,
    near, far, grad_modulation, grad_middle, modulate_down, modulate_up
):
    early = attend[...] + attend_there[...]
    late = feed[...] + feed_there[...]
    rows = [early[row : row + 1] if row < 2 else late[row : row + 1] for row in range(6)]
    grads = jnp.concatenate(rows, axis=1).astype(bf16)
    grad_modulation[...] = grads
    back = product_back(grads, up[...]).astype(bf16)
    grad_middle[...] = back
    keep = jnp.where(core[0] == 0, 1.0, 0.0)
    modulate_down[...] = product_rows(back, lifted[...]) * keep
    modulate_up[...] = product_rows(middle[...], grads) * keep
    pack_into(own, core, (modulate_down, modulate_up, down_grad, up_grad), near, far)


def pack_early(own, core, sums, middle, lifted, up, grads):
    return pl.pallas_call(
        lambda *refs: pack_early_kernel(own, *refs),
        out_shape=packed_shapes(own, grads[0].shape[1] // own[2] // 2)
        + [jax.ShapeDtypeStruct((1, 6 * D), bf16), jax.ShapeDtypeStruct((1, RANK), bf16)],
        in_specs=[smem()] + vmem(9),
        out_specs=vmem(4),
        scratch_shapes=[pltpu.VMEM((RANK, D), f32), pltpu.VMEM((RANK, 6 * D), f32)],
        cost_estimate=TINY,
        name="pack_early",
    )(core, *sums, middle, lifted, up, *grads)


def condition_kernel(grads, weight, back, down, condition, out):
    total = jnp.zeros((weight.shape[0], 128), f32)
    for start in range(0, weight.shape[1], 128):
        lanes = slice(start, start + 128)
        total += weight[:, lanes].astype(f32) * grads[:, lanes].astype(f32)
    lifted = jnp.sum(total.T, axis=0, keepdims=True) + product(back[...], down[...])
    values = condition[...].astype(f32)
    gate = 1.0 / (1.0 + jnp.exp(-values))
    out[...] = lifted * gate * (1.0 + values * (1.0 - gate))


def condition_back(grads, weight, back, down, condition):
    part = pl.BlockSpec((1, 128), lambda j: (0, j))
    return pl.pallas_call(
        condition_kernel,
        grid=(D // 128,),
        in_specs=[
            whole(grads.shape),
            pl.BlockSpec((128, weight.shape[1]), lambda j: (j, 0)),
            whole(back.shape),
            pl.BlockSpec((RANK, 128), lambda j: (0, j)),
            part,
        ],
        out_specs=part,
        out_shape=jax.ShapeDtypeStruct(condition.shape, f32),
        cost_estimate=TINY,
        compiler_params=params(),
        name="condition_back",
    )(grads, weight, back, down, condition)


def sums_kernel(own, starts, choice, grads, *refs):
    outs, total = refs[:-1], refs[-1]
    lanes = lax.broadcasted_iota(jnp.int32, grads.shape[1:], 1)
    total[...] = jnp.zeros_like(total)
    for latent in range(grads.shape[0]):
        for member in range(5):
            first = starts[2 * member]
            last = starts[2 * member + 1] + own[2 * member + 1]
            inside = jnp.logical_and(lanes >= first, lanes < last)
            total[choice[latent, member]] += jnp.where(inside, grads[latent].astype(f32), 0.0)
    for entry in range(NADAPT):
        values = total[entry]
        for start, width, out in zip(starts, own, outs):
            out[entry] = values[:, start : start + width]


def table_sums(own, starts, choice, grads):
    sums = pl.pallas_call(
        lambda *refs: sums_kernel(own, starts, *refs),
        out_shape=[jax.ShapeDtypeStruct((NADAPT, RANK, width), f32) for width in own],
        in_specs=[smem()] + vmem(1),
        out_specs=vmem(len(own)),
        scratch_shapes=[pltpu.VMEM((NADAPT,) + grads.shape[1:], f32)],
        cost_estimate=TINY,
        name="table_sums",
    )(choice, grads)
    return [array.transpose(0, 2, 1) if which % 2 == 0 else array for which, array in enumerate(sums)]


def swap_all(arrays):
    return list(arrays) + [swap_cores(array) for array in arrays]


def after(values, *others):
    return lax.optimization_barrier((values, *others))[0]


def cut_kernel(project, expand, contract, main, last):
    deep = project.shape[0]
    main[:deep] = project[...]
    for part in range(4):
        main[(1 + part) * deep : (2 + part) * deep] = expand[:, part * D : (part + 1) * D]
    main[5 * deep :] = contract[: FIRST_ROWS]
    last[...] = contract[FIRST_ROWS:]


def cut_weights(project_weight, expand_weight, contract_weight):
    rows = contract_weight.shape[0] - FIRST_ROWS
    return pl.pallas_call(
        cut_kernel,
        in_specs=vmem(3),
        out_specs=vmem(2),
        out_shape=[
            jax.ShapeDtypeStruct((5 * project_weight.shape[0] + FIRST_ROWS, D), bf16),
            jax.ShapeDtypeStruct((rows, D), bf16),
        ],
        cost_estimate=TINY,
        name="cut_weights",
    )(project_weight, expand_weight, contract_weight)


class PermutedGather:
    chips = 16

    def exchange(self, values, over):
        return lax.ppermute(values, "dp", [(chip, chip ^ over) for chip in range(self.chips)])

    def along(self, values, step=1):
        return lax.ppermute(
            values, "dp", [(chip, (chip + 4 * step) % self.chips) for chip in range(self.chips)]
        )

    def begin(self, attend_weight, project_weight, expand_weight, contract_weight):
        main, last = cut_weights(project_weight, expand_weight, contract_weight)
        self.attend = [attend_weight] + [self.along(attend_weight, step) for step in (1, 2, 3)]
        self.main = self.lines(main)
        self.last = last
        self.attend_crossed = self.cross(jnp.stack(self.attend[:2]), jnp.stack(self.attend[2:]))
        return [self.attend_crossed[1], self.attend_crossed[3]]

    def cross_last(self):
        self.plane = [self.last, self.exchange(self.last, 1), self.exchange(self.last, 2)]
        return self.plane[1:]

    def cross_last_again(self, *before):
        self.attend = self.cross_again(*self.attend_crossed)
        more = [*self.attend[2:], self.exchange(self.plane[1], 2)]
        before, more = self.join(more, before)
        self.attend[2:] = more[:2]
        self.plane += more[2:]
        return before

    def lines(self, values):
        groups = [[z * 4 + line for z in range(self.chips // 4)] for line in range(4)]
        return lax.all_gather(values, "dp", axis=0, tiled=False, axis_index_groups=groups)

    def cross(self, first, second):
        return first, self.exchange(first, 1), second, self.exchange(second, 2)

    def cross_again(self, first, first_there, second, second_there):
        first = jnp.stack([first, first_there])
        second = jnp.stack([second, second_there])
        return [first, second, self.exchange(first, 2), self.exchange(second, 1)]

    def attend_all(self):
        return swap_all(self.attend)

    def cross_main(self):
        planes = lax.all_gather(
            jnp.stack(self.plane),
            ("dp", "seq"),
            axis=0,
            tiled=False,
            axis_index_groups=[
                [2 * (z * 4 + line) + core for z in range(self.chips // 4) for core in range(2)]
                for line in range(4)
            ],
        )
        self.planes = planes.reshape(self.chips // 4, 2, *planes.shape[1:])
        first, second = self.main[:2], self.main[2:]
        self.crossed = [
            self.exchange(first, 1), self.exchange(second, 1),
            self.exchange(first, 2), self.exchange(second, 2),
        ]

    def join(self, held, before):
        joined = lax.optimization_barrier((*before, *held))
        return joined[: len(before)], list(joined[len(before) :])

    def early_main(self, *before):
        before, joined = self.join([self.crossed[0], self.crossed[3]], before)
        self.crossed[0], self.crossed[3] = joined
        return before

    def more_main(self, *before):
        far = [swap_cores(self.main), swap_cores(self.crossed[0])]
        before, joined = self.join([self.crossed[1], self.crossed[2], *far], before)
        self.crossed[1:3], self.far = joined[:2], joined[2:]
        first, second = after(self.crossed[0], before[0]), after(self.crossed[3], before[0])
        self.diagonal = [self.exchange(first, 2), self.exchange(second, 1)]
        return before

    def feed_all(self, *before):
        far = [swap_cores(array) for array in self.crossed[1:]]
        before, joined = self.join([*self.diagonal, *far, self.planes], before)
        diagonal, far, planes = joined[:2], joined[2:-1], joined[-1]
        main = [self.main, *self.crossed, *diagonal]
        other = [*self.far, *far, *(swap_cores(array) for array in diagonal)]
        return before, main + other + [planes]


class WholeGather:
    def begin(self, *matrices):
        self.all = [
            lax.all_gather(array, ("dp", "seq"), axis=0, tiled=True) for array in matrices
        ]
        return []

    def attend_all(self):
        return self.all[:1]

    def cross_last(self):
        return []

    def cross_last_again(self, *before):
        return before

    def cross_main(self):
        pass

    def early_main(self, *before):
        return before

    def more_main(self, *before):
        return before

    def feed_all(self, *before):
        return before, self.all[1:]


def make_local(chips):
    devices = 2 * chips
    own = tuple(width // devices for width in WIDTHS)
    early, late = own[:4], own[4:]
    wide = D // devices

    def local(
        latents,
        condition,
        adapter_choice,
        cotangent,
        modulate_weight,
        attend_weight,
        project_weight,
        expand_weight,
        contract_weight,
        *tables,
    ):
        chip = lax.axis_index("dp")
        core = lax.axis_index("seq")
        place = jnp.stack([chip // 4, chip // 2 % 2, chip % 2, core]).astype(jnp.int32)
        core_at = place[3:]
        tokens = latents[0]

        def to_chips(values):
            return lax.all_to_all(values, "dp", split_axis=0, concat_axis=0, tiled=True)

        gather = PermutedGather() if chips == PermutedGather.chips else WholeGather()
        begun = gather.begin(attend_weight, project_weight, expand_weight, contract_weight)

        notes = to_chips(write_notes(chips, condition, adapter_choice))
        notes = after(notes, *gather.cross_last())
        choice = notes[:, 8, :5].astype(jnp.int32)
        row = 2 * wide * chip // 128
        lifted_all = lax.dynamic_index_in_dim(notes, row, 1, keepdims=False)
        lifted_all = jax.nn.silu(lifted_all.astype(f32)).astype(bf16)

        def columns_of(which):
            return jnp.concatenate(
                [
                    lax.dynamic_slice_in_dim(modulate_weight, which * D, D, 1),
                    lax.dynamic_slice_in_dim(modulate_weight, 2 * D + which * 2 * D, 2 * D, 1),
                ],
                axis=1,
            )

        def laid_out(own, tables):
            values = jnp.concatenate(
                [table.transpose(0, 2, 1) if which % 2 == 0 else table for which, table in enumerate(tables)],
                axis=2,
            )
            span = values.shape[2]
            return jnp.pad(values, ((0, 0), (0, 0), (0, rounded_up(span) - span)))

        at = jnp.stack([2 * wide * chip % 128, core])
        block = prepare(
            early,
            late,
            choice,
            at.astype(jnp.int32),
            lifted_all,
            columns_of(core),
            swap_cores(after(columns_of(1 - core), notes)),
            jnp.concatenate([laid_out(early, tables[:4]), laid_out(late, tables[4:])], axis=2),
        )
        block = after(block, *begun)
        (block,) = gather.cross_last_again(to_chips(block))
        *chosen, modulation, middle_modulate, lifted = open_block(
            early, late, core_at, condition, block, swap_cores(block)
        )
        modulate_down, modulate_up, attend_down, attend_up, *chosen_late = chosen

        attend_all = gather.attend_all()
        gather.cross_main()
        queries, near, middle_attend = enter(
            place, tokens, modulation, attend_all, attend_down, attend_up
        )
        queries, near = gather.early_main(queries, near)
        far = swap_cores(near)
        attended, logsum_0 = attend(queries, near, far, 0, 2)
        logsum_0, far = gather.more_main(logsum_0, far)
        attended, logsum_1 = attend(queries, near, far, 2, 2, attended)
        (attended, logsum_1), feed_all = gather.feed_all(attended, logsum_1)
        modulate_all = lax.all_gather(
            after(modulate_weight, *feed_all), ("dp", "seq"), axis=0, tiled=True
        )
        block_output, grad_middle, grad_attended, sums_feed, *grads_late = feed(
            place, tokens, attended, cotangent[0], modulation, feed_all, chosen_late
        )
        grads_attended = [
            attend_back(queries, near, far, grad_attended, logsum, 2 * half)
            for half, logsum in enumerate((logsum_0, logsum_1))
        ]
        grad_queries, grad_near, grad_far = zip(*grads_attended)
        packed, packed_far = pack_late(
            late, core_at, [after(grads_late[0], *grad_far), *grads_late[1:]]
        )
        grad_queries = [after(grad_queries[0], packed), grad_queries[1]]
        input_grad, sums_attend, *grads_attend = leave(
            place,
            grad_queries,
            grad_near,
            [swap_cores(grad) for grad in grad_far],
            attend_all,
            attend_down,
            attend_up,
            middle_attend,
            tokens,
            modulation,
            grad_middle,
        )

        grads_late = (packed + swap_cores(packed_far)).astype(bf16)
        packed, packed_far, grad_modulation, grad_middle_modulate = pack_early(
            early,
            core_at,
            (sums_attend, swap_cores(sums_attend), sums_feed, swap_cores(sums_feed)),
            middle_modulate,
            lifted,
            modulate_up,
            grads_attend,
        )
        grads_early = (packed + swap_cores(packed_far)).astype(bf16)
        arrived = to_chips(jnp.concatenate([grads_early, grads_late], axis=2))
        condition_grad = condition_back(
            grad_modulation, modulate_all, grad_middle_modulate, modulate_down, condition
        )
        arrived = after(arrived, condition_grad)
        starts = [sum(early[:member]) for member in range(4)]
        starts += [rounded_up(sum(early)) + sum(late[:member]) for member in range(6)]
        owned = table_sums(own, starts, choice, arrived)
        return (block_output[None], input_grad[None], condition_grad, *owned)

    return local


def solution(mesh):
    rows = P(("dp", "seq"), None)
    down = P(None, ("dp", "seq"), None)
    up = P(None, None, ("dp", "seq"))
    tokens = P("dp", "seq", None)
    return jax.shard_map(
        make_local(mesh.shape["dp"]),
        mesh=mesh,
        in_specs=(tokens, P("dp", None), P("dp", None), tokens) + (rows,) * 5 + (down, up) * 5,
        out_specs=(tokens, tokens, P("dp", None)) + (down, up) * 5,
        check_vma=False,
    )
```

```python
import jax
import jax.numpy as jnp
from jax import lax
from jax.experimental import pallas as pl
from jax.experimental.pallas import tpu as pltpu
from jax.sharding import PartitionSpec as P

D = 1024
HEADS = 16
HEAD_DIM = 64
FF = 4096
RANK = 16
bf16 = jnp.bfloat16
f32 = jnp.float32
EPSILON = 1e-06
TINY = pl.CostEstimate(flops=1, bytes_accessed=1, transcendentals=0)
LOG2E = 1.4426950408889634
GROUP = 256
TILE = 512
WIDE = D + 128
NADAPT = 8
CHUNK = 256
VMEM_LIMIT = 62 * 1024 * 1024
FIRST_ROWS = 32
SHIFT_ATTEND, SCALE_ATTEND, GATE_ATTEND, SHIFT_EXPAND, SCALE_EXPAND, GATE_EXPAND = range(6)


def product(left, right):
    return lax.dot_general(left, right, (((1,), (0,)), ((), ())), preferred_element_type=f32)


def product_back(grads, right):
    return lax.dot_general(grads, right, (((1,), (1,)), ((), ())), preferred_element_type=f32)


def product_rows(left, right):
    return lax.dot_general(left, right, (((0,), (0,)), ((), ())), preferred_element_type=f32)


def normalize(values):
    centred = values - jnp.mean(values, axis=-1, keepdims=True)
    variance = jnp.mean(centred * centred, axis=-1, keepdims=True)
    inverse = lax.rsqrt(variance + EPSILON)
    return centred * inverse, inverse


def normalize_back(grads, normed, inverse):
    mean = jnp.mean(grads, axis=-1, keepdims=True)
    along = jnp.mean(grads * normed, axis=-1, keepdims=True)
    return (grads - mean - normed * along) * inverse


def each_chunk(rows, step):
    def body(position, carry):
        step(pl.ds(pl.multiple_of(position * CHUNK, CHUNK), CHUNK))
        return carry

    lax.fori_loop(0, rows // CHUNK, body, 0)


def whole(shape):
    return pl.BlockSpec(shape, lambda *_: (0,) * len(shape))


def params():
    return pltpu.CompilerParams(vmem_limit_bytes=VMEM_LIMIT)


def piece_places(place, far, relative):
    chip_z, chip_y, chip_x, core = (place[axis] for axis in range(4))
    for dz in range(4):
        z = lax.rem(chip_z + 4 - dz, 4) if relative else dz
        for dy in range(2):
            for dx in range(2):
                chip = z * 4 + (chip_y ^ dy) * 2 + (chip_x ^ dx)
                yield dz, dy, dx, chip * 2 + (core ^ far)


def crossed(refs, half, dz, dy, dx):
    if half == 0:
        return refs[2 * dy].at[dx, dz % 2]
    return refs[1 + 2 * dx].at[dy, dz % 2]


def wait_for(target, semaphore):
    pltpu.make_async_copy(target, target, semaphore).wait()


def fetch_attend(place, refs, weight, semaphores):
    for part in range(3):
        columns = pl.ds(part * D, D)
        if len(refs) == 1:
            pltpu.make_async_copy(
                refs[0].at[:, columns], weight.at[pl.ds(0, D), columns], semaphores.at[part]
            ).start()
            continue
        for far in range(2):
            for dz, dy, dx, device in piece_places(place, far, True):
                rows = pl.ds(pl.multiple_of(device * 32, 32), 32)
                pltpu.make_async_copy(
                    crossed(refs[4 * far : 4 * far + 4], dz // 2, dz, dy, dx).at[:, columns],
                    weight.at[rows, columns],
                    semaphores.at[part],
                ).start()


def wait_attend(weight, semaphores, part):
    columns = pl.ds(pl.multiple_of(part * D, D), D)
    wait_for(weight.at[pl.ds(0, D), columns], semaphores.at[part])


def padded_rows(values):
    values = values.astype(f32)
    rest = jnp.zeros((WIDE - D - RANK, values.shape[1]), f32)
    return jnp.concatenate([values, rest])


def widen(target, middle):
    rest = jnp.zeros((middle.shape[0], WIDE - D - RANK), f32)
    target[:, D:] = jnp.concatenate([middle, rest], axis=1).astype(bf16)


def fetch_feed(place, refs, project, expand, contract, semaphores):
    if len(refs) == 3:
        pltpu.make_async_copy(refs[0], project, semaphores.at[0]).start()
        for part in range(4):
            pltpu.make_async_copy(
                refs[1].at[:, pl.ds(part * D, D)],
                expand.at[part, pl.ds(0, D)],
                semaphores.at[1 + part],
            ).start()
            pltpu.make_async_copy(
                refs[2].at[pl.ds(part * D, D)],
                contract.at[pl.ds(part * D, D), pl.ds(0, D)],
                semaphores.at[5 + part],
            ).start()
        return

    def rows_of(device, deep, first, count):
        return pl.ds(pl.multiple_of(device * deep + first, 16), count)

    def main_rows(first, count, far, dz, dy, dx):
        held = refs[7 * far : 7 * far + 7]
        block = (
            held[0].at[dz] if dy + dx == 0 else held[2 * (dx + 2 * dy) - 1 + dz // 2].at[dz % 2]
        )
        return block.at[pl.ds(first, count)]

    every = [
        (far, dz, dy, dx, device)
        for far in range(2)
        for dz, dy, dx, device in piece_places(place, far, False)
    ]
    for *at, device in every:
        pltpu.make_async_copy(
            main_rows(0, 32, *at), project.at[rows_of(device, 32, 0, 32)], semaphores.at[0]
        ).start()
    for part in range(4):
        for *at, device in every:
            pltpu.make_async_copy(
                main_rows(32 * (1 + part), 32, *at),
                expand.at[part, rows_of(device, 32, 0, 32)],
                semaphores.at[1 + part],
            ).start()
        for far, dz, dy, dx, device in every:
            if dz != part:
                continue
            columns = pl.ds(0, D)
            pltpu.make_async_copy(
                main_rows(160, FIRST_ROWS, far, dz, dy, dx),
                contract.at[rows_of(device, 128, 0, FIRST_ROWS), columns],
                semaphores.at[5 + part],
            ).start()
            pltpu.make_async_copy(
                refs[14].at[dz, place[3] ^ far, 2 * dy + dx],
                contract.at[rows_of(device, 128, FIRST_ROWS, 128 - FIRST_ROWS), columns],
                semaphores.at[5 + part],
            ).start()


def smem():
    return pl.BlockSpec(memory_space=pltpu.SMEM)


def anywhere(arrays):
    return [pl.BlockSpec(memory_space=pltpu.HBM)] * len(arrays)


def enter_kernel(count, place, latents, modulation, down, up, *refs):
    weights = refs[:count]
    queries, keys_values, middle, wide, weight, semaphores = refs[count:]
    step_at = pl.program_id(0)

    @pl.when(step_at == 0)
    def _():
        fetch_attend(place, weights, weight, semaphores)

        def step(rows):
            normed, _ = normalize(latents[rows].astype(f32))
            values = normed * (1.0 + modulation[SCALE_ATTEND : SCALE_ATTEND + 1]) + modulation[
                SHIFT_ATTEND : SHIFT_ATTEND + 1
            ]
            wide[rows, :D] = values.astype(bf16)

        each_chunk(latents.shape[0], step)
        weight[D:] = padded_rows(up[...]).astype(bf16)
        values = product_back(wide[:, :D], down[...]).astype(bf16)
        middle[...] = values
        widen(wide, values.astype(f32))

    wait_attend(weight, semaphores, step_at)
    projected = product(wide[...], weight[:, pl.ds(pl.multiple_of(step_at * D, D), D)]).astype(bf16)

    @pl.when(step_at == 0)
    def _():
        queries[...] = projected

    @pl.when(step_at > 0)
    def _():
        keys_values[...] = projected


def enter(place, latents, modulation, weights, down, up):
    rows = latents.shape[0]
    columns = up.shape[1]
    return pl.pallas_call(
        lambda *refs: enter_kernel(len(weights), *refs),
        grid=(columns // D,),
        in_specs=[
            smem(),
            whole((rows, D)),
            whole(modulation.shape),
            whole(down.shape),
            whole(up.shape),
        ]
        + anywhere(weights),
        out_specs=[
            whole((rows, D)),
            pl.BlockSpec((rows, D), lambda j: (0, jnp.maximum(j - 1, 0))),
            whole((rows, RANK)),
        ],
        out_shape=[
            jax.ShapeDtypeStruct((rows, D), bf16),
            jax.ShapeDtypeStruct((rows, columns - D), bf16),
            jax.ShapeDtypeStruct((rows, RANK), bf16),
        ],
        scratch_shapes=[
            pltpu.VMEM((rows, WIDE), bf16),
            pltpu.VMEM((WIDE, columns), bf16),
            pltpu.SemaphoreType.DMA((3,)),
        ],
        compiler_params=params(),
        cost_estimate=TINY,
        name="enter",
    )(place, latents, modulation, down, up, *weights)


def head_mask(head, dtype=jnp.bool_):
    lane = lax.broadcasted_iota(jnp.int32, (1, GROUP), 1)
    return jnp.logical_and(lane >= head * HEAD_DIM, lane < (head + 1) * HEAD_DIM)


def attend_kernel(queries, keys_near, values_near, keys_far, values_far, attended, logsum):
    rows = queries.shape[0]
    block = 256
    scale = HEAD_DIM ** (-0.5)
    lane = lax.broadcasted_iota(jnp.int32, (1, 128), 1)
    heads = GROUP // HEAD_DIM
    work = [(start, head) for start in range(0, rows, block) for head in range(heads)]

    def scores(start, head):
        q = queries[start : start + block] * jnp.asarray(scale, bf16)
        mine = jnp.where(head_mask(head), q, jnp.zeros_like(q))
        return product_back(mine, keys_near[...]), product_back(mine, keys_far[...])

    ready = scores(*work[0])
    for at, (start, head) in enumerate(work):
        near, far = ready
        if at + 1 < len(work):
            ready = scores(*work[at + 1])
        if head == 0:
            total = jnp.zeros((block, GROUP), f32)
            sums = jnp.zeros((block, 128), f32)
        highest = jnp.maximum(
            jnp.max(near, axis=1, keepdims=True), jnp.max(far, axis=1, keepdims=True)
        )
        near = jnp.exp2((near - highest) * LOG2E)
        far = jnp.exp2((far - highest) * LOG2E)
        denominator = jnp.sum(near, axis=1, keepdims=True) + jnp.sum(far, axis=1, keepdims=True)
        share = 1.0 / denominator
        out = product((near * share).astype(bf16), values_near[...]) + product(
            (far * share).astype(bf16), values_far[...]
        )
        total = jnp.where(head_mask(head), out, total)
        sums = jnp.where(lane == head, highest + jnp.log(denominator), sums)
        if head == heads - 1:
            attended[start : start + block] = total.astype(bf16)
            logsum[0, start : start + block] = sums


def attend(queries, near, far, first, groups, earlier=None):
    rows = queries.shape[0]
    every = D // GROUP

    def at(start):
        return pl.BlockSpec((rows, GROUP), lambda g: (0, start + first + g))

    given = [] if earlier is None else [earlier]
    return pl.pallas_call(
        lambda *refs: attend_kernel(*refs[:5], *refs[5 + len(given) :]),
        grid=(groups,),
        in_specs=[at(0), at(0), at(every), at(0), at(every)] + anywhere(given),
        out_specs=[at(0), pl.BlockSpec((1, rows, 128), lambda g: (g, 0, 0))],
        out_shape=[
            jax.ShapeDtypeStruct((rows, D), bf16),
            jax.ShapeDtypeStruct((groups, rows, 128), f32),
        ],
        input_output_aliases={5: 0} if given else {},
        compiler_params=params(),
        cost_estimate=TINY,
        name="attend",
    )(queries, near, near, far, far, *given)


def attend_back_kernel(
    queries, keys_near, values_near, keys_far, values_far, grads, logsum,
    grad_queries, grad_near, grad_far, keys_sum, values_sum
):
    rows = queries.shape[0]
    block = 512
    scale = HEAD_DIM ** (-0.5)
    scaled = queries[...] * jnp.asarray(scale, bf16)
    scaled_t = scaled.T
    grads_t = grads[...].T
    heads = GROUP // HEAD_DIM
    work = [(start, head) for start in range(0, rows, block) for head in range(heads)]

    def scores(start, head):
        here = slice(start, start + block)
        mask = head_mask(head)
        q = scaled[here]
        g = grads[here]
        mine = jnp.where(mask, q, jnp.zeros_like(q))
        mine_g = jnp.where(mask, g, jnp.zeros_like(g))
        return (
            product_back(mine, keys_near[...]),
            product_back(mine, keys_far[...]),
            product_back(mine_g, values_near[...]),
            product_back(mine_g, values_far[...]),
        )

    ready = scores(*work[0])
    for at, (start, head) in enumerate(work):
        sn, sf, gn, gf = ready
        if at + 1 < len(work):
            ready = scores(*work[at + 1])
        here = slice(start, start + block)
        part = slice(head * HEAD_DIM, (head + 1) * HEAD_DIM)
        if head == 0:
            total = jnp.zeros((block, GROUP), f32)
        shift = logsum[0, here, head : head + 1]
        pn = jnp.exp2((sn - shift) * LOG2E)
        pf = jnp.exp2((sf - shift) * LOG2E)
        inner = jnp.sum(pn * gn, axis=1, keepdims=True) + jnp.sum(pf * gf, axis=1, keepdims=True)
        dn = (pn * (gn - inner)).astype(bf16)
        df = (pf * (gf - inner)).astype(bf16)
        pn = pn.astype(bf16)
        pf = pf.astype(bf16)
        out = product(dn, keys_near[...]) + product(df, keys_far[...])
        total = jnp.where(head_mask(head), out * scale, total)
        vn = product(grads_t[part, here], pn)
        vf = product(grads_t[part, here], pf)
        kn = product(scaled_t[part, here], dn)
        kf = product(scaled_t[part, here], df)
        if start == 0:
            values_sum[part, :rows] = vn
            values_sum[part, rows:] = vf
            keys_sum[part, :rows] = kn
            keys_sum[part, rows:] = kf
        else:
            values_sum[part, :rows] += vn
            values_sum[part, rows:] += vf
            keys_sum[part, :rows] += kn
            keys_sum[part, rows:] += kf
        if head == heads - 1:
            grad_queries[here] = total.astype(bf16)
    grad_near[0] = keys_sum[:, :rows].T.astype(bf16)
    grad_near[1] = values_sum[:, :rows].T.astype(bf16)
    grad_far[0] = keys_sum[:, rows:].T.astype(bf16)
    grad_far[1] = values_sum[:, rows:].T.astype(bf16)


def attend_back(queries, near, far, grads, logsum, first):
    rows = queries.shape[0]
    every = D // GROUP
    groups = logsum.shape[0]

    def at(start):
        return pl.BlockSpec((rows, GROUP), lambda g: (0, start + first + g))

    pair = pl.BlockSpec((2, rows, GROUP), lambda g: (0, 0, g))
    return pl.pallas_call(
        attend_back_kernel,
        grid=(groups,),
        in_specs=[at(0), at(0), at(every), at(0), at(every), at(0),
                  pl.BlockSpec((1, rows, 128), lambda g: (g, 0, 0))],
        out_specs=[pl.BlockSpec((rows, GROUP), lambda g: (0, g)), pair, pair],
        out_shape=[
            jax.ShapeDtypeStruct((rows, groups * GROUP), bf16),
            jax.ShapeDtypeStruct((2, rows, groups * GROUP), bf16),
            jax.ShapeDtypeStruct((2, rows, groups * GROUP), bf16),
        ],
        scratch_shapes=[pltpu.VMEM((GROUP, 2 * rows), f32), pltpu.VMEM((GROUP, 2 * rows), f32)],
        compiler_params=params(),
        cost_estimate=TINY,
        name="attend_back",
    )(queries, near, near, far, far, grads, logsum)


def gelu_both(values):
    root = 0.7978845608028654
    square = values * values
    inner = jnp.tanh(values * (root + (root * 0.044715) * square))
    half = 0.5 + 0.5 * inner
    slope = half + (0.5 * values) * (1.0 - inner * inner) * (root + (3.0 * root * 0.044715) * square)
    return values * half, slope


def feed_kernel(
    count, place, latents, attended, cotangent, modulation,
    project_down, project_up, expand_down, expand_up, contract_down, contract_up,
    *refs,
):
    weights = refs[:count]
    (
        block_output, grad_middle, grad_attended, sums,
        grad_project_down, grad_project_up, grad_expand_down, grad_expand_up,
        grad_contract_down, grad_contract_up,
        branch_attend, middle_tokens, entering, grad_branch, branch, grad_entering,
        middle_project, middle_expand, back_contract, grad_branch_attend, back_project,
        project, expand, contract, semaphores,
    ) = refs[count:]
    step_at = pl.program_id(0)
    rows_all = latents.shape[0]

    def row(which):
        return modulation[which : which + 1]

    @pl.when(step_at == 0)
    def _():
        fetch_feed(place, weights, project, expand, contract, semaphores)

        def first(rows):
            grad_branch[rows, :D] = (cotangent[rows].astype(f32) * row(GATE_EXPAND)).astype(bf16)
            branch[rows] = jnp.zeros((CHUNK, WIDE), f32)
            grad_entering[rows] = jnp.zeros((CHUNK, WIDE), f32)

        each_chunk(rows_all, first)
        middle = product_back(grad_branch[:, :D], contract_up[...]).astype(bf16)
        back_contract[...] = middle
        widen(grad_branch, middle.astype(f32))
        middle_project[...] = product_back(attended[...], project_down[...]).astype(bf16)
        wait_for(project, semaphores.at[0])
        branch_attend[...] = product(attended[...], project[...]) + product(
            middle_project[...], project_up[...]
        )

        def step(rows):
            tokens = latents[rows].astype(f32) + row(GATE_ATTEND) * branch_attend[rows]
            middle_tokens[rows] = tokens
            normed, _ = normalize(tokens)
            values = normed * (1.0 + row(SCALE_EXPAND)) + row(SHIFT_EXPAND)
            entering[rows, :D] = values.astype(bf16)

        each_chunk(rows_all, step)
        middle = product_back(entering[:, :D], expand_down[...]).astype(bf16)
        middle_expand[...] = middle
        widen(entering, middle.astype(f32))

    here = pl.ds(pl.multiple_of(step_at * D, D), D)
    expand[step_at, D:] = padded_rows(expand_up[...]).astype(bf16)
    contract[here, D:] = padded_rows(contract_down[...]).T.astype(bf16)
    wait_for(expand.at[step_at, pl.ds(0, D)], semaphores.at[1 + step_at])
    wait_for(contract.at[here, pl.ds(0, D)], semaphores.at[5 + step_at])
    wide = expand[step_at]
    deep = contract[here]
    grads = product_back(grad_branch[...], deep)
    hidden = product(entering[...], wide)
    activated, slope = gelu_both(hidden)
    activated = activated.astype(bf16)
    grads = (grads * slope).astype(bf16)
    branch[...] += product(activated, deep)
    grad_entering[...] += product_back(grads, wide)
    grad_contract_down[...] = product_rows(back_contract[...], activated)
    grad_expand_up[...] = product_rows(middle_expand[...], grads)

    @pl.when(step_at == pl.num_programs(0) - 1)
    def _():
        sums[...] = jnp.zeros_like(sums)
        last_middle = branch[:, D : D + RANK].astype(bf16)
        last_back = grad_entering[:, D : D + RANK].astype(bf16)
        grad_contract_up[...] = product_rows(last_middle, grad_branch[:, :D])
        grad_expand_down[...] = product_rows(last_back, entering[:, :D])
        branch[:, :D] += product(last_middle, contract_up[...])
        grad_entering[:, :D] += product(last_back, expand_down[...])

        def add(which, values):
            sums[which : which + 1] += jnp.sum(values, axis=0, keepdims=True)

        def step(rows):
            out = branch[rows, :D]
            tokens = middle_tokens[rows]
            block_output[rows] = (tokens + row(GATE_EXPAND) * out).astype(bf16)
            cotangents = cotangent[rows].astype(f32)
            add(GATE_EXPAND, cotangents * out)
            grad = grad_entering[rows, :D]
            normed, inverse = normalize(tokens)
            add(SHIFT_EXPAND, grad)
            add(SCALE_EXPAND, grad * normed)
            grad = cotangents + normalize_back(grad * (1.0 + row(SCALE_EXPAND)), normed, inverse)
            grad_middle[rows] = grad
            add(GATE_ATTEND, grad * branch_attend[rows])
            grad_branch_attend[rows] = (grad * row(GATE_ATTEND)).astype(bf16)

        each_chunk(rows_all, step)
        back_project[...] = product_back(grad_branch_attend[...], project_up[...]).astype(bf16)
        grad_attended[...] = (
            product_back(grad_branch_attend[...], project[...])
            + product(back_project[...], project_down[...])
        ).astype(bf16)
        grad_project_up[...] = product_rows(middle_project[...], grad_branch_attend[...])
        grad_project_down[...] = product_rows(back_project[...], attended[...])


def feed(place, latents, attended, cotangent, modulation, weights, chosen):
    rows = latents.shape[0]
    project_down, project_up, expand_down, expand_up, contract_down, contract_up = chosen
    tile = pl.BlockSpec((RANK, D), lambda j: (0, j))
    narrow = whole((RANK, D))

    def buffer(columns, dtype):
        return pltpu.VMEM((rows, columns), dtype)

    return pl.pallas_call(
        lambda *refs: feed_kernel(len(weights), *refs),
        grid=(FF // D,),
        in_specs=[
            smem(),
            whole((rows, D)),
            whole((rows, D)),
            whole((rows, D)),
            whole(modulation.shape),
            narrow,
            narrow,
            narrow,
            tile,
            tile,
            narrow,
        ]
        + anywhere(weights),
        out_specs=[
            whole((rows, D)),
            whole((rows, D)),
            whole((rows, D)),
            whole((8, D)),
            narrow,
            narrow,
            narrow,
            tile,
            tile,
            narrow,
        ],
        out_shape=[
            jax.ShapeDtypeStruct((rows, D), bf16),
            jax.ShapeDtypeStruct((rows, D), f32),
            jax.ShapeDtypeStruct((rows, D), bf16),
            jax.ShapeDtypeStruct((8, D), f32),
            jax.ShapeDtypeStruct((RANK, D), f32),
            jax.ShapeDtypeStruct((RANK, D), f32),
            jax.ShapeDtypeStruct((RANK, D), f32),
            jax.ShapeDtypeStruct((RANK, FF), f32),
            jax.ShapeDtypeStruct((RANK, FF), f32),
            jax.ShapeDtypeStruct((RANK, D), f32),
        ],
        scratch_shapes=[
            buffer(D, f32),
            buffer(D, f32),
            buffer(WIDE, bf16),
            buffer(WIDE, bf16),
            buffer(WIDE, f32),
            buffer(WIDE, f32),
            buffer(RANK, bf16),
            buffer(RANK, bf16),
            buffer(RANK, bf16),
            buffer(D, bf16),
            buffer(RANK, bf16),
            pltpu.VMEM((D, D), bf16),
            pltpu.VMEM((4, WIDE, D), bf16),
            pltpu.VMEM((FF, WIDE), bf16),
            pltpu.SemaphoreType.DMA((9,)),
        ],
        compiler_params=params(),
        cost_estimate=TINY,
        name="feed",
    )(place, latents, attended, cotangent, modulation,
      project_down, project_up, expand_down, expand_up, contract_down, contract_up, *weights)


def leave_kernel(
    count, place, queries_0, queries_1, own_0, own_1, other_0, other_1, down, up, middle,
    modulation, *refs,
):
    weights = refs[:count]
    (
        latents_there, grad_middle_there, input_grad, sums, grad_down, grad_up,
        total, weight, entering, latents, grad_middle, semaphores, semaphore,
    ) = refs[count:]
    step_at = pl.program_id(0)
    rows_all = latents.shape[0]
    copies = [
        pltpu.make_async_copy(source, target, semaphore.at[which])
        for which, (source, target) in enumerate(
            ((latents_there, latents), (grad_middle_there, grad_middle))
        )
    ]

    def through(first, second):
        grads = jnp.concatenate([first, second], axis=1)
        grad_up[...] = product_rows(middle[...], grads)
        return product_back(grads, weight[:, pl.ds(pl.multiple_of(step_at * D, D), D)])

    @pl.when(step_at == 0)
    def _():
        fetch_attend(place, weights, weight, semaphores)
        for copy in copies:
            copy.start()
        weight[D:] = padded_rows(up[...]).astype(bf16)
        wait_attend(weight, semaphores, 0)
        total[...] = through(queries_0[...], queries_1[...])

    @pl.when(step_at > 0)
    def _():
        wait_attend(weight, semaphores, step_at)
        total[...] += through(
            (own_0[0].astype(f32) + other_0[0].astype(f32)).astype(bf16),
            (own_1[0].astype(f32) + other_1[0].astype(f32)).astype(bf16),
        )

    @pl.when(step_at == pl.num_programs(0) - 1)
    def _():
        for copy in copies:
            copy.wait()
        sums[...] = jnp.zeros_like(sums)
        last = total[:, D : D + RANK].astype(bf16)
        total[:, :D] += product(last, down[...])

        def step(rows):
            grad = total[rows, :D]
            normed, inverse = normalize(latents[rows].astype(f32))
            sums[0:1] += jnp.sum(grad, axis=0, keepdims=True)
            sums[1:2] += jnp.sum(grad * normed, axis=0, keepdims=True)
            scale = 1.0 + modulation[SCALE_ATTEND : SCALE_ATTEND + 1]
            shift = modulation[SHIFT_ATTEND : SHIFT_ATTEND + 1]
            entering[rows] = (normed * scale + shift).astype(bf16)
            input_grad[rows] = grad_middle[rows] + normalize_back(grad * scale, normed, inverse)

        each_chunk(rows_all, step)
        grad_down[...] = product_rows(last, entering[...])


def leave(place, queries, own, other, weights, down, up, middle, latents, modulation, grad_middle):
    rows = latents.shape[0]
    columns = up.shape[1]
    tile = pl.BlockSpec((RANK, D), lambda j: (0, j))
    pair = pl.BlockSpec((1, rows, TILE), lambda j: (j // 2, 0, 0))
    return pl.pallas_call(
        lambda *refs: leave_kernel(len(weights), *refs),
        grid=(columns // D,),
        in_specs=[smem()]
        + [whole((rows, TILE))] * 2
        + [pair] * 4
        + [whole(down.shape), whole(up.shape), whole((rows, RANK)), whole(modulation.shape)]
        + anywhere(weights)
        + anywhere(range(2)),
        out_specs=[whole((rows, D)), whole((8, D)), whole((RANK, D)), tile],
        out_shape=[
            jax.ShapeDtypeStruct((rows, D), f32),
            jax.ShapeDtypeStruct((8, D), f32),
            jax.ShapeDtypeStruct((RANK, D), f32),
            jax.ShapeDtypeStruct((RANK, columns), f32),
        ],
        scratch_shapes=[
            pltpu.VMEM((rows, WIDE), f32),
            pltpu.VMEM((WIDE, columns), bf16),
            pltpu.VMEM((rows, D), bf16),
            pltpu.VMEM((rows, D), bf16),
            pltpu.VMEM((rows, D), f32),
            pltpu.SemaphoreType.DMA((3,)),
            pltpu.SemaphoreType.DMA((2,)),
        ],
        compiler_params=params(),
        cost_estimate=TINY,
        name="leave",
    )(place, *queries, *own, *other, down, up, middle, modulation, *weights, latents,
      grad_middle)


PARTS_OF_HALVES = (
    (SHIFT_ATTEND, GATE_ATTEND, SHIFT_EXPAND),
    (SCALE_ATTEND, SCALE_EXPAND, GATE_EXPAND),
)
WIDTHS = (D, 6 * D, D, 3 * D, D, D, D, FF, FF, D)


def swap_cores(values):
    return lax.ppermute(values, "seq", [(0, 1), (1, 0)])


def vmem(count):
    return [pl.BlockSpec(memory_space=pltpu.VMEM)] * count


def rounded_up(span):
    return -(-span // 128) * 128


def note_kernel(condition, choice, out):
    values = condition[...].astype(f32)
    lanes = lax.broadcasted_iota(jnp.int32, (1, 128), 1)
    last = jnp.zeros((1, 128), f32)
    for member in range(5):
        last = jnp.where(lanes == member, choice[0, member].astype(f32), last)
    rows = [values[:, 128 * at : 128 * (at + 1)] for at in range(D // 128)]
    note = jnp.concatenate(rows + [last] + [jnp.zeros((7, 128), f32)], axis=0).astype(bf16)
    for chip in range(out.shape[0]):
        out[chip] = note


def write_notes(chips, condition, choice):
    return pl.pallas_call(
        note_kernel,
        in_specs=vmem(1) + [smem()],
        out_specs=vmem(1)[0],
        out_shape=jax.ShapeDtypeStruct((chips, 16, 128), bf16),
        cost_estimate=TINY,
        name="write_notes",
    )(condition, choice)


def prepare_kernel(early, late, choice, at, lifted, mine, other, tables, out, weight, parts):
    weight[...] = jnp.zeros_like(weight)
    rows = 2 * mine.shape[0]
    m = mine[...].astype(f32)
    o = other[...].astype(f32)
    both = jnp.where(at[1] == 0, jnp.concatenate([m, o]), jnp.concatenate([o, m]))
    weight[pl.ds(pl.multiple_of(at[0], rows), rows)] = both.astype(bf16)
    partial = product(lifted[...], weight[...])
    high = partial.astype(bf16).astype(f32)
    span = parts.shape[2]
    for row in range(8):
        part = slice(row * span, (row + 1) * span)
        parts[:, row] = high[:, part]
        parts[:, 8 + row] = partial[:, part] - high[:, part]
    size = tables.shape[2]
    lanes = lax.broadcasted_iota(jnp.int32, (RANK, size), 1)
    starts = [0, early[0] + early[1], rounded_up(sum(early))]
    starts += [starts[2] + late[0] + late[1], starts[2] + sum(late[:4])]
    for latent in range(out.shape[0]):
        picked = tables[choice[latent, 0]]
        for member in range(1, 5):
            picked = jnp.where(lanes >= starts[member], tables[choice[latent, member]], picked)
        out[latent, :, :size] = picked
        out[latent, :, size:] = parts[latent].astype(bf16)


def prepare(early, late, choice, at, lifted, mine, other, tables):
    chips = choice.shape[0]
    size = tables.shape[2]
    span = mine.shape[1] // 8
    return pl.pallas_call(
        lambda *refs: prepare_kernel(early, late, *refs),
        in_specs=[smem()] * 2 + vmem(4),
        out_specs=vmem(1)[0],
        out_shape=jax.ShapeDtypeStruct((chips, RANK, size + span), bf16),
        scratch_shapes=[
            pltpu.VMEM((128, mine.shape[1]), bf16),
            pltpu.VMEM((chips, 16, span), f32),
        ],
        cost_estimate=TINY,
        name="prepare",
    )(choice, at, lifted, mine, other, tables)


def put_together(own, blocks, first, outs):
    for width, out in zip(own, outs):
        for start in range(0, out.shape[1], 128):
            pieces = []
            for device in range(start // width, (start + 127) // width + 1):
                low = max(start - device * width, 0)
                high = min(start + 128 - device * width, width)
                pieces.append(blocks[device][:, first + low : first + high])
            out[:, start : start + 128] = joined(pieces).astype(bf16)
        first += width


def open_kernel(early, late, core, condition, near, far, *outs):
    tables, (modulation, middle, lifted) = outs[:10], outs[10:]
    size = rounded_up(sum(early)) + rounded_up(sum(late))
    on_first = core[0] == 0
    blocks = []
    near_sum = jnp.zeros((16, near.shape[2] - size), f32)
    far_sum = near_sum
    for chip in range(near.shape[0]):
        n = near[chip].astype(f32)
        f = far[chip].astype(f32)
        near_sum += n[:, size:]
        far_sum += f[:, size:]
        n, f = n[:, :size], f[:, :size]
        blocks += [jnp.where(on_first, n, f), jnp.where(on_first, f, n)]
    put_together(early, blocks, 0, tables[:4])
    put_together(late, blocks, rounded_up(sum(early)), tables[4:])
    near_sum = near_sum[:8] + near_sum[8:]
    far_sum = far_sum[:8] + far_sum[8:]
    values = condition[...].astype(f32)
    lifted[...] = (values * (1.0 / (1.0 + jnp.exp(-values)))).astype(bf16)
    middle[...] = product_back(lifted[...], tables[0][...]).astype(bf16)
    adapted = product(middle[...], tables[1][...])
    halves = (jnp.where(on_first, near_sum, far_sum), jnp.where(on_first, far_sum, near_sum))
    modulation[...] = jnp.zeros_like(modulation)
    for half, targets in zip(halves, PARTS_OF_HALVES):
        for place in range(3 * D // 128):
            row, lane = targets[place // 8], place % 8 * 128
            modulation[row : row + 1, lane : lane + 128] = (
                half[place // 3 : place // 3 + 1, place % 3 * 128 : (place % 3 + 1) * 128]
                + adapted[:, row * D + lane : row * D + lane + 128]
            )


def open_block(early, late, core, condition, near, far):
    chips = near.shape[0]
    shapes = [((RANK, 2 * chips * width), bf16) for width in early + late]
    shapes += [((8, D), f32), ((1, RANK), bf16), ((1, D), bf16)]
    return pl.pallas_call(
        lambda *refs: open_kernel(early, late, *refs),
        in_specs=[smem()] + vmem(3),
        out_specs=vmem(len(shapes)),
        out_shape=[jax.ShapeDtypeStruct(*shape) for shape in shapes],
        compiler_params=params(),
        cost_estimate=TINY,
        name="open_block",
    )(core, condition, near, far)


def joined(pieces):
    return pieces[0] if len(pieces) == 1 else jnp.concatenate(pieces, axis=1)

def pack_into(own, core, grads, near, far):
    chips, span = near.shape[0], near.shape[2]
    on_first = core[0] == 0
    for chip in range(chips):
        parts = []
        for device in (2 * chip, 2 * chip + 1):
            pieces = [grad[:, device * width : (device + 1) * width] for width, grad in zip(own, grads)]
            if span > sum(own):
                pieces.append(jnp.zeros((RANK, span - sum(own)), f32))
            parts.append(joined(pieces))
        near[chip] = jnp.where(on_first, parts[0], parts[1])
        far[chip] = jnp.where(on_first, parts[1], parts[0])


def packed_shapes(own, chips):
    return [jax.ShapeDtypeStruct((chips, RANK, rounded_up(sum(own))), f32)] * 2


def pack_late(own, core, grads):
    return pl.pallas_call(
        lambda core, *refs: pack_into(own, core, refs[:-2], *refs[-2:]),
        out_shape=packed_shapes(own, grads[0].shape[1] // own[0] // 2),
        in_specs=[smem()] + vmem(len(grads)),
        out_specs=vmem(2),
        cost_estimate=TINY,
        name="pack_late",
    )(core, *grads)


def pack_early_kernel(
    own, core, attend, attend_there, feed, feed_there, middle, lifted, up, down_grad, up_grad,
    near, far, grad_modulation, grad_middle, modulate_down, modulate_up
):
    early = attend[...] + attend_there[...]
    late = feed[...] + feed_there[...]
    rows = [early[row : row + 1] if row < 2 else late[row : row + 1] for row in range(6)]
    grads = jnp.concatenate(rows, axis=1).astype(bf16)
    grad_modulation[...] = grads
    back = product_back(grads, up[...]).astype(bf16)
    grad_middle[...] = back
    keep = jnp.where(core[0] == 0, 1.0, 0.0)
    modulate_down[...] = product_rows(back, lifted[...]) * keep
    modulate_up[...] = product_rows(middle[...], grads) * keep
    pack_into(own, core, (modulate_down, modulate_up, down_grad, up_grad), near, far)


def pack_early(own, core, sums, middle, lifted, up, grads):
    return pl.pallas_call(
        lambda *refs: pack_early_kernel(own, *refs),
        out_shape=packed_shapes(own, grads[0].shape[1] // own[2] // 2)
        + [jax.ShapeDtypeStruct((1, 6 * D), bf16), jax.ShapeDtypeStruct((1, RANK), bf16)],
        in_specs=[smem()] + vmem(9),
        out_specs=vmem(4),
        scratch_shapes=[pltpu.VMEM((RANK, D), f32), pltpu.VMEM((RANK, 6 * D), f32)],
        cost_estimate=TINY,
        name="pack_early",
    )(core, *sums, middle, lifted, up, *grads)


def condition_kernel(grads, weight, back, down, condition, out):
    total = jnp.zeros((weight.shape[0], 128), f32)
    for start in range(0, weight.shape[1], 128):
        lanes = slice(start, start + 128)
        total += weight[:, lanes].astype(f32) * grads[:, lanes].astype(f32)
    lifted = jnp.sum(total.T, axis=0, keepdims=True) + product(back[...], down[...])
    values = condition[...].astype(f32)
    gate = 1.0 / (1.0 + jnp.exp(-values))
    out[...] = lifted * gate * (1.0 + values * (1.0 - gate))


def condition_back(grads, weight, back, down, condition):
    part = pl.BlockSpec((1, 128), lambda j: (0, j))
    return pl.pallas_call(
        condition_kernel,
        grid=(D // 128,),
        in_specs=[
            whole(grads.shape),
            pl.BlockSpec((128, weight.shape[1]), lambda j: (j, 0)),
            whole(back.shape),
            pl.BlockSpec((RANK, 128), lambda j: (0, j)),
            part,
        ],
        out_specs=part,
        out_shape=jax.ShapeDtypeStruct(condition.shape, f32),
        cost_estimate=TINY,
        compiler_params=params(),
        name="condition_back",
    )(grads, weight, back, down, condition)


def sums_kernel(own, starts, choice, grads, *refs):
    outs, total = refs[:-1], refs[-1]
    lanes = lax.broadcasted_iota(jnp.int32, grads.shape[1:], 1)
    total[...] = jnp.zeros_like(total)
    for latent in range(grads.shape[0]):
        for member in range(5):
            first = starts[2 * member]
            last = starts[2 * member + 1] + own[2 * member + 1]
            inside = jnp.logical_and(lanes >= first, lanes < last)
            total[choice[latent, member]] += jnp.where(inside, grads[latent].astype(f32), 0.0)
    for entry in range(NADAPT):
        values = total[entry]
        for start, width, out in zip(starts, own, outs):
            out[entry] = values[:, start : start + width]


def table_sums(own, starts, choice, grads):
    sums = pl.pallas_call(
        lambda *refs: sums_kernel(own, starts, *refs),
        out_shape=[jax.ShapeDtypeStruct((NADAPT, RANK, width), f32) for width in own],
        in_specs=[smem()] + vmem(1),
        out_specs=vmem(len(own)),
        scratch_shapes=[pltpu.VMEM((NADAPT,) + grads.shape[1:], f32)],
        cost_estimate=TINY,
        name="table_sums",
    )(choice, grads)
    return [array.transpose(0, 2, 1) if which % 2 == 0 else array for which, array in enumerate(sums)]


def swap_all(arrays):
    return list(arrays) + [swap_cores(array) for array in arrays]


def after(values, *others):
    return lax.optimization_barrier((values, *others))[0]


def cut_kernel(project, expand, contract, main, last):
    deep = project.shape[0]
    main[:deep] = project[...]
    for part in range(4):
        main[(1 + part) * deep : (2 + part) * deep] = expand[:, part * D : (part + 1) * D]
    main[5 * deep :] = contract[: FIRST_ROWS]
    last[...] = contract[FIRST_ROWS:]


def cut_weights(project_weight, expand_weight, contract_weight):
    rows = contract_weight.shape[0] - FIRST_ROWS
    return pl.pallas_call(
        cut_kernel,
        in_specs=vmem(3),
        out_specs=vmem(2),
        out_shape=[
            jax.ShapeDtypeStruct((5 * project_weight.shape[0] + FIRST_ROWS, D), bf16),
            jax.ShapeDtypeStruct((rows, D), bf16),
        ],
        cost_estimate=TINY,
        name="cut_weights",
    )(project_weight, expand_weight, contract_weight)


class PermutedGather:
    chips = 16

    def exchange(self, values, over):
        return lax.ppermute(values, "dp", [(chip, chip ^ over) for chip in range(self.chips)])

    def along(self, values, step=1):
        return lax.ppermute(
            values, "dp", [(chip, (chip + 4 * step) % self.chips) for chip in range(self.chips)]
        )

    def begin(self, attend_weight, project_weight, expand_weight, contract_weight):
        main, last = cut_weights(project_weight, expand_weight, contract_weight)
        self.attend = [attend_weight] + [self.along(attend_weight, step) for step in (1, 2, 3)]
        self.main = self.lines(main)
        self.last = last
        self.attend_crossed = self.cross(jnp.stack(self.attend[:2]), jnp.stack(self.attend[2:]))
        return [self.attend_crossed[1], self.attend_crossed[3]]

    def cross_last(self):
        self.plane = [self.last, self.exchange(self.last, 1), self.exchange(self.last, 2)]
        return self.plane[1:]

    def cross_last_again(self, *before):
        self.attend = self.cross_again(*self.attend_crossed)
        more = [*self.attend[2:], self.exchange(self.plane[1], 2)]
        before, more = self.join(more, before)
        self.attend[2:] = more[:2]
        self.plane += more[2:]
        return before

    def lines(self, values):
        groups = [[z * 4 + line for z in range(self.chips // 4)] for line in range(4)]
        return lax.all_gather(values, "dp", axis=0, tiled=False, axis_index_groups=groups)

    def cross(self, first, second):
        return first, self.exchange(first, 1), second, self.exchange(second, 2)

    def cross_again(self, first, first_there, second, second_there):
        first = jnp.stack([first, first_there])
        second = jnp.stack([second, second_there])
        return [first, second, self.exchange(first, 2), self.exchange(second, 1)]

    def attend_all(self):
        return swap_all(self.attend)

    def cross_main(self):
        planes = lax.all_gather(
            jnp.stack(self.plane),
            ("dp", "seq"),
            axis=0,
            tiled=False,
            axis_index_groups=[
                [2 * (z * 4 + line) + core for z in range(self.chips // 4) for core in range(2)]
                for line in range(4)
            ],
        )
        self.planes = planes.reshape(self.chips // 4, 2, *planes.shape[1:])
        first, second = self.main[:2], self.main[2:]
        self.crossed = [
            self.exchange(first, 1), self.exchange(second, 1),
            self.exchange(first, 2), self.exchange(second, 2),
        ]

    def join(self, held, before):
        joined = lax.optimization_barrier((*before, *held))
        return joined[: len(before)], list(joined[len(before) :])

    def early_main(self, *before):
        before, joined = self.join([self.crossed[0], self.crossed[3]], before)
        self.crossed[0], self.crossed[3] = joined
        return before

    def more_main(self, *before):
        far = [swap_cores(self.main), swap_cores(self.crossed[0])]
        before, joined = self.join([self.crossed[1], self.crossed[2], *far], before)
        self.crossed[1:3], self.far = joined[:2], joined[2:]
        first, second = after(self.crossed[0], before[0]), after(self.crossed[3], before[0])
        self.diagonal = [self.exchange(first, 2), self.exchange(second, 1)]
        return before

    def feed_all(self, *before):
        far = [swap_cores(array) for array in self.crossed[1:]]
        before, joined = self.join([*self.diagonal, *far, self.planes], before)
        diagonal, far, planes = joined[:2], joined[2:-1], joined[-1]
        main = [self.main, *self.crossed, *diagonal]
        other = [*self.far, *far, *(swap_cores(array) for array in diagonal)]
        return before, main + other + [planes]


class WholeGather:
    def begin(self, *matrices):
        self.all = [
            lax.all_gather(array, ("dp", "seq"), axis=0, tiled=True) for array in matrices
        ]
        return []

    def attend_all(self):
        return self.all[:1]

    def cross_last(self):
        return []

    def cross_last_again(self, *before):
        return before

    def cross_main(self):
        pass

    def early_main(self, *before):
        return before

    def more_main(self, *before):
        return before

    def feed_all(self, *before):
        return before, self.all[1:]


def make_local(chips):
    devices = 2 * chips
    own = tuple(width // devices for width in WIDTHS)
    early, late = own[:4], own[4:]
    wide = D // devices

    def local(
        latents,
        condition,
        adapter_choice,
        cotangent,
        modulate_weight,
        attend_weight,
        project_weight,
        expand_weight,
        contract_weight,
        *tables,
    ):
        chip = lax.axis_index("dp")
        core = lax.axis_index("seq")
        place = jnp.stack([chip // 4, chip // 2 % 2, chip % 2, core]).astype(jnp.int32)
        core_at = place[3:]
        tokens = latents[0]

        def to_chips(values):
            return lax.all_to_all(values, "dp", split_axis=0, concat_axis=0, tiled=True)

        gather = PermutedGather() if chips == PermutedGather.chips else WholeGather()
        begun = gather.begin(attend_weight, project_weight, expand_weight, contract_weight)

        notes = to_chips(write_notes(chips, condition, adapter_choice))
        notes = after(notes, *gather.cross_last())
        choice = notes[:, 8, :5].astype(jnp.int32)
        row = 2 * wide * chip // 128
        lifted_all = lax.dynamic_index_in_dim(notes, row, 1, keepdims=False)
        lifted_all = jax.nn.silu(lifted_all.astype(f32)).astype(bf16)

        def columns_of(which):
            return jnp.concatenate(
                [
                    lax.dynamic_slice_in_dim(modulate_weight, which * D, D, 1),
                    lax.dynamic_slice_in_dim(modulate_weight, 2 * D + which * 2 * D, 2 * D, 1),
                ],
                axis=1,
            )

        def laid_out(own, tables):
            values = jnp.concatenate(
                [table.transpose(0, 2, 1) if which % 2 == 0 else table for which, table in enumerate(tables)],
                axis=2,
            )
            span = values.shape[2]
            return jnp.pad(values, ((0, 0), (0, 0), (0, rounded_up(span) - span)))

        at = jnp.stack([2 * wide * chip % 128, core])
        block = prepare(
            early,
            late,
            choice,
            at.astype(jnp.int32),
            lifted_all,
            columns_of(core),
            swap_cores(after(columns_of(1 - core), notes)),
            jnp.concatenate([laid_out(early, tables[:4]), laid_out(late, tables[4:])], axis=2),
        )
        block = after(block, *begun)
        (block,) = gather.cross_last_again(to_chips(block))
        *chosen, modulation, middle_modulate, lifted = open_block(
            early, late, core_at, condition, block, swap_cores(block)
        )
        modulate_down, modulate_up, attend_down, attend_up, *chosen_late = chosen

        attend_all = gather.attend_all()
        gather.cross_main()
        queries, near, middle_attend = enter(
            place, tokens, modulation, attend_all, attend_down, attend_up
        )
        queries, near = gather.early_main(queries, near)
        far = swap_cores(near)
        attended, logsum_0 = attend(queries, near, far, 0, 2)
        logsum_0, far = gather.more_main(logsum_0, far)
        attended, logsum_1 = attend(queries, near, far, 2, 2, attended)
        (attended, logsum_1), feed_all = gather.feed_all(attended, logsum_1)
        modulate_all = lax.all_gather(
            after(modulate_weight, *feed_all), ("dp", "seq"), axis=0, tiled=True
        )
        block_output, grad_middle, grad_attended, sums_feed, *grads_late = feed(
            place, tokens, attended, cotangent[0], modulation, feed_all, chosen_late
        )
        grads_attended = [
            attend_back(queries, near, far, grad_attended, logsum, 2 * half)
            for half, logsum in enumerate((logsum_0, logsum_1))
        ]
        grad_queries, grad_near, grad_far = zip(*grads_attended)
        packed, packed_far = pack_late(
            late, core_at, [after(grads_late[0], *grad_far), *grads_late[1:]]
        )
        grad_queries = [after(grad_queries[0], packed), grad_queries[1]]
        input_grad, sums_attend, *grads_attend = leave(
            place,
            grad_queries,
            grad_near,
            [swap_cores(grad) for grad in grad_far],
            attend_all,
            attend_down,
            attend_up,
            middle_attend,
            tokens,
            modulation,
            grad_middle,
        )

        grads_late = (packed + swap_cores(packed_far)).astype(bf16)
        packed, packed_far, grad_modulation, grad_middle_modulate = pack_early(
            early,
            core_at,
            (sums_attend, swap_cores(sums_attend), sums_feed, swap_cores(sums_feed)),
            middle_modulate,
            lifted,
            modulate_up,
            grads_attend,
        )
        grads_early = (packed + swap_cores(packed_far)).astype(bf16)
        arrived = to_chips(jnp.concatenate([grads_early, grads_late], axis=2))
        condition_grad = condition_back(
            grad_modulation, modulate_all, grad_middle_modulate, modulate_down, condition
        )
        arrived = after(arrived, condition_grad)
        starts = [sum(early[:member]) for member in range(4)]
        starts += [rounded_up(sum(early)) + sum(late[:member]) for member in range(6)]
        owned = table_sums(own, starts, choice, arrived)
        return (block_output[None], input_grad[None], condition_grad, *owned)

    return local


def solution(mesh):
    rows = P(("dp", "seq"), None)
    down = P(None, ("dp", "seq"), None)
    up = P(None, None, ("dp", "seq"))
    tokens = P("dp", "seq", None)
    return jax.shard_map(
        make_local(mesh.shape["dp"]),
        mesh=mesh,
        in_specs=(tokens, P("dp", None), P("dp", None), tokens) + (rows,) * 5 + (down, up) * 5,
        out_specs=(tokens, tokens, P("dp", None)) + (down, up) * 5,
        check_vma=False,
    )
```
